128 devices in a mesh: blk: 64 (over z, y, x), grid: 2 (over core).
Axes of the slice: x: 4, y: 4, z: 4, core: 2. Of those that a mesh axis runs over, the one named last changes fastest.
Arguments:
- orbitals: bfloat16 [2048, 64, 4096], P('blk', 'grid'), may hold values from -6 to 6
- pair_first: int32 [64, 4], P('blk'), may hold values from 0 to 31
- pair_second: int32 [64, 4], P('blk'), may hold values from 0 to 31
- pair_count: int32 [64], P('blk'), may hold values from 1 to 4, as said below
Outputs:
- exchange: bfloat16 [2048, 64, 4096], P('blk', 'grid')
The draws below stay inside these ranges and needn't reach their ends.
Inputs may be any that keep to these rules, and one draw needn't show every extreme that they name: `pair_count`: some block has exactly 4 live slots in every draw.
All inputs are finite; a program needn't handle non-finite values.
Results may differ from the reference program's by a relative error of at most 0.002.
Values may be sent and summed in bfloat16 or wider, within the bound.
A program may use at most 192 MiB of HBM per device.

```python
import math
import jax
import jax.numpy as jnp
from jax import lax

L = 64
ORB_DEV = 32
PAIR_MAX = 4
BLOCKS = 64
NORB = 2048


def draw_pair_count(key, part):
    key = jax.random.fold_in(key, 7)
    count_key, busy_key = jax.random.split(key)
    counts = jax.random.randint(count_key, (BLOCKS,), 1, PAIR_MAX // 2 + 1)
    busiest = jax.random.randint(busy_key, (2,), 0, BLOCKS)
    counts = counts.at[busiest].set(PAIR_MAX)
    return counts.astype(jnp.int32)


def touch_ends(result, own_key, least, largest):
    place = [jax.random.randint(jax.random.fold_in(own_key, axis), (), 0, length) for axis, length in enumerate(result.shape)]
    longest = result.shape.index(max(result.shape))
    neighbour = place[:longest] + [(place[longest] + 1) % result.shape[longest]] + place[longest + 1:]
    return result.at[tuple(place)].set(least).at[tuple(neighbour)].set(largest)


def shard_levels(key, shape, cuts, smallest, top_value):
    def one(position, shards_of):
        heights = jax.random.uniform(jax.random.fold_in(jax.random.fold_in(key, 6), position), (shards_of,), jnp.float32, smallest / len(cuts), top_value / len(cuts))
        return jnp.repeat(jnp.exp(heights), shape[position] // shards_of).reshape((-1,) + (1,) * (len(shape) - position - 1))

    gain = one(*cuts[0])
    for cut in cuts[1:]:
        gain = gain * one(*cut)
    return gain


def centred(rng, extent, scale, bound, cuts=(), held_as=jnp.bfloat16):
    drawn = scale * jax.random.normal(rng, extent, jnp.float32)
    if cuts:
        drawn = drawn * shard_levels(rng, extent, cuts, -0.22, 0.18)
    return jnp.clip(drawn, -bound, bound).astype(held_as)


def setup_inputs(seed: int = 0) -> dict:
    key_of = jax.random.split(jax.random.key(seed), 5)
    orbitals = centred(key_of[0], (NORB, L, L * L), 1.0, 6.0, ((0, 64), (1, 2)))
    pair_first = touch_ends(jax.random.randint(key_of[1], (BLOCKS, PAIR_MAX), 0, ORB_DEV), jax.random.fold_in(key_of[1], 1), 0, ORB_DEV - 1).astype(jnp.int32)
    pair_second = touch_ends(jax.random.randint(key_of[2], (BLOCKS, PAIR_MAX), 0, ORB_DEV), jax.random.fold_in(key_of[2], 1), 0, ORB_DEV - 1).astype(jnp.int32)
    pair_count = draw_pair_count(jax.random.fold_in(key_of[4], 71), 0)
    return dict(orbitals=orbitals, pair_first=pair_first, pair_second=pair_second, pair_count=pair_count)


spacing = 0.5
fraction = 0.25


def coulomb_kernel():
    positions = jnp.arange(L, dtype=jnp.int32)
    wrapped = jnp.where(positions >= L // 2, positions - L, positions).astype(jnp.float32)
    squares = (wrapped * (2.0 * math.pi / (L * spacing))) ** 2
    square_sum = squares[:, None, None] + squares[None, :, None] + squares[None, None, :]
    at_anchor = square_sum <= 0.0
    return jnp.where(at_anchor, 0.0, 4.0 * math.pi / jnp.where(at_anchor, 1.0, square_sum))


def pair_potential(density, kernel):
    spectrum = jnp.fft.fftn(density.reshape(L, L, L))
    field_values = jnp.real(jnp.fft.ifftn(kernel * spectrum))
    return field_values.reshape(L, L * L).astype(jnp.float32)


def block_terms(own_block, visit_block, firsts, seconds, live_count, kernel):
    def slot_step(totals, slot_number):
        own_total, back_total = totals
        own_index = firsts[slot_number]
        visit_index = seconds[slot_number]
        live_value = (slot_number < live_count).astype(jnp.float32)
        own_rows = own_block[own_index].astype(jnp.float32)
        visit_rows = visit_block[visit_index].astype(jnp.float32)
        potential = pair_potential(own_rows * visit_rows, kernel) * live_value
        own_total = own_total.at[own_index].add(-fraction * potential * visit_rows)
        back_total = back_total.at[visit_index].add(-fraction * potential * own_rows)
        return (own_total, back_total), None

    empty_sums = jnp.zeros((ORB_DEV, L, L * L), jnp.float32)
    totals, unused = lax.scan(slot_step, (empty_sums, empty_sums), jnp.arange(PAIR_MAX, dtype=jnp.int32))
    return totals


def reference(orbitals, pair_first, pair_second, pair_count):
    kernel = coulomb_kernel()
    blocks = orbitals.reshape(BLOCKS, ORB_DEV, L, L * L)

    def one_block(block_index):
        before = (block_index + BLOCKS - 1) % BLOCKS
        after = (block_index + 1) % BLOCKS
        own_total, unused_back = block_terms(blocks[block_index], blocks[before], pair_first[block_index], pair_second[block_index], pair_count[block_index], kernel)
        unused_own, back_total = block_terms(blocks[after], blocks[block_index], pair_first[after], pair_second[after], pair_count[after], kernel)
        back_rows = lax.optimization_barrier(back_total.astype(jnp.bfloat16))
        return (own_total + back_rows.astype(jnp.float32)).astype(jnp.bfloat16)

    merged = lax.map(one_block, jnp.arange(BLOCKS, dtype=jnp.int32))
    return merged.reshape(NORB, L, L * L)
```

```python
import functools
import math

import jax
import jax.numpy as jnp
import ml_dtypes
import numpy as np
from jax import lax
from jax.experimental import pallas as pl
from jax.experimental.pallas import tpu as pltpu
from jax.sharding import PartitionSpec as P

spacing = 0.5
fraction = 0.25
L = 64
HALF = L // 2
LANES = 128
ROWS = 17
MINE = 9
f32 = jnp.float32
bf16 = jnp.bfloat16


def split_table(table):
    high = table.astype(ml_dtypes.bfloat16)
    low = (table - high.astype(np.float64)).astype(ml_dtypes.bfloat16)
    return high, low


def lane_tables():
    position = np.arange(L)
    angle = 2.0 * np.pi * (np.outer(position, position) % L) / L
    sign = np.array([[1.0, 1.0], [1.0, -1.0]])
    real = np.kron(sign, np.cos(angle))
    imag = np.kron(sign, -np.sin(angle))
    forward = np.block([[real, imag], [-imag, real]])
    inverse = np.block([[real, -imag], [imag, real]])
    return np.stack(split_table(forward)), np.stack(split_table(inverse))


def row_tables():
    position = np.arange(L)
    angle = 2.0 * np.pi * (np.outer(position, position) % L) / L
    both = np.concatenate([np.cos(angle), np.sin(angle)], 0)
    forwards, inverses = [], []
    for core in range(2):
        order = np.concatenate([np.arange(HALF) + HALF * core, np.arange(HALF) + HALF * (1 - core)])
        high, low = split_table(both[:, order])
        forwards.append(np.concatenate([high, high, low], 1))
        back = np.concatenate([both[:L, order].T, both[L:, order].T], 0)
        high, low = split_table(back)
        inverses.append(np.concatenate([high, high, low], 1))
    return np.stack(forwards), np.stack(inverses)


def filter_table():
    wrapped = np.arange(L)
    wrapped = np.where(wrapped >= HALF, wrapped - L, wrapped)
    squares = (wrapped * (2.0 * np.pi / (L * spacing))) ** 2
    ky = np.arange(ROWS)[:, None] + HALF * np.arange(2)[None, :]
    total = squares[None, :, None, None] + squares[ky][:, None, :, None] + squares[None, None, None, :]
    kernel = np.where(total > 0, 4.0 * np.pi / np.where(total > 0, total, 1.0), 0.0)
    return (-fraction / L**3 * kernel).reshape(ROWS, L, LANES).astype(np.float32)


def twiddle_table():
    odd = np.repeat(np.arange(2), L)
    angle = 2.0 * np.pi * np.outer(np.arange(ROWS), odd) / L
    return np.stack([np.cos(angle), -np.sin(angle)], 1).astype(np.float32)


def real_forward(values):
    count = len(values)
    if count == 2:
        return [values[0] + values[1], values[0] - values[1]], [None, None]
    even_re, even_im = real_forward(values[0::2])
    odd_re, odd_im = real_forward(values[1::2])
    half, quarter = count // 2, count // 4
    re, im = [None] * (half + 1), [None] * (half + 1)
    re[0], re[half] = even_re[0] + odd_re[0], even_re[0] - odd_re[0]
    re[quarter], im[quarter] = even_re[quarter], -odd_re[quarter]
    for k in range(1, quarter):
        c, s = math.cos(2.0 * math.pi * k / count), math.sin(2.0 * math.pi * k / count)
        if 2 * k == quarter:
            turned_re, turned_im = c * (odd_re[k] + odd_im[k]), c * (odd_im[k] - odd_re[k])
        else:
            turned_re = c * odd_re[k] + s * odd_im[k]
            turned_im = c * odd_im[k] - s * odd_re[k]
        re[k], im[k] = even_re[k] + turned_re, even_im[k] + turned_im
        re[half - k], im[half - k] = even_re[k] - turned_re, turned_im - even_im[k]
    return re, im


def real_inverse(re, im):
    half = len(re) - 1
    count = 2 * half
    if count == 2:
        return [re[0] + re[1], re[0] - re[1]]
    quarter = half // 2
    even_re, even_im = [None] * (quarter + 1), [None] * (quarter + 1)
    odd_re, odd_im = [None] * (quarter + 1), [None] * (quarter + 1)
    even_re[0], odd_re[0] = re[0] + re[half], re[0] - re[half]
    even_re[quarter], odd_re[quarter] = 2.0 * re[quarter], -2.0 * im[quarter]
    for k in range(1, quarter):
        c, s = math.cos(2.0 * math.pi * k / count), math.sin(2.0 * math.pi * k / count)
        even_re[k], even_im[k] = re[k] + re[half - k], im[k] - im[half - k]
        part_re, part_im = re[k] - re[half - k], im[k] + im[half - k]
        if 2 * k == quarter:
            odd_re[k], odd_im[k] = c * (part_re - part_im), c * (part_re + part_im)
        else:
            odd_re[k] = c * part_re - s * part_im
            odd_im[k] = s * part_re + c * part_im
    evens, odds = real_inverse(even_re, even_im), real_inverse(odd_re, odd_im)
    return [value for pair in zip(evens, odds) for value in pair]


def split(values):
    high = values.astype(bf16)
    return high, (values - high.astype(f32)).astype(bf16)


def dot(left, right):
    return jnp.dot(left, right, preferred_element_type=f32)


def pair_kernel(
    blocks, slots,
    orbitals, second_in, count_in, first_s, second_s, count_s,
    lane_fwd, lane_inv, row_fwd, row_inv, filters, twiddles,
    own_out, back_out, next_second, next_count,
    orb, sending, visiting, own_terms, back_terms, back_rows,
    spectra_hi, spectra_lo, planes, others, filtered, returned, result,
    lane_fwd_v, lane_inv_v, row_fwd_v, row_inv_v, filters_v, twiddles_v,
    load_sem, table_sem, index_send, index_recv, visit_send, visit_recv,
    back_send, back_recv, own_sem, first_send, first_recv, second_send, second_recv,
):
    me, core = lax.axis_index("blk"), lax.axis_index("grid")
    right, left = lax.rem(me + 1, blocks), lax.rem(me + blocks - 1, blocks)
    to_right, to_left, to_partner = {"blk": right}, {"blk": left}, {"grid": 1 - core}

    load = pltpu.make_async_copy(orbitals, orb, load_sem)
    load.start()
    base = 8 * core
    tables = [
        pltpu.make_async_copy(source, target, table_sem.at[place])
        for place, (source, target) in enumerate([
            (lane_fwd, lane_fwd_v), (lane_inv, lane_inv_v),
            (row_fwd.at[core], row_fwd_v), (row_inv.at[core], row_inv_v),
            (filters.at[pl.ds(base, MINE)], filters_v), (twiddles, twiddles_v),
        ])
    ]
    for table in tables:
        table.start()

    barrier = pltpu.get_barrier_semaphore()
    for device in (to_right, to_left, to_partner):
        pl.semaphore_signal(barrier, inc=1, device_id=device)
    pl.semaphore_wait(barrier, 3)

    def remote(source, target, send, recv, device):
        return pltpu.make_async_remote_copy(
            src_ref=source, dst_ref=target, send_sem=send, recv_sem=recv, device_id=device
        )

    index_copies = [
        remote(second_in, next_second, index_send.at[0], index_recv.at[0], to_left),
        remote(count_in, next_count, index_send.at[1], index_recv.at[1], to_left),
    ]
    for copy in index_copies:
        copy.start()
    for copy in index_copies:
        copy.wait()
    load.wait()

    def visit_copy(slot):
        return remote(sending.at[slot], visiting.at[slot], visit_send.at[slot], visit_recv.at[slot], to_right)

    def back_copy(slot):
        return remote(back_rows.at[slot], back_out.at[slot], back_send.at[slot], back_recv.at[slot], to_left)

    def own_copy(slot):
        return pltpu.make_async_copy(own_terms.at[slot], own_out.at[slot], own_sem.at[slot])

    for slot in range(slots):
        sending[slot] = orb[next_second[0, slot]]
        visit_copy(slot).start()
    for table in tables:
        table.wait()

    other_base = 8 * (1 - core)
    first_copy = remote(planes.at[pl.ds(other_base, MINE)], others, first_send, first_recv, to_partner)
    second_copy = remote(
        filtered.at[pl.ds(core, 8)], returned.at[pl.ds(base + core, 8)], second_send, second_recv, to_partner
    )

    def one_slot(slot, carry):
        mine = first_s[0, slot]
        visit_copy(slot).wait_recv()

        def forward_group(group, carry):
            rows = pl.ds(pl.multiple_of(16 * group, 16), 16)
            values = []
            for column in range(HALF):
                lanes = pl.ds(LANES * column, LANES)
                values.append(orb[mine, rows, lanes].astype(f32) * visiting[slot, rows, lanes].astype(f32))
            re, im = real_forward(values)
            for k in range(ROWS):
                if k == 0:
                    turned_re, turned_im = re[0], jnp.zeros_like(re[0])
                else:
                    c, s = twiddles_v[k, 0:1], twiddles_v[k, 1:2]
                    if im[k] is None:
                        turned_re, turned_im = re[k] * c, re[k] * s
                    else:
                        turned_re, turned_im = re[k] * c - im[k] * s, re[k] * s + im[k] * c
                for part, value in enumerate((turned_re, turned_im)):
                    high, low = split(value)
                    spectra_hi[k, rows, LANES * part : LANES * (part + 1)] = high
                    spectra_lo[k, rows, LANES * part : LANES * (part + 1)] = low
            return carry

        lax.fori_loop(0, 2, forward_group, 0)

        def to_planes(start, count):
            where = pl.ds(start, count)
            high = spectra_hi[where].reshape(count * HALF, 2 * LANES)
            low = spectra_lo[where].reshape(count * HALF, 2 * LANES)
            out = dot(high, lane_fwd_v[0]) + dot(low, lane_fwd_v[0]) + dot(high, lane_fwd_v[1])
            planes[where] = out.reshape(count, HALF, 2 * LANES)

        to_planes(other_base, MINE)
        first_copy.start()
        to_planes(base + core, 8)
        first_copy.wait()

        def solve(k, carry):
            values = jnp.concatenate([planes[base + k], others[k]], 0)
            high, low = split(values)
            out = dot(row_fwd_v[...], jnp.concatenate([high, low, high], 0))
            kernel = filters_v[k]
            re = (out[:L, :LANES] + out[L:, LANES:]) * kernel
            im = (out[:L, LANES:] - out[L:, :LANES]) * kernel
            high, low = split(jnp.concatenate([re, im], 1))
            out = dot(row_inv_v[...], jnp.concatenate([high, low, high], 0))
            re = out[:L, :LANES] - out[L:, LANES:]
            im = out[:L, LANES:] + out[L:, :LANES]
            whole = jnp.concatenate([re, im], 1)
            returned[base + k] = whole[:HALF]
            filtered[k] = whole[HALF:]
            return carry

        lax.fori_loop(0, MINE, solve, 0)
        second_copy.start()

        def from_planes(start, count):
            where = pl.ds(start, count)
            values = returned[where].reshape(count * HALF, 2 * LANES)
            high, low = split(values)
            out = dot(high, lane_inv_v[0]) + dot(low, lane_inv_v[0]) + dot(high, lane_inv_v[1])
            result[where] = out.reshape(count, HALF, 2 * LANES)

        from_planes(base, MINE)
        second_copy.wait()
        from_planes(9 * (1 - core), 8)

        live = jnp.where(slot < count_s[0], 1.0, 0.0).astype(f32)

        def inverse_group(group, carry):
            rows = pl.ds(pl.multiple_of(16 * group, 16), 16)
            re, im = [], []
            for k in range(ROWS):
                value_re = result[k, rows, :LANES]
                if k == 0:
                    re.append(value_re)
                    im.append(None)
                    continue
                value_im = result[k, rows, LANES:]
                c, s = twiddles_v[k, 0:1], twiddles_v[k, 1:2]
                re.append(value_re * c + value_im * s)
                im.append(None if k == ROWS - 1 else value_im * c - value_re * s)
            potential = real_inverse(re, im)
            for column in range(HALF):
                lanes = pl.ds(LANES * column, LANES)
                value = potential[column] * live
                own_terms[slot, rows, lanes] = value * visiting[slot, rows, lanes].astype(f32)
                back_terms[slot, rows, lanes] = value * orb[mine, rows, lanes].astype(f32)
            return carry

        lax.fori_loop(0, 2, inverse_group, 0)
        own_copy(slot).start()

        target = second_s[0, slot]

        def message(piece, carry):
            lanes = pl.ds(pl.multiple_of(512 * piece, 512), 512)

            def earlier(other, total):
                same = jnp.where(second_s[0, other] == target, 1.0, 0.0).astype(f32)
                return total + same * back_terms[other, :, lanes]

            total = lax.fori_loop(0, slot, earlier, back_terms[slot, :, lanes])
            back_rows[slot, :, lanes] = total.astype(bf16)
            return carry

        lax.fori_loop(0, 8, message, 0)
        back_copy(slot).start()
        return carry

    lax.fori_loop(0, slots, one_slot, 0)
    for slot in range(slots):
        visit_copy(slot).wait_send()
        own_copy(slot).wait()
        back_copy(slot).wait()


def exchange(orbitals, pair_first, pair_second, pair_count):
    blocks = lax.axis_size("blk")
    slots = pair_first.shape[1]
    block, rows, cells = orbitals.shape
    lane_fwd, lane_inv = lane_tables()
    row_fwd, row_inv = row_tables()
    tables = [jnp.asarray(t) for t in (lane_fwd, lane_inv, row_fwd, row_inv, filter_table(), twiddle_table())]
    anywhere, vmem, smem = (pl.BlockSpec(memory_space=space) for space in (pl.ANY, pltpu.VMEM, pltpu.SMEM))
    dma, dmas = pltpu.SemaphoreType.DMA, lambda *shape: pltpu.SemaphoreType.DMA(shape)
    return pl.pallas_call(
        functools.partial(pair_kernel, blocks, slots),
        out_shape=[
            jax.ShapeDtypeStruct((slots, rows, cells), f32),
            jax.ShapeDtypeStruct((slots, rows, cells), bf16),
            jax.ShapeDtypeStruct(pair_second.shape, jnp.int32),
            jax.ShapeDtypeStruct(pair_count.shape, jnp.int32),
        ],
        in_specs=[anywhere] * 3 + [smem] * 3 + [anywhere] * len(tables),
        out_specs=[anywhere, anywhere, smem, smem],
        scratch_shapes=[
            pltpu.VMEM((block, rows, cells), bf16),
            pltpu.VMEM((slots, rows, cells), bf16),
            pltpu.VMEM((slots, rows, cells), bf16),
            pltpu.VMEM((slots, rows, cells), f32),
            pltpu.VMEM((slots, rows, cells), f32),
            pltpu.VMEM((slots, rows, cells), bf16),
            pltpu.VMEM((ROWS, HALF, 2 * LANES), bf16),
            pltpu.VMEM((ROWS, HALF, 2 * LANES), bf16),
            pltpu.VMEM((ROWS, HALF, 2 * LANES), f32),
            pltpu.VMEM((MINE, HALF, 2 * LANES), f32),
            pltpu.VMEM((MINE, HALF, 2 * LANES), f32),
            pltpu.VMEM((ROWS, HALF, 2 * LANES), f32),
            pltpu.VMEM((ROWS, HALF, 2 * LANES), f32),
            pltpu.VMEM(lane_fwd.shape, bf16),
            pltpu.VMEM(lane_inv.shape, bf16),
            pltpu.VMEM(row_fwd.shape[1:], bf16),
            pltpu.VMEM(row_inv.shape[1:], bf16),
            pltpu.VMEM((MINE, L, LANES), f32),
            pltpu.VMEM((ROWS, 2, LANES), f32),
            dma, dmas(6), dmas(2), dmas(2), dmas(slots), dmas(slots),
            dmas(slots), dmas(slots), dmas(slots), dma, dma, dma, dma,
        ],
        compiler_params=pltpu.CompilerParams(
            collective_id=0, has_side_effects=True, vmem_limit_bytes=56 * 2**20
        ),
        name="pair_exchange",
    )(orbitals, pair_second, pair_count, pair_first, pair_second, pair_count, *tables)


def merge_kernel(
    slots, block, own_in, back_in, first, count, second, second_count,
    out, own, back, zero, staged, own_sem, back_sem, out_sem,
):
    loads = [pltpu.make_async_copy(own_in, own, own_sem), pltpu.make_async_copy(back_in, back, back_sem)]
    for load in loads:
        load.start()
    zero[...] = jnp.zeros_like(zero)

    def own_live(slot):
        return slot < count[0]

    def back_live(slot):
        return slot < second_count[0]

    for row in range(block):
        touched = jnp.bool_(False)
        for slot in range(slots):
            touched |= own_live(slot) & (first[0, slot] == row)
            touched |= back_live(slot) & (second[0, slot] == row)

        @pl.when(jnp.logical_not(touched))
        def _():
            pltpu.make_async_copy(zero, out.at[row], out_sem).start()

    for load in loads:
        load.wait()

    for slot in range(slots):
        row = first[0, slot]
        seen = jnp.bool_(False)
        for earlier in range(slot):
            seen |= first[0, earlier] == row

        @pl.when(own_live(slot) & jnp.logical_not(seen))
        def _():
            for later in range(slot + 1, slots):

                @pl.when(own_live(later) & (first[0, later] == row))
                def _():
                    own[slot] += own[later]

            for other in range(slots):
                last = back_live(other) & (second[0, other] == row)
                for later in range(other + 1, slots):
                    last &= jnp.logical_not(back_live(later) & (second[0, later] == row))

                @pl.when(last)
                def _():
                    own[slot] += back[other].astype(f32)

            staged[slot] = own[slot].astype(bf16)
            pltpu.make_async_copy(staged.at[slot], out.at[row], out_sem).start()

    for slot in range(slots):
        row = second[0, slot]
        alone = back_live(slot)
        for later in range(slot + 1, slots):
            alone &= jnp.logical_not(back_live(later) & (second[0, later] == row))
        for other in range(slots):
            alone &= jnp.logical_not(own_live(other) & (first[0, other] == row))

        @pl.when(alone)
        def _():
            pltpu.make_async_copy(back.at[slot], out.at[row], out_sem).start()

    pltpu.make_async_copy(out, out, out_sem).wait()


def merge(own, back, pair_first, pair_count, next_second, next_count, shape):
    slots, rows, cells = own.shape
    anywhere, smem = (pl.BlockSpec(memory_space=space) for space in (pl.ANY, pltpu.SMEM))
    return pl.pallas_call(
        functools.partial(merge_kernel, slots, shape[0]),
        out_shape=jax.ShapeDtypeStruct(shape, bf16),
        in_specs=[anywhere] * 2 + [smem] * 4,
        out_specs=anywhere,
        scratch_shapes=[
            pltpu.VMEM((slots, rows, cells), f32),
            pltpu.VMEM((slots, rows, cells), bf16),
            pltpu.VMEM((rows, cells), bf16),
            pltpu.VMEM((slots, rows, cells), bf16),
            pltpu.SemaphoreType.DMA,
            pltpu.SemaphoreType.DMA,
            pltpu.SemaphoreType.DMA,
        ],
        compiler_params=pltpu.CompilerParams(vmem_limit_bytes=32 * 2**20),
        name="merge_rows",
    )(own, back, pair_first, pair_count, next_second, next_count)


def per_device(orbitals, pair_first, pair_second, pair_count):
    own, back, next_second, next_count = exchange(orbitals, pair_first, pair_second, pair_count)
    return merge(own, back, pair_first, pair_count, next_second, next_count, orbitals.shape)


def solution(mesh):
    return jax.shard_map(
        per_device,
        mesh=mesh,
        in_specs=(P("blk", "grid", None), P("blk", None), P("blk", None), P("blk")),
        out_specs=P("blk", "grid", None),
        check_vma=False,
    )
```

```python
import functools
import math

import jax
import jax.numpy as jnp
import ml_dtypes
import numpy as np
from jax import lax
from jax.experimental import pallas as pl
from jax.experimental.pallas import tpu as pltpu
from jax.sharding import PartitionSpec as P

spacing = 0.5
fraction = 0.25
L = 64
HALF = L // 2
LANES = 128
ROWS = 17
MINE = 9
f32 = jnp.float32
bf16 = jnp.bfloat16


def split_table(table):
    high = table.astype(ml_dtypes.bfloat16)
    low = (table - high.astype(np.float64)).astype(ml_dtypes.bfloat16)
    return high, low


def lane_tables():
    position = np.arange(L)
    angle = 2.0 * np.pi * (np.outer(position, position) % L) / L
    sign = np.array([[1.0, 1.0], [1.0, -1.0]])
    real = np.kron(sign, np.cos(angle))
    imag = np.kron(sign, -np.sin(angle))
    forward = np.block([[real, imag], [-imag, real]])
    inverse = np.block([[real, -imag], [imag, real]])
    return np.stack(split_table(forward)), np.stack(split_table(inverse))


def row_tables():
    position = np.arange(L)
    angle = 2.0 * np.pi * (np.outer(position, position) % L) / L
    both = np.concatenate([np.cos(angle), np.sin(angle)], 0)
    forwards, inverses = [], []
    for core in range(2):
        order = np.concatenate([np.arange(HALF) + HALF * core, np.arange(HALF) + HALF * (1 - core)])
        high, low = split_table(both[:, order])
        forwards.append(np.concatenate([high, high, low], 1))
        back = np.concatenate([both[:L, order].T, both[L:, order].T], 0)
        high, low = split_table(back)
        inverses.append(np.concatenate([high, high, low], 1))
    return np.stack(forwards), np.stack(inverses)


def filter_table():
    wrapped = np.arange(L)
    wrapped = np.where(wrapped >= HALF, wrapped - L, wrapped)
    squares = (wrapped * (2.0 * np.pi / (L * spacing))) ** 2
    ky = np.arange(ROWS)[:, None] + HALF * np.arange(2)[None, :]
    total = squares[None, :, None, None] + squares[ky][:, None, :, None] + squares[None, None, None, :]
    kernel = np.where(total > 0, 4.0 * np.pi / np.where(total > 0, total, 1.0), 0.0)
    return (-fraction / L**3 * kernel).reshape(ROWS, L, LANES).astype(np.float32)


def twiddle_table():
    odd = np.repeat(np.arange(2), L)
    angle = 2.0 * np.pi * np.outer(np.arange(ROWS), odd) / L
    return np.stack([np.cos(angle), -np.sin(angle)], 1).astype(np.float32)


def real_forward(values):
    count = len(values)
    if count == 2:
        return [values[0] + values[1], values[0] - values[1]], [None, None]
    even_re, even_im = real_forward(values[0::2])
    odd_re, odd_im = real_forward(values[1::2])
    half, quarter = count // 2, count // 4
    re, im = [None] * (half + 1), [None] * (half + 1)
    re[0], re[half] = even_re[0] + odd_re[0], even_re[0] - odd_re[0]
    re[quarter], im[quarter] = even_re[quarter], -odd_re[quarter]
    for k in range(1, quarter):
        c, s = math.cos(2.0 * math.pi * k / count), math.sin(2.0 * math.pi * k / count)
        if 2 * k == quarter:
            turned_re, turned_im = c * (odd_re[k] + odd_im[k]), c * (odd_im[k] - odd_re[k])
        else:
            turned_re = c * odd_re[k] + s * odd_im[k]
            turned_im = c * odd_im[k] - s * odd_re[k]
        re[k], im[k] = even_re[k] + turned_re, even_im[k] + turned_im
        re[half - k], im[half - k] = even_re[k] - turned_re, turned_im - even_im[k]
    return re, im


def real_inverse(re, im):
    half = len(re) - 1
    count = 2 * half
    if count == 2:
        return [re[0] + re[1], re[0] - re[1]]
    quarter = half // 2
    even_re, even_im = [None] * (quarter + 1), [None] * (quarter + 1)
    odd_re, odd_im = [None] * (quarter + 1), [None] * (quarter + 1)
    even_re[0], odd_re[0] = re[0] + re[half], re[0] - re[half]
    even_re[quarter], odd_re[quarter] = 2.0 * re[quarter], -2.0 * im[quarter]
    for k in range(1, quarter):
        c, s = math.cos(2.0 * math.pi * k / count), math.sin(2.0 * math.pi * k / count)
        even_re[k], even_im[k] = re[k] + re[half - k], im[k] - im[half - k]
        part_re, part_im = re[k] - re[half - k], im[k] + im[half - k]
        if 2 * k == quarter:
            odd_re[k], odd_im[k] = c * (part_re - part_im), c * (part_re + part_im)
        else:
            odd_re[k] = c * part_re - s * part_im
            odd_im[k] = s * part_re + c * part_im
    evens, odds = real_inverse(even_re, even_im), real_inverse(odd_re, odd_im)
    return [value for pair in zip(evens, odds) for value in pair]


def split(values):
    high = values.astype(bf16)
    return high, (values - high.astype(f32)).astype(bf16)


def dot(left, right):
    return jnp.dot(left, right, preferred_element_type=f32)


def pair_kernel(
    blocks, slots,
    orbitals, first_in, second_in, count_in,
    lane_fwd, lane_inv, row_fwd, row_inv, filters, twiddles,
    own_out, back_out, next_second, next_count,
    orb, sending, visiting, own_terms, back_terms, back_rows,
    spectra_hi, spectra_lo, planes, others, filtered, returned, result,
    lane_fwd_v, lane_inv_v, row_fwd_v, row_inv_v, filters_v, twiddles_v, first_s, second_s, count_s,
    load_sem, table_sem, index_send, index_recv, visit_send, visit_recv,
    back_send, back_recv, own_sem, first_send, first_recv, second_send, second_recv,
):
    me, core = lax.axis_index("blk"), lax.axis_index("grid")
    right, left = lax.rem(me + 1, blocks), lax.rem(me + blocks - 1, blocks)
    to_right, to_left, to_partner = {"blk": right}, {"blk": left}, {"grid": 1 - core}

    load = pltpu.make_async_copy(orbitals, orb, load_sem)
    load.start()
    base = 8 * core
    tables = [
        pltpu.make_async_copy(source, target, table_sem.at[place])
        for place, (source, target) in enumerate([
            (lane_fwd, lane_fwd_v), (lane_inv, lane_inv_v),
            (row_fwd.at[core], row_fwd_v), (row_inv.at[core], row_inv_v),
            (filters.at[pl.ds(base, MINE)], filters_v), (twiddles, twiddles_v),
            (first_in, first_s), (second_in, second_s), (count_in, count_s),
        ])
    ]
    for table in tables:
        table.start()

    barrier = pltpu.get_barrier_semaphore()
    for device in (to_right, to_left, to_partner):
        pl.semaphore_signal(barrier, inc=1, device_id=device)
    pl.semaphore_wait(barrier, 3)

    def remote(source, target, send, recv, device):
        return pltpu.make_async_remote_copy(
            src_ref=source, dst_ref=target, send_sem=send, recv_sem=recv, device_id=device
        )

    index_copies = [
        remote(second_in, next_second, index_send.at[0], index_recv.at[0], to_left),
        remote(count_in, next_count, index_send.at[1], index_recv.at[1], to_left),
    ]
    for copy in index_copies:
        copy.start()
    for copy in index_copies:
        copy.wait()
    load.wait()

    def visit_copy(slot):
        return remote(sending.at[slot], visiting.at[slot], visit_send.at[slot], visit_recv.at[slot], to_right)

    def back_copy(slot):
        return remote(back_rows.at[slot], back_out.at[slot], back_send.at[slot], back_recv.at[slot], to_left)

    def own_copy(slot):
        return pltpu.make_async_copy(own_terms.at[slot], own_out.at[slot], own_sem.at[slot])

    for slot in range(slots):
        sending[slot] = orb[next_second[0, slot]]
        visit_copy(slot).start()
    for table in tables:
        table.wait()

    other_base = 8 * (1 - core)
    first_copy = remote(planes.at[pl.ds(other_base, MINE)], others, first_send, first_recv, to_partner)
    second_copy = remote(
        filtered.at[pl.ds(core, 8)], returned.at[pl.ds(base + core, 8)], second_send, second_recv, to_partner
    )

    def one_slot(slot, carry):
        mine = first_s[0, slot]
        visit_copy(slot).wait_recv()

        def forward_group(group, carry):
            rows = pl.ds(pl.multiple_of(16 * group, 16), 16)
            values = []
            for column in range(HALF):
                lanes = pl.ds(LANES * column, LANES)
                values.append(orb[mine, rows, lanes].astype(f32) * visiting[slot, rows, lanes].astype(f32))
            re, im = real_forward(values)
            for k in range(ROWS):
                if k == 0:
                    turned_re, turned_im = re[0], jnp.zeros_like(re[0])
                else:
                    c, s = twiddles_v[k, 0:1], twiddles_v[k, 1:2]
                    if im[k] is None:
                        turned_re, turned_im = re[k] * c, re[k] * s
                    else:
                        turned_re, turned_im = re[k] * c - im[k] * s, re[k] * s + im[k] * c
                for part, value in enumerate((turned_re, turned_im)):
                    high, low = split(value)
                    spectra_hi[k, rows, LANES * part : LANES * (part + 1)] = high
                    spectra_lo[k, rows, LANES * part : LANES * (part + 1)] = low
            return carry

        lax.fori_loop(0, 2, forward_group, 0)

        def to_planes(start, count):
            where = pl.ds(start, count)
            high = spectra_hi[where].reshape(count * HALF, 2 * LANES)
            low = spectra_lo[where].reshape(count * HALF, 2 * LANES)
            out = dot(high, lane_fwd_v[0]) + dot(low, lane_fwd_v[0]) + dot(high, lane_fwd_v[1])
            planes[where] = out.reshape(count, HALF, 2 * LANES)

        to_planes(other_base, MINE)
        first_copy.start()
        to_planes(base + core, 8)
        first_copy.wait()

        def solve(k, carry):
            values = jnp.concatenate([planes[base + k], others[k]], 0)
            high, low = split(values)
            out = dot(row_fwd_v[...], jnp.concatenate([high, low, high], 0))
            kernel = filters_v[k]
            re = (out[:L, :LANES] + out[L:, LANES:]) * kernel
            im = (out[:L, LANES:] - out[L:, :LANES]) * kernel
            high, low = split(jnp.concatenate([re, im], 1))
            out = dot(row_inv_v[...], jnp.concatenate([high, low, high], 0))
            re = out[:L, :LANES] - out[L:, LANES:]
            im = out[:L, LANES:] + out[L:, :LANES]
            whole = jnp.concatenate([re, im], 1)
            returned[base + k] = whole[:HALF]
            filtered[k] = whole[HALF:]
            return carry

        lax.fori_loop(0, MINE, solve, 0, unroll=True)
        second_copy.start()

        def from_planes(start, count):
            where = pl.ds(start, count)
            values = returned[where].reshape(count * HALF, 2 * LANES)
            high, low = split(values)
            out = dot(high, lane_inv_v[0]) + dot(low, lane_inv_v[0]) + dot(high, lane_inv_v[1])
            result[where] = out.reshape(count, HALF, 2 * LANES)

        from_planes(base, MINE)
        second_copy.wait()
        from_planes(9 * (1 - core), 8)

        live = jnp.where(slot < count_s[0], 1.0, 0.0).astype(f32)

        def inverse_group(group, carry):
            rows = pl.ds(pl.multiple_of(16 * group, 16), 16)
            re, im = [], []
            for k in range(ROWS):
                value_re = result[k, rows, :LANES]
                if k == 0:
                    re.append(value_re)
                    im.append(None)
                    continue
                value_im = result[k, rows, LANES:]
                c, s = twiddles_v[k, 0:1], twiddles_v[k, 1:2]
                re.append(value_re * c + value_im * s)
                im.append(None if k == ROWS - 1 else value_im * c - value_re * s)
            potential = real_inverse(re, im)
            for column in range(HALF):
                lanes = pl.ds(LANES * column, LANES)
                value = potential[column] * live
                own_terms[slot, rows, lanes] = value * visiting[slot, rows, lanes].astype(f32)
                back_terms[slot, rows, lanes] = value * orb[mine, rows, lanes].astype(f32)
            return carry

        lax.fori_loop(0, 2, inverse_group, 0)
        own_copy(slot).start()

        target = second_s[0, slot]

        def message(piece, carry):
            lanes = pl.ds(pl.multiple_of(512 * piece, 512), 512)

            def earlier(other, total):
                same = jnp.where(second_s[0, other] == target, 1.0, 0.0).astype(f32)
                return total + same * back_terms[other, :, lanes]

            total = lax.fori_loop(0, slot, earlier, back_terms[slot, :, lanes])
            back_rows[slot, :, lanes] = total.astype(bf16)
            return carry

        lax.fori_loop(0, 8, message, 0)
        back_copy(slot).start()
        return carry

    lax.fori_loop(0, slots, one_slot, 0)
    for slot in range(slots):
        visit_copy(slot).wait_send()
        own_copy(slot).wait()
        back_copy(slot).wait()


def exchange(orbitals, pair_first, pair_second, pair_count):
    blocks = lax.axis_size("blk")
    slots = pair_first.shape[1]
    block, rows, cells = orbitals.shape
    lane_fwd, lane_inv = lane_tables()
    row_fwd, row_inv = row_tables()
    tables = [jnp.asarray(t) for t in (lane_fwd, lane_inv, row_fwd, row_inv, filter_table(), twiddle_table())]
    anywhere, smem = (pl.BlockSpec(memory_space=space) for space in (pl.ANY, pltpu.SMEM))
    dma, dmas = pltpu.SemaphoreType.DMA, lambda *shape: pltpu.SemaphoreType.DMA(shape)
    return pl.pallas_call(
        functools.partial(pair_kernel, blocks, slots),
        out_shape=[
            jax.ShapeDtypeStruct((slots, rows, cells), f32),
            jax.ShapeDtypeStruct((slots, rows, cells), bf16),
            jax.ShapeDtypeStruct(pair_second.shape, jnp.int32),
            jax.ShapeDtypeStruct(pair_count.shape, jnp.int32),
        ],
        in_specs=[anywhere] * (4 + len(tables)),
        out_specs=[anywhere, anywhere, smem, smem],
        scratch_shapes=[
            pltpu.VMEM((block, rows, cells), bf16),
            pltpu.VMEM((slots, rows, cells), bf16),
            pltpu.VMEM((slots, rows, cells), bf16),
            pltpu.VMEM((slots, rows, cells), f32),
            pltpu.VMEM((slots, rows, cells), f32),
            pltpu.VMEM((slots, rows, cells), bf16),
            pltpu.VMEM((ROWS, HALF, 2 * LANES), bf16),
            pltpu.VMEM((ROWS, HALF, 2 * LANES), bf16),
            pltpu.VMEM((ROWS, HALF, 2 * LANES), f32),
            pltpu.VMEM((MINE, HALF, 2 * LANES), f32),
            pltpu.VMEM((MINE, HALF, 2 * LANES), f32),
            pltpu.VMEM((ROWS, HALF, 2 * LANES), f32),
            pltpu.VMEM((ROWS, HALF, 2 * LANES), f32),
            pltpu.VMEM(lane_fwd.shape, bf16),
            pltpu.VMEM(lane_inv.shape, bf16),
            pltpu.VMEM(row_fwd.shape[1:], bf16),
            pltpu.VMEM(row_inv.shape[1:], bf16),
            pltpu.VMEM((MINE, L, LANES), f32),
            pltpu.VMEM((ROWS, 2, LANES), f32),
            pltpu.SMEM(pair_first.shape, jnp.int32),
            pltpu.SMEM(pair_second.shape, jnp.int32),
            pltpu.SMEM(pair_count.shape, jnp.int32),
            dma, dmas(9), dmas(2), dmas(2), dmas(slots), dmas(slots),
            dmas(slots), dmas(slots), dmas(slots), dma, dma, dma, dma,
        ],
        compiler_params=pltpu.CompilerParams(
            collective_id=0, has_side_effects=True, vmem_limit_bytes=60 * 2**20
        ),
        name="pair_exchange",
    )(orbitals, pair_first, pair_second, pair_count, *tables)


def merge_kernel(
    slots, block, own_in, back_in, first, count, second, second_count,
    out, own, back, zero, staged, own_sem, back_sem, out_sem,
):
    loads = [pltpu.make_async_copy(own_in, own, own_sem), pltpu.make_async_copy(back_in, back, back_sem)]
    for load in loads:
        load.start()
    zero[...] = jnp.zeros_like(zero)

    def own_live(slot):
        return slot < count[0]

    def back_live(slot):
        return slot < second_count[0]

    for row in range(block):
        touched = jnp.bool_(False)
        for slot in range(slots):
            touched |= own_live(slot) & (first[0, slot] == row)
            touched |= back_live(slot) & (second[0, slot] == row)

        @pl.when(jnp.logical_not(touched))
        def _():
            pltpu.make_async_copy(zero, out.at[row], out_sem).start()

    for load in loads:
        load.wait()

    for slot in range(slots):
        row = first[0, slot]
        seen = jnp.bool_(False)
        for earlier in range(slot):
            seen |= first[0, earlier] == row

        @pl.when(own_live(slot) & jnp.logical_not(seen))
        def _():
            for later in range(slot + 1, slots):

                @pl.when(own_live(later) & (first[0, later] == row))
                def _():
                    own[slot] += own[later]

            for other in range(slots):
                last = back_live(other) & (second[0, other] == row)
                for later in range(other + 1, slots):
                    last &= jnp.logical_not(back_live(later) & (second[0, later] == row))

                @pl.when(last)
                def _():
                    own[slot] += back[other].astype(f32)

            staged[slot] = own[slot].astype(bf16)
            pltpu.make_async_copy(staged.at[slot], out.at[row], out_sem).start()

    for slot in range(slots):
        row = second[0, slot]
        alone = back_live(slot)
        for later in range(slot + 1, slots):
            alone &= jnp.logical_not(back_live(later) & (second[0, later] == row))
        for other in range(slots):
            alone &= jnp.logical_not(own_live(other) & (first[0, other] == row))

        @pl.when(alone)
        def _():
            pltpu.make_async_copy(back.at[slot], out.at[row], out_sem).start()

    pltpu.make_async_copy(out, out, out_sem).wait()


def merge(own, back, pair_first, pair_count, next_second, next_count, shape):
    slots, rows, cells = own.shape
    anywhere, smem = (pl.BlockSpec(memory_space=space) for space in (pl.ANY, pltpu.SMEM))
    return pl.pallas_call(
        functools.partial(merge_kernel, slots, shape[0]),
        out_shape=jax.ShapeDtypeStruct(shape, bf16),
        in_specs=[anywhere] * 2 + [smem] * 4,
        out_specs=anywhere,
        scratch_shapes=[
            pltpu.VMEM((slots, rows, cells), f32),
            pltpu.VMEM((slots, rows, cells), bf16),
            pltpu.VMEM((rows, cells), bf16),
            pltpu.VMEM((slots, rows, cells), bf16),
            pltpu.SemaphoreType.DMA,
            pltpu.SemaphoreType.DMA,
            pltpu.SemaphoreType.DMA,
        ],
        compiler_params=pltpu.CompilerParams(vmem_limit_bytes=60 * 2**20),
        name="merge_rows",
    )(own, back, pair_first, pair_count, next_second, next_count)


def per_device(orbitals, pair_first, pair_second, pair_count):
    own, back, next_second, next_count = exchange(orbitals, pair_first, pair_second, pair_count)
    return merge(own, back, pair_first, pair_count, next_second, next_count, orbitals.shape)


def solution(mesh):
    return jax.shard_map(
        per_device,
        mesh=mesh,
        in_specs=(P("blk", "grid", None), P("blk", None), P("blk", None), P("blk")),
        out_specs=P("blk", "grid", None),
        check_vma=False,
    )
```

```python
import functools
import math

import jax
import jax.numpy as jnp
import ml_dtypes
import numpy as np
from jax import lax
from jax.experimental import pallas as pl
from jax.experimental.pallas import tpu as pltpu
from jax.sharding import PartitionSpec as P

spacing = 0.5
fraction = 0.25
L = 64
HALF = L // 2
LANES = 128
ROWS = 17
MINE = 9
CODE = 32767.0
f32 = jnp.float32
bf16 = jnp.bfloat16


def split_table(table):
    high = table.astype(ml_dtypes.bfloat16)
    low = (table - high.astype(np.float64)).astype(ml_dtypes.bfloat16)
    return high, low


def lane_tables():
    position = np.arange(L)
    angle = 2.0 * np.pi * (np.outer(position, position) % L) / L
    sign = np.array([[1.0, 1.0], [1.0, -1.0]])
    real = np.kron(sign, np.cos(angle))
    imag = np.kron(sign, -np.sin(angle))
    forward = np.block([[real, imag], [-imag, real]])
    inverse = np.block([[real, -imag], [imag, real]])
    return np.stack(split_table(forward)), np.stack(split_table(inverse))


def row_tables():
    position = np.arange(L)
    angle = 2.0 * np.pi * (np.outer(position, position) % L) / L
    both = np.concatenate([np.cos(angle), np.sin(angle)], 0)
    forwards, inverses = [], []
    for core in range(2):
        order = np.concatenate([np.arange(HALF) + HALF * core, np.arange(HALF) + HALF * (1 - core)])
        high, low = split_table(both[:, order])
        forwards.append(np.concatenate([high, high, low], 1))
        back = np.concatenate([both[:L, order].T, both[L:, order].T], 0)
        high, low = split_table(back)
        inverses.append(np.concatenate([high, high, low], 1))
    return np.stack(forwards), np.stack(inverses)


def filter_table():
    wrapped = np.arange(L)
    wrapped = np.where(wrapped >= HALF, wrapped - L, wrapped)
    squares = (wrapped * (2.0 * np.pi / (L * spacing))) ** 2
    ky = np.arange(ROWS)[:, None] + HALF * np.arange(2)[None, :]
    total = squares[None, :, None, None] + squares[ky][:, None, :, None] + squares[None, None, None, :]
    kernel = np.where(total > 0, 4.0 * np.pi / np.where(total > 0, total, 1.0), 0.0)
    return (-fraction / L**3 * kernel).reshape(ROWS, L, LANES).astype(np.float32)


def twiddle_table():
    odd = np.repeat(np.arange(2), L)
    angle = 2.0 * np.pi * np.outer(np.arange(ROWS), odd) / L
    return np.stack([np.cos(angle), -np.sin(angle)], 1).astype(np.float32)


def real_forward(values):
    count = len(values)
    if count == 2:
        return [values[0] + values[1], values[0] - values[1]], [None, None]
    even_re, even_im = real_forward(values[0::2])
    odd_re, odd_im = real_forward(values[1::2])
    half, quarter = count // 2, count // 4
    re, im = [None] * (half + 1), [None] * (half + 1)
    re[0], re[half] = even_re[0] + odd_re[0], even_re[0] - odd_re[0]
    re[quarter], im[quarter] = even_re[quarter], -odd_re[quarter]
    for k in range(1, quarter):
        c, s = math.cos(2.0 * math.pi * k / count), math.sin(2.0 * math.pi * k / count)
        if 2 * k == quarter:
            turned_re, turned_im = c * (odd_re[k] + odd_im[k]), c * (odd_im[k] - odd_re[k])
        else:
            turned_re = c * odd_re[k] + s * odd_im[k]
            turned_im = c * odd_im[k] - s * odd_re[k]
        re[k], im[k] = even_re[k] + turned_re, even_im[k] + turned_im
        re[half - k], im[half - k] = even_re[k] - turned_re, turned_im - even_im[k]
    return re, im


def real_inverse(re, im):
    half = len(re) - 1
    count = 2 * half
    if count == 2:
        return [re[0] + re[1], re[0] - re[1]]
    quarter = half // 2
    even_re, even_im = [None] * (quarter + 1), [None] * (quarter + 1)
    odd_re, odd_im = [None] * (quarter + 1), [None] * (quarter + 1)
    even_re[0], odd_re[0] = re[0] + re[half], re[0] - re[half]
    even_re[quarter], odd_re[quarter] = 2.0 * re[quarter], -2.0 * im[quarter]
    for k in range(1, quarter):
        c, s = math.cos(2.0 * math.pi * k / count), math.sin(2.0 * math.pi * k / count)
        even_re[k], even_im[k] = re[k] + re[half - k], im[k] - im[half - k]
        part_re, part_im = re[k] - re[half - k], im[k] + im[half - k]
        if 2 * k == quarter:
            odd_re[k], odd_im[k] = c * (part_re - part_im), c * (part_re + part_im)
        else:
            odd_re[k] = c * part_re - s * part_im
            odd_im[k] = s * part_re + c * part_im
    evens, odds = real_inverse(even_re, even_im), real_inverse(odd_re, odd_im)
    return [value for pair in zip(evens, odds) for value in pair]


def split(values):
    high = values.astype(bf16)
    return high, (values - high.astype(f32)).astype(bf16)


def dot(left, right):
    return jnp.dot(left, right, preferred_element_type=f32)


def pair_kernel(
    blocks, half,
    orbitals, first_in, second_in, count_in,
    lane_fwd, lane_inv, row_fwd, row_inv, filters, twiddles,
    kept_out, codes_out, scales_out, next_second, next_count,
    orb, sending, arriving, kept, codes, scales,
    spectra_hi, spectra_lo, planes, others, filtered, returned, result,
    lane_fwd_v, lane_inv_v, row_fwd_v, row_inv_v, filters_v, twiddles_v, first_s, second_s, count_s,
    load_sem, table_sem, index_send, index_recv, orbital_send, orbital_recv,
    code_send, code_recv, scale_send, scale_recv, kept_sem,
    first_send, first_recv, second_send, second_recv,
):
    me, core = lax.axis_index("blk"), lax.axis_index("grid")
    right, left = lax.rem(me + 1, blocks), lax.rem(me + blocks - 1, blocks)
    to_right, to_left, to_partner = {"blk": right}, {"blk": left}, {"grid": 1 - core}

    barrier = pltpu.get_barrier_semaphore()
    for device in (to_right, to_left, to_partner):
        pl.semaphore_signal(barrier, inc=1, device_id=device)

    load = pltpu.make_async_copy(orbitals, orb, load_sem)
    load.start()
    base = 8 * core
    tables = [
        pltpu.make_async_copy(source, target, table_sem.at[place])
        for place, (source, target) in enumerate([
            (first_in, first_s), (second_in, second_s), (count_in, count_s),
            (lane_fwd, lane_fwd_v), (lane_inv, lane_inv_v),
            (row_fwd.at[core], row_fwd_v), (row_inv.at[core], row_inv_v),
            (filters.at[pl.ds(base, MINE)], filters_v), (twiddles, twiddles_v),
        ])
    ]
    for table in tables:
        table.start()

    def remote(source, target, send, recv, device):
        return pltpu.make_async_remote_copy(
            src_ref=source, dst_ref=target, send_sem=send, recv_sem=recv, device_id=device
        )

    index_copies = [
        remote(second_in, next_second, index_send.at[0], index_recv.at[0], to_left),
        remote(count_in, next_count, index_send.at[1], index_recv.at[1], to_left),
    ]
    pl.semaphore_wait(barrier, 3)
    for copy in index_copies:
        copy.start()
    for table in tables[:3]:
        table.wait()
    load.wait()

    def orbital_copy(m, device):
        return remote(sending.at[m], arriving.at[m], orbital_send.at[m], orbital_recv.at[m], device)

    for m in range(half, 2 * half):
        sending[m] = orb[first_s[0, m]]
        orbital_copy(m, to_left).start()
    for copy in index_copies:
        copy.wait()
    for m in range(half):
        sending[m] = orb[next_second[0, m]]
        orbital_copy(m, to_right).start()
    for table in tables[3:]:
        table.wait()

    def kept_copy(m):
        return pltpu.make_async_copy(kept.at[m], kept_out.at[m], kept_sem.at[m])

    def code_copy(m, device):
        return remote(codes.at[m], codes_out.at[m], code_send.at[m], code_recv.at[m], device)

    def scale_copy(m, device):
        return remote(scales.at[m], scales_out.at[m], scale_send.at[m], scale_recv.at[m], device)

    other_base = 8 * (1 - core)

    def first_copy(which):
        return remote(
            planes.at[which, pl.ds(other_base, MINE)], others.at[which],
            first_send.at[which], first_recv.at[which], to_partner,
        )

    def second_copy(which):
        return remote(
            filtered.at[which, pl.ds(core, 8)], returned.at[which, pl.ds(base + core, 8)],
            second_send.at[which], second_recv.at[which], to_partner,
        )

    def forward(which, left_part, right_part):
        def forward_group(group, carry):
            rows = pl.ds(pl.multiple_of(16 * group, 16), 16)
            values = []
            for column in range(HALF):
                lanes = pl.ds(LANES * column, LANES)
                values.append(left_part(rows, lanes).astype(f32) * right_part(rows, lanes).astype(f32))
            re, im = real_forward(values)
            for k in range(ROWS):
                if k == 0:
                    turned_re, turned_im = re[0], jnp.zeros_like(re[0])
                else:
                    c, s = twiddles_v[k, 0:1], twiddles_v[k, 1:2]
                    if im[k] is None:
                        turned_re, turned_im = re[k] * c, re[k] * s
                    else:
                        turned_re, turned_im = re[k] * c - im[k] * s, re[k] * s + im[k] * c
                for part, value in enumerate((turned_re, turned_im)):
                    high, low = split(value)
                    spectra_hi[k, rows, LANES * part : LANES * (part + 1)] = high
                    spectra_lo[k, rows, LANES * part : LANES * (part + 1)] = low
            return carry

        lax.fori_loop(0, 2, forward_group, 0)

        def to_planes(start, count):
            where = pl.ds(start, count)
            high = spectra_hi[where].reshape(count * HALF, 2 * LANES)
            low = spectra_lo[where].reshape(count * HALF, 2 * LANES)
            out = dot(high, lane_fwd_v[0]) + dot(low, lane_fwd_v[0]) + dot(high, lane_fwd_v[1])
            planes[which, where] = out.reshape(count, HALF, 2 * LANES)

        to_planes(other_base, MINE)
        first_copy(which).start()
        to_planes(base + core, 8)

    def solve(which):
        first_copy(which).wait()
        for k in range(MINE):
            values = jnp.concatenate([planes[which, base + k], others[which, k]], 0)
            high, low = split(values)
            out = dot(row_fwd_v[...], jnp.concatenate([high, low, high], 0))
            kernel = filters_v[k]
            re = (out[:L, :LANES] + out[L:, LANES:]) * kernel
            im = (out[:L, LANES:] - out[L:, :LANES]) * kernel
            high, low = split(jnp.concatenate([re, im], 1))
            out = dot(row_inv_v[...], jnp.concatenate([high, low, high], 0))
            re = out[:L, :LANES] - out[L:, LANES:]
            im = out[:L, LANES:] + out[L:, :LANES]
            whole = jnp.concatenate([re, im], 1)
            returned[which, base + k] = whole[:HALF]
            filtered[which, k] = whole[HALF:]
        second_copy(which).start()

    def inverse(which, m, live, here, came):
        def from_planes(start, count):
            where = pl.ds(start, count)
            values = returned[which, where].reshape(count * HALF, 2 * LANES)
            high, low = split(values)
            out = dot(high, lane_inv_v[0]) + dot(low, lane_inv_v[0]) + dot(high, lane_inv_v[1])
            result[where] = out.reshape(count, HALF, 2 * LANES)

        from_planes(base, MINE)
        second_copy(which).wait()
        from_planes(9 * (1 - core), 8)

        def inverse_group(group, carry):
            rows = pl.ds(pl.multiple_of(16 * group, 16), 16)
            re, im = [], []
            for k in range(ROWS):
                value_re = result[k, rows, :LANES]
                if k == 0:
                    re.append(value_re)
                    im.append(None)
                    continue
                value_im = result[k, rows, LANES:]
                c, s = twiddles_v[k, 0:1], twiddles_v[k, 1:2]
                re.append(value_re * c + value_im * s)
                im.append(None if k == ROWS - 1 else value_im * c - value_re * s)
            potential = real_inverse(re, im)
            terms, largest = [], None
            for column in range(HALF):
                lanes = pl.ds(LANES * column, LANES)
                value = potential[column] * live
                kept[m, rows, lanes] = value * came(rows, lanes).astype(f32)
                terms.append(value * here(rows, lanes).astype(f32))
                size = jnp.abs(terms[-1])
                largest = size if largest is None else jnp.maximum(largest, size)
            bound = jnp.maximum(jnp.max(largest, axis=1, keepdims=True), 1e-30)
            scales[m, rows, :] = jnp.broadcast_to(bound * (1.0 / CODE), (16, LANES))
            inverse_scale = CODE / bound
            for column in range(HALF):
                lanes = pl.ds(LANES * column, LANES)
                code = jnp.round(terms[column] * inverse_scale)
                codes[m, rows, lanes] = code.astype(jnp.int32).astype(jnp.int16)
            return carry

        lax.fori_loop(0, 2, inverse_group, 0)
        kept_copy(m).start()

    def one_stage(stage, carry):
        mine, second = first_s[0, stage], next_second[0, half + stage]
        pairs = (
            (lambda rows, lanes: orb[mine, rows, lanes], lambda rows, lanes: arriving[stage, rows, lanes]),
            (lambda rows, lanes: orb[second, rows, lanes], lambda rows, lanes: arriving[half + stage, rows, lanes]),
        )
        orbital_copy(half + stage, to_left).wait_recv()
        forward(1, *pairs[1])
        orbital_copy(stage, to_right).wait_recv()
        forward(0, *pairs[0])
        solve(1)
        solve(0)
        inverse(1, half + stage, jnp.where(half + stage < next_count[0], 1.0, 0.0).astype(f32), *pairs[1])
        code_copy(half + stage, to_right).start()
        scale_copy(half + stage, to_right).start()
        inverse(0, stage, jnp.where(stage < count_s[0], 1.0, 0.0).astype(f32), *pairs[0])
        code_copy(stage, to_left).start()
        scale_copy(stage, to_left).start()
        return carry

    lax.fori_loop(0, half, one_stage, 0)
    for m in range(2 * half):
        orbital_copy(m, to_left).wait_send()
        kept_copy(m).wait()
        code_copy(m, to_left).wait()
        scale_copy(m, to_left).wait()


def exchange(orbitals, pair_first, pair_second, pair_count):
    blocks = lax.axis_size("blk")
    slots = pair_first.shape[1]
    block, rows, cells = orbitals.shape
    lane_fwd, lane_inv = lane_tables()
    row_fwd, row_inv = row_tables()
    tables = [jnp.asarray(t) for t in (lane_fwd, lane_inv, row_fwd, row_inv, filter_table(), twiddle_table())]
    anywhere, smem = (pl.BlockSpec(memory_space=space) for space in (pl.ANY, pltpu.SMEM))
    dma, dmas = pltpu.SemaphoreType.DMA, lambda *shape: pltpu.SemaphoreType.DMA(shape)
    return pl.pallas_call(
        functools.partial(pair_kernel, blocks, slots // 2),
        out_shape=[
            jax.ShapeDtypeStruct((slots, rows, cells), f32),
            jax.ShapeDtypeStruct((slots, rows, cells), jnp.int16),
            jax.ShapeDtypeStruct((slots, rows, LANES), f32),
            jax.ShapeDtypeStruct(pair_second.shape, jnp.int32),
            jax.ShapeDtypeStruct(pair_count.shape, jnp.int32),
        ],
        in_specs=[anywhere] * (4 + len(tables)),
        out_specs=[anywhere, anywhere, anywhere, smem, smem],
        scratch_shapes=[
            pltpu.VMEM((block, rows, cells), bf16),
            pltpu.VMEM((slots, rows, cells), bf16),
            pltpu.VMEM((slots, rows, cells), bf16),
            pltpu.VMEM((slots, rows, cells), f32),
            pltpu.VMEM((slots, rows, cells), jnp.int16),
            pltpu.VMEM((slots, rows, LANES), f32),
            pltpu.VMEM((ROWS, HALF, 2 * LANES), bf16),
            pltpu.VMEM((ROWS, HALF, 2 * LANES), bf16),
            pltpu.VMEM((2, ROWS, HALF, 2 * LANES), f32),
            pltpu.VMEM((2, MINE, HALF, 2 * LANES), f32),
            pltpu.VMEM((2, MINE, HALF, 2 * LANES), f32),
            pltpu.VMEM((2, ROWS, HALF, 2 * LANES), f32),
            pltpu.VMEM((ROWS, HALF, 2 * LANES), f32),
            pltpu.VMEM(lane_fwd.shape, bf16),
            pltpu.VMEM(lane_inv.shape, bf16),
            pltpu.VMEM(row_fwd.shape[1:], bf16),
            pltpu.VMEM(row_inv.shape[1:], bf16),
            pltpu.VMEM((MINE, L, LANES), f32),
            pltpu.VMEM((ROWS, 2, LANES), f32),
            pltpu.SMEM(pair_first.shape, jnp.int32),
            pltpu.SMEM(pair_second.shape, jnp.int32),
            pltpu.SMEM(pair_count.shape, jnp.int32),
            dma, dmas(9), dmas(2), dmas(2), dmas(slots), dmas(slots),
            dmas(slots), dmas(slots), dmas(slots), dmas(slots), dmas(slots),
            dmas(2), dmas(2), dmas(2), dmas(2),
        ],
        compiler_params=pltpu.CompilerParams(
            collective_id=0, has_side_effects=True, vmem_limit_bytes=60 * 2**20
        ),
        name="pair_exchange",
    )(orbitals, pair_first, pair_second, pair_count, *tables)


def merge_kernel(
    half, block, kept_in, codes_in, scales_in, first, count, second, second_count,
    out, kept, codes, scales, total, zero, staged, kept_sem, code_sem, scale_sem, out_sem,
):
    slots = 2 * half
    pieces, width = 8, zero.shape[1] // 8

    def own_live(slot):
        return slot < count[0]

    def back_live(slot):
        return slot < second_count[0]

    loads = []
    for m in range(slots):
        kept_live, code_live = (own_live(m), back_live(m)) if m < half else (back_live(m), own_live(m))
        loads.append((kept_live, pltpu.make_async_copy(kept_in.at[m], kept.at[m], kept_sem.at[m])))
        loads.append((code_live, pltpu.make_async_copy(codes_in.at[m], codes.at[m], code_sem.at[m])))
        loads.append((code_live, pltpu.make_async_copy(scales_in.at[m], scales.at[m], scale_sem.at[m])))
    for needed, load in loads:
        pl.when(needed)(load.start)
    zero[...] = jnp.zeros_like(zero)

    for row in range(block):
        touched = jnp.bool_(False)
        for slot in range(slots):
            touched |= own_live(slot) & (first[0, slot] == row)
            touched |= back_live(slot) & (second[0, slot] == row)

        @pl.when(jnp.logical_not(touched))
        def _():
            pltpu.make_async_copy(zero, out.at[row], out_sem).start()

    for needed, load in loads:
        pl.when(needed)(load.wait)

    def over_pieces(body):
        def piece(index, carry):
            body(pl.ds(pl.multiple_of(width * index, width), width))
            return carry

        lax.fori_loop(0, pieces, piece, 0)

    def term(is_kept, m, lanes):
        if is_kept:
            return kept[m, :, lanes]
        return codes[m, :, lanes].astype(f32) * scales[m, :, 0:1]

    def add_up(place, kind_half, lead, live, rows, extra):
        several = jnp.bool_(False)
        for later in range(lead + 1, slots):
            several |= live(later) & (rows[0, later] == rows[0, lead])
        for flag, other in extra:
            several |= flag

        @pl.when(jnp.logical_not(several))
        def _():
            def only(lanes):
                staged[place, :, lanes] = term(kind_half(lead), lead, lanes).astype(bf16)

            over_pieces(only)

        @pl.when(several)
        def _():
            def begin(lanes):
                total[:, lanes] = term(kind_half(lead), lead, lanes)

            over_pieces(begin)
            for later in range(lead + 1, slots):

                @pl.when(live(later) & (rows[0, later] == rows[0, lead]))
                def _():
                    def more(lanes):
                        total[:, lanes] += term(kind_half(later), later, lanes)

                    over_pieces(more)

            for flag, other in extra:

                @pl.when(flag)
                def _():
                    def more(lanes):
                        total[:, lanes] += staged[other, :, lanes].astype(f32)

                    over_pieces(more)

            def end(lanes):
                staged[place, :, lanes] = total[:, lanes].astype(bf16)

            over_pieces(end)

    leads = []
    for slot in range(slots):
        lead = back_live(slot)
        for earlier in range(slot):
            lead &= second[0, earlier] != second[0, slot]
        leads.append(lead)

        @pl.when(lead)
        def _():
            add_up(slot, lambda s: s >= half, slot, back_live, second, [])
            owned = jnp.bool_(False)
            for other in range(slots):
                owned |= own_live(other) & (first[0, other] == second[0, slot])

            @pl.when(jnp.logical_not(owned))
            def _():
                pltpu.make_async_copy(staged.at[slot], out.at[second[0, slot]], out_sem).start()

    for slot in range(slots):
        lead = own_live(slot)
        for earlier in range(slot):
            lead &= first[0, earlier] != first[0, slot]

        @pl.when(lead)
        def _():
            extra = [(leads[other] & (second[0, other] == first[0, slot]), other) for other in range(slots)]
            add_up(slots + slot, lambda s: s < half, slot, own_live, first, extra)
            pltpu.make_async_copy(staged.at[slots + slot], out.at[first[0, slot]], out_sem).start()

    pltpu.make_async_copy(out, out, out_sem).wait()


def merge(kept, codes, scales, pair_first, pair_count, next_second, next_count, shape):
    slots, rows, cells = kept.shape
    anywhere, smem = (pl.BlockSpec(memory_space=space) for space in (pl.ANY, pltpu.SMEM))
    dma, dmas = pltpu.SemaphoreType.DMA, pltpu.SemaphoreType.DMA((slots,))
    return pl.pallas_call(
        functools.partial(merge_kernel, slots // 2, shape[0]),
        out_shape=jax.ShapeDtypeStruct(shape, bf16),
        in_specs=[anywhere] * 3 + [smem] * 4,
        out_specs=anywhere,
        scratch_shapes=[
            pltpu.VMEM(kept.shape, f32),
            pltpu.VMEM(codes.shape, jnp.int16),
            pltpu.VMEM(scales.shape, f32),
            pltpu.VMEM((rows, cells), f32),
            pltpu.VMEM((rows, cells), bf16),
            pltpu.VMEM((2 * slots, rows, cells), bf16),
            dmas, dmas, dmas, dma,
        ],
        compiler_params=pltpu.CompilerParams(vmem_limit_bytes=60 * 2**20),
        name="merge_rows",
    )(kept, codes, scales, pair_first, pair_count, next_second, next_count)


def per_device(orbitals, pair_first, pair_second, pair_count):
    kept, codes, scales, next_second, next_count = exchange(orbitals, pair_first, pair_second, pair_count)
    return merge(kept, codes, scales, pair_first, pair_count, next_second, next_count, orbitals.shape)


def solution(mesh):
    return jax.shard_map(
        per_device,
        mesh=mesh,
        in_specs=(P("blk", "grid", None), P("blk", None), P("blk", None), P("blk")),
        out_specs=P("blk", "grid", None),
        check_vma=False,
    )
```

```python
import functools
import math

import jax
import jax.numpy as jnp
import ml_dtypes
import numpy as np
from jax import lax
from jax.experimental import pallas as pl
from jax.experimental.pallas import tpu as pltpu
from jax.sharding import PartitionSpec as P

spacing = 0.5
fraction = 0.25
L = 64
HALF = L // 2
LANES = 128
ROWS = 17
MINE = 9
CODE = 32767.0
f32 = jnp.float32
bf16 = jnp.bfloat16


def split_table(table):
    high = table.astype(ml_dtypes.bfloat16)
    low = (table - high.astype(np.float64)).astype(ml_dtypes.bfloat16)
    return high, low


def lane_tables():
    position = np.arange(L)
    angle = 2.0 * np.pi * (np.outer(position, position) % L) / L
    sign = np.array([[1.0, 1.0], [1.0, -1.0]])
    real = np.kron(sign, np.cos(angle))
    imag = np.kron(sign, -np.sin(angle))
    forward = np.block([[real, imag], [-imag, real]])
    inverse = np.block([[real, -imag], [imag, real]])
    (forward, low), (inverse, inverse_low) = split_table(forward), split_table(inverse)
    return np.concatenate([forward, forward, low]), np.concatenate([inverse, inverse, inverse_low])


def row_tables():
    position = np.arange(L)
    angle = 2.0 * np.pi * (np.outer(position, position) % L) / L
    both = np.concatenate([np.cos(angle), np.sin(angle)], 0)
    forwards, inverses = [], []
    for core in range(2):
        order = np.concatenate([np.arange(HALF) + HALF * core, np.arange(HALF) + HALF * (1 - core)])
        high, low = split_table(both[:, order])
        forwards.append(np.concatenate([high, high, low], 1))
        back = np.concatenate([both[:L, order].T, both[L:, order].T], 0)
        high, low = split_table(back)
        inverses.append(np.concatenate([high, high, low], 1))
    return np.stack(forwards), np.stack(inverses)


def filter_table():
    wrapped = np.arange(L)
    wrapped = np.where(wrapped >= HALF, wrapped - L, wrapped)
    squares = (wrapped * (2.0 * np.pi / (L * spacing))) ** 2
    ky = np.arange(ROWS)[:, None] + HALF * np.arange(2)[None, :]
    total = squares[None, :, None, None] + squares[ky][:, None, :, None] + squares[None, None, None, :]
    kernel = np.where(total > 0, 4.0 * np.pi / np.where(total > 0, total, 1.0), 0.0)
    return (-fraction / L**3 * kernel).reshape(ROWS, L, LANES).astype(np.float32)


def twiddle_table():
    odd = np.repeat(np.arange(2), L)
    angle = 2.0 * np.pi * np.outer(np.arange(ROWS), odd) / L
    return np.stack([np.cos(angle), -np.sin(angle)], 1).astype(np.float32)


def real_forward(values):
    count = len(values)
    if count == 2:
        return [values[0] + values[1], values[0] - values[1]], [None, None]
    even_re, even_im = real_forward(values[0::2])
    odd_re, odd_im = real_forward(values[1::2])
    half, quarter = count // 2, count // 4
    re, im = [None] * (half + 1), [None] * (half + 1)
    re[0], re[half] = even_re[0] + odd_re[0], even_re[0] - odd_re[0]
    re[quarter], im[quarter] = even_re[quarter], -odd_re[quarter]
    for k in range(1, quarter):
        c, s = math.cos(2.0 * math.pi * k / count), math.sin(2.0 * math.pi * k / count)
        if 2 * k == quarter:
            turned_re, turned_im = c * (odd_re[k] + odd_im[k]), c * (odd_im[k] - odd_re[k])
        else:
            turned_re = c * odd_re[k] + s * odd_im[k]
            turned_im = c * odd_im[k] - s * odd_re[k]
        re[k], im[k] = even_re[k] + turned_re, even_im[k] + turned_im
        re[half - k], im[half - k] = even_re[k] - turned_re, turned_im - even_im[k]
    return re, im


def real_inverse(re, im):
    half = len(re) - 1
    count = 2 * half
    if count == 2:
        return [re[0] + re[1], re[0] - re[1]]
    quarter = half // 2
    even_re, even_im = [None] * (quarter + 1), [None] * (quarter + 1)
    odd_re, odd_im = [None] * (quarter + 1), [None] * (quarter + 1)
    even_re[0], odd_re[0] = re[0] + re[half], re[0] - re[half]
    even_re[quarter], odd_re[quarter] = 2.0 * re[quarter], -2.0 * im[quarter]
    for k in range(1, quarter):
        c, s = math.cos(2.0 * math.pi * k / count), math.sin(2.0 * math.pi * k / count)
        even_re[k], even_im[k] = re[k] + re[half - k], im[k] - im[half - k]
        part_re, part_im = re[k] - re[half - k], im[k] + im[half - k]
        if 2 * k == quarter:
            odd_re[k], odd_im[k] = c * (part_re - part_im), c * (part_re + part_im)
        else:
            odd_re[k] = c * part_re - s * part_im
            odd_im[k] = s * part_re + c * part_im
    evens, odds = real_inverse(even_re, even_im), real_inverse(odd_re, odd_im)
    return [value for pair in zip(evens, odds) for value in pair]


def split(values):
    high = values.astype(bf16)
    return high, (values - high.astype(f32)).astype(bf16)


def dot(left, right):
    return jnp.dot(left, right, preferred_element_type=f32)


def pair_kernel(
    blocks, slots,
    orbitals, first_in, second_in, count_in,
    lane_fwd, lane_inv, row_fwd, row_inv, filters, twiddles,
    kept_out, codes_out, scales_out, info,
    orb, sending, arriving, kept, codes, scales,
    spectra, planes, others, filtered, returned, result,
    lane_fwd_v, lane_inv_v, row_fwd_v, row_inv_v, filters_v, twiddles_v, first_s, second_s, count_s,
    next_second, next_count, relay_second, relay_count, final_here, relay_send, relay_recv, load_sem, table_sem, index_send, index_recv, orbital_send, orbital_recv,
    code_send, code_recv, scale_send, scale_recv, kept_sem,
    first_send, first_recv, second_send, second_recv,
):
    half = slots // 2
    me, core = lax.axis_index("blk"), lax.axis_index("grid")
    right, left = lax.rem(me + 1, blocks), lax.rem(me + blocks - 1, blocks)
    to_right, to_left, to_partner = {"blk": right}, {"blk": left}, {"grid": 1 - core}

    final, relay = blocks - 1, max(2, blocks // 4) - 1
    is_first, is_final, is_relay = me == 0, me == final, me == relay
    barrier = pltpu.get_barrier_semaphore()
    for device in (to_left, to_partner):
        pl.semaphore_signal(barrier, inc=1, device_id=device)

    @pl.when(jnp.logical_not(is_final))
    def _():
        pl.semaphore_signal(barrier, inc=1, device_id=to_right)

    @pl.when(is_relay)
    def _():
        pl.semaphore_signal(barrier, inc=1, device_id={"blk": 0})
        pl.semaphore_signal(barrier, inc=1, device_id={"blk": final})

    load = pltpu.make_async_copy(orbitals, orb, load_sem)
    load.start()
    base = 8 * core
    tables = [
        pltpu.make_async_copy(source, target, table_sem.at[place])
        for place, (source, target) in enumerate([
            (first_in, first_s), (second_in, second_s), (count_in, count_s),
            (lane_fwd, lane_fwd_v), (lane_inv, lane_inv_v),
            (row_fwd.at[core], row_fwd_v), (row_inv.at[core], row_inv_v),
            (filters.at[pl.ds(base, MINE)], filters_v), (twiddles, twiddles_v),
        ])
    ]
    for table in tables:
        table.start()

    def remote(source, target, send, recv, device):
        return pltpu.make_async_remote_copy(
            src_ref=source, dst_ref=target, send_sem=send, recv_sem=recv, device_id=device
        )

    def index_copies(targets, sent, arrived, device, sources=(second_in, count_in)):
        return [
            remote(source, target, sent.at[part], arrived.at[part], device)
            for part, (source, target) in enumerate(zip(sources, targets))
        ]

    to_next = index_copies((next_second, next_count), index_send, index_recv, to_left)
    to_relay = index_copies((relay_second, relay_count), index_send, relay_recv, {"blk": relay})

    def orbital_copy(m, group, device):
        part = pl.ds(16 * group, 16)
        return remote(
            sending.at[m, part], arriving.at[m, part], orbital_send.at[m, group], orbital_recv.at[m, group], device
        )

    def send_first(m, device):
        for group in range(2):
            orbital_copy(m, group, device).start()

    def load_own():
        for table in tables[:3]:
            table.wait()
        load.wait()
        for m in range(half, slots):
            sending[m] = orb[first_s[0, m]]

    def load_visits():
        for copy in to_next:
            copy.wait_recv()
        for m in range(half):
            sending[m] = orb[next_second[0, m]]

    @pl.when(jnp.logical_not(is_final))
    def _():
        pl.semaphore_wait(barrier, 3)

    @pl.when(is_final)
    def _():
        pl.semaphore_wait(barrier, 4)
        pl.semaphore_signal(final_here, inc=1, device_id=to_right)
        pl.semaphore_signal(final_here, inc=1, device_id={"blk": relay})

    @pl.when(is_first)
    def _():
        for copy in to_relay:
            copy.start()
        load_own()
        load_visits()
        send_first(0, to_right)
        pl.semaphore_wait(final_here, 1)
        send_first(half, to_left)

    @pl.when(jnp.logical_not(is_first))
    def _():
        for copy in to_next:
            copy.start()
        load_own()
        send_first(half, to_left)

        @pl.when(is_relay)
        def _():
            for copy in to_relay:
                copy.wait_recv()
            pl.semaphore_wait(final_here, 1)
            onward = index_copies(
                (next_second, next_count), relay_send, index_recv, {"blk": final}, (relay_second, relay_count)
            )
            for copy in onward:
                copy.start()
            for copy in onward:
                copy.wait_send()

        load_visits()
        send_first(0, to_right)

    for copy in to_next:
        copy.wait_send()
    for stage in range(1, half):
        for group in range(2):
            for m, device in ((half + stage, to_left), (stage, to_right)):
                orbital_copy(m - 1, group, device).wait_send()
                orbital_copy(m, group, device).start()
    for table in tables[3:]:
        table.wait()

    def kept_copy(m):
        return pltpu.make_async_copy(kept.at[m], kept_out.at[m], kept_sem.at[m])

    def code_copy(m, group, device):
        part = pl.ds(16 * group, 16)
        return remote(
            codes.at[m, part], codes_out.at[m, part], code_send.at[m, group], code_recv.at[m, group], device
        )

    def scale_copy(m, device):
        return remote(scales.at[m], scales_out.at[m], scale_send.at[m], scale_recv.at[m], device)

    other_base = 8 * (1 - core)

    def first_copy(which):
        return remote(
            planes.at[which, pl.ds(other_base, MINE)], others.at[which],
            first_send.at[which], first_recv.at[which], to_partner,
        )

    def second_copy(which):
        return remote(
            filtered.at[which, pl.ds(core, 8)], returned.at[which, pl.ds(base + core, 8)],
            second_send.at[which], second_recv.at[which], to_partner,
        )

    def forward(stage, which):
        m, here = stage + half * which, jnp.where(which == 0, first_s[0, stage], next_second[0, half + stage])

        def forward_group(group, carry):
            orbital_copy(m, group, to_left).wait_recv()
            rows = pl.ds(pl.multiple_of(16 * group, 16), 16)
            values = []
            for column in range(HALF):
                lanes = pl.ds(LANES * column, LANES)
                values.append(orb[here, rows, lanes].astype(f32) * arriving[m, rows, lanes].astype(f32))
            re, im = real_forward(values)
            for k in range(ROWS):
                if k == 0:
                    turned_re, turned_im = re[0], jnp.zeros_like(re[0])
                else:
                    c, s = twiddles_v[k, 0:1], twiddles_v[k, 1:2]
                    if im[k] is None:
                        turned_re, turned_im = re[k] * c, re[k] * s
                    else:
                        turned_re, turned_im = re[k] * c - im[k] * s, re[k] * s + im[k] * c
                for part, value in enumerate((turned_re, turned_im)):
                    high, low = split(value)
                    for place, piece in enumerate((high, low, high)):
                        start = LANES * (2 * place + part)
                        spectra[k, rows, start : start + LANES] = piece
            return carry

        lax.fori_loop(0, 2, forward_group, 0)

        def to_planes(start, count):
            where = pl.ds(start, count)
            out = dot(spectra[where].reshape(count * HALF, 6 * LANES), lane_fwd_v[...])
            planes[which, where] = out.reshape(count, HALF, 2 * LANES)

        to_planes(other_base, MINE)
        first_copy(which).start()
        to_planes(base + core, 8)

    def solve(stage, which):
        first_copy(which).wait()
        for k in range(MINE):
            values = jnp.concatenate([planes[which, base + k], others[which, k]], 0)
            high, low = split(values)
            out = dot(row_fwd_v[...], jnp.concatenate([high, low, high], 0))
            kernel = filters_v[k]
            re = (out[:L, :LANES] + out[L:, LANES:]) * kernel
            im = (out[:L, LANES:] - out[L:, :LANES]) * kernel
            high, low = split(jnp.concatenate([re, im], 1))
            out = dot(row_inv_v[...], jnp.concatenate([high, low, high], 0))
            re = out[:L, :LANES] - out[L:, LANES:]
            im = out[:L, LANES:] + out[L:, :LANES]
            whole = jnp.concatenate([re, im], 1)
            returned[which, base + k] = whole[:HALF]
            filtered[which, k] = whole[HALF:]
        second_copy(which).start()

    def inverse(stage, which):
        m, here = stage + half * which, jnp.where(which == 0, first_s[0, stage], next_second[0, half + stage])
        live = jnp.where(m < jnp.where(which == 0, count_s[0], next_count[0]), 1.0, 0.0).astype(f32)
        device = {"blk": jnp.where(which == 0, left, right)}

        def from_planes(start, count):
            where = pl.ds(start, count)
            values = returned[which, where].reshape(count * HALF, 2 * LANES)
            high, low = split(values)
            out = dot(jnp.concatenate([high, low, high], 1), lane_inv_v[...])
            result[where] = out.reshape(count, HALF, 2 * LANES)

        from_planes(base, MINE)
        second_copy(which).wait()
        from_planes(9 * (1 - core), 8)

        def inverse_group(group, carry):
            rows = pl.ds(pl.multiple_of(16 * group, 16), 16)
            re, im = [], []
            for k in range(ROWS):
                value_re = result[k, rows, :LANES]
                if k == 0:
                    re.append(value_re)
                    im.append(None)
                    continue
                value_im = result[k, rows, LANES:]
                c, s = twiddles_v[k, 0:1], twiddles_v[k, 1:2]
                re.append(value_re * c + value_im * s)
                im.append(None if k == ROWS - 1 else value_im * c - value_re * s)
            potential = real_inverse(re, im)
            terms, largest = [], None
            for column in range(HALF):
                lanes = pl.ds(LANES * column, LANES)
                value = potential[column] * live
                kept[m, rows, lanes] = value * arriving[m, rows, lanes].astype(f32)
                terms.append(value * orb[here, rows, lanes].astype(f32))
                size = jnp.abs(terms[-1])
                largest = size if largest is None else jnp.maximum(largest, size)
            bound = jnp.maximum(jnp.max(largest, axis=1, keepdims=True), 1e-30)
            scales[m, rows, :] = jnp.broadcast_to(bound * (1.0 / CODE), (16, LANES))
            inverse_scale = CODE / bound
            for column in range(HALF):
                lanes = pl.ds(LANES * column, LANES)
                code = jnp.round(terms[column] * inverse_scale)
                codes[m, rows, lanes] = code.astype(jnp.int32).astype(jnp.int16)
            code_copy(m, group, device).start()
            return carry

        lax.fori_loop(0, 2, inverse_group, 0)
        scale_copy(m, device).start()
        kept_copy(m).start()

    def one_stage(stage, carry):
        for phase in (forward, solve, inverse):
            def one_slot(turn, carry):
                phase(stage, 1 - turn)
                return carry

            lax.fori_loop(0, 2, one_slot, 0)
        return carry

    for m in range(slots):
        info[0, m] = first_s[0, m]
        info[0, slots + m] = next_second[0, m]
    info[0, 2 * slots] = count_s[0]
    info[0, 2 * slots + 1] = next_count[0]

    lax.fori_loop(0, half, one_stage, 0)
    for m in range(slots):
        device = to_left if m < half else to_right
        for group in range(2):
            if m % half == half - 1:
                orbital_copy(m, group, device).wait_send()
            code_copy(m, group, device).wait()
        scale_copy(m, device).wait()
        kept_copy(m).wait()


def exchange(orbitals, pair_first, pair_second, pair_count):
    blocks = lax.axis_size("blk")
    slots = pair_first.shape[1]
    block, rows, cells = orbitals.shape
    lane_fwd, lane_inv = lane_tables()
    row_fwd, row_inv = row_tables()
    tables = [jnp.asarray(t) for t in (lane_fwd, lane_inv, row_fwd, row_inv, filter_table(), twiddle_table())]
    anywhere, smem = (pl.BlockSpec(memory_space=space) for space in (pl.ANY, pltpu.SMEM))
    dma, dmas = pltpu.SemaphoreType.DMA, lambda *shape: pltpu.SemaphoreType.DMA(shape)
    return pl.pallas_call(
        functools.partial(pair_kernel, blocks, slots),
        out_shape=[
            jax.ShapeDtypeStruct((slots, rows, cells), f32),
            jax.ShapeDtypeStruct((slots, rows, cells), jnp.int16),
            jax.ShapeDtypeStruct((slots, rows, LANES), f32),
            jax.ShapeDtypeStruct((1, 2 * slots + 2), jnp.int32),
        ],
        in_specs=[anywhere] * (4 + len(tables)),
        out_specs=[anywhere, anywhere, anywhere, smem],
        scratch_shapes=[
            pltpu.VMEM((block, rows, cells), bf16),
            pltpu.VMEM((slots, rows, cells), bf16),
            pltpu.VMEM((slots, rows, cells), bf16),
            pltpu.VMEM((slots, rows, cells), f32),
            pltpu.VMEM((slots, rows, cells), jnp.int16),
            pltpu.VMEM((slots, rows, LANES), f32),
            pltpu.VMEM((ROWS, HALF, 6 * LANES), bf16),
            pltpu.VMEM((2, ROWS, HALF, 2 * LANES), f32),
            pltpu.VMEM((2, MINE, HALF, 2 * LANES), f32),
            pltpu.VMEM((2, MINE, HALF, 2 * LANES), f32),
            pltpu.VMEM((2, ROWS, HALF, 2 * LANES), f32),
            pltpu.VMEM((ROWS, HALF, 2 * LANES), f32),
            pltpu.VMEM(lane_fwd.shape, bf16),
            pltpu.VMEM(lane_inv.shape, bf16),
            pltpu.VMEM(row_fwd.shape[1:], bf16),
            pltpu.VMEM(row_inv.shape[1:], bf16),
            pltpu.VMEM((MINE, L, LANES), f32),
            pltpu.VMEM((ROWS, 2, LANES), f32),
            pltpu.SMEM(pair_first.shape, jnp.int32),
            pltpu.SMEM(pair_second.shape, jnp.int32),
            pltpu.SMEM(pair_count.shape, jnp.int32),
            pltpu.SMEM(pair_second.shape, jnp.int32),
            pltpu.SMEM(pair_count.shape, jnp.int32),
            pltpu.SMEM(pair_second.shape, jnp.int32),
            pltpu.SMEM(pair_count.shape, jnp.int32),
            pltpu.SemaphoreType.REGULAR, dmas(2), dmas(2),
            dma, dmas(9), dmas(2), dmas(2), dmas(slots, 2), dmas(slots, 2),
            dmas(slots, 2), dmas(slots, 2), dmas(slots), dmas(slots), dmas(slots),
            dmas(2), dmas(2), dmas(2), dmas(2),
        ],
        compiler_params=pltpu.CompilerParams(
            collective_id=0, has_side_effects=True, vmem_limit_bytes=60 * 2**20
        ),
        name="pair_exchange",
    )(orbitals, pair_first, pair_second, pair_count, *tables)


def merge_kernel(
    half, block, kept_in, codes_in, scales_in, info,
    out, kept, codes, scales, total, zero, staged, kept_sem, code_sem, scale_sem, out_sem,
):
    slots = 2 * half
    first = [info[0, slot] for slot in range(slots)]
    second = [info[0, slots + slot] for slot in range(slots)]
    count, second_count = info[0, 2 * slots], info[0, 2 * slots + 1]
    pieces, width = 8, zero.shape[1] // 8

    def own_live(slot):
        return slot < count

    def back_live(slot):
        return slot < second_count

    loads = []
    for m in range(slots):
        kept_live, code_live = (own_live(m), back_live(m)) if m < half else (back_live(m), own_live(m))
        loads.append((kept_live, pltpu.make_async_copy(kept_in.at[m], kept.at[m], kept_sem.at[m])))
        loads.append((code_live, pltpu.make_async_copy(codes_in.at[m], codes.at[m], code_sem.at[m])))
        loads.append((code_live, pltpu.make_async_copy(scales_in.at[m], scales.at[m], scale_sem.at[m])))
    for needed, load in loads:
        pl.when(needed)(load.start)
    zero[...] = jnp.zeros_like(zero)

    for row in range(block):
        touched = jnp.bool_(False)
        for slot in range(slots):
            touched |= own_live(slot) & (first[slot] == row)
            touched |= back_live(slot) & (second[slot] == row)

        @pl.when(jnp.logical_not(touched))
        def _():
            pltpu.make_async_copy(zero, out.at[row], out_sem).start()

    for needed, load in loads:
        pl.when(needed)(load.wait)

    def over_pieces(body):
        def piece(index, carry):
            body(pl.ds(pl.multiple_of(width * index, width), width))
            return carry

        lax.fori_loop(0, pieces, piece, 0)

    def term(is_kept, m, lanes):
        if is_kept:
            return kept[m, :, lanes]
        return codes[m, :, lanes].astype(f32) * scales[m, :, 0:1]

    def add_up(place, kind_half, lead, live, rows, extra):
        several = jnp.bool_(False)
        for later in range(lead + 1, slots):
            several |= live(later) & (rows[later] == rows[lead])
        for flag, other in extra:
            several |= flag

        @pl.when(jnp.logical_not(several))
        def _():
            def only(lanes):
                staged[place, :, lanes] = term(kind_half(lead), lead, lanes).astype(bf16)

            over_pieces(only)

        @pl.when(several)
        def _():
            def begin(lanes):
                total[:, lanes] = term(kind_half(lead), lead, lanes)

            over_pieces(begin)
            for later in range(lead + 1, slots):

                @pl.when(live(later) & (rows[later] == rows[lead]))
                def _():
                    def more(lanes):
                        total[:, lanes] += term(kind_half(later), later, lanes)

                    over_pieces(more)

            for flag, other in extra:

                @pl.when(flag)
                def _():
                    def more(lanes):
                        total[:, lanes] += staged[other, :, lanes].astype(f32)

                    over_pieces(more)

            def end(lanes):
                staged[place, :, lanes] = total[:, lanes].astype(bf16)

            over_pieces(end)

    leads = []
    for slot in range(slots):
        lead = back_live(slot)
        for earlier in range(slot):
            lead &= second[earlier] != second[slot]
        leads.append(lead)

        @pl.when(lead)
        def _():
            add_up(slot, lambda s: s >= half, slot, back_live, second, [])
            owned = jnp.bool_(False)
            for other in range(slots):
                owned |= own_live(other) & (first[other] == second[slot])

            @pl.when(jnp.logical_not(owned))
            def _():
                pltpu.make_async_copy(staged.at[slot], out.at[second[slot]], out_sem).start()

    for slot in range(slots):
        lead = own_live(slot)
        for earlier in range(slot):
            lead &= first[earlier] != first[slot]

        @pl.when(lead)
        def _():
            extra = [(leads[other] & (second[other] == first[slot]), other) for other in range(slots)]
            add_up(slots + slot, lambda s: s < half, slot, own_live, first, extra)
            pltpu.make_async_copy(staged.at[slots + slot], out.at[first[slot]], out_sem).start()

    pltpu.make_async_copy(out, out, out_sem).wait()


def merge(kept, codes, scales, info, shape):
    slots, rows, cells = kept.shape
    anywhere, smem = (pl.BlockSpec(memory_space=space) for space in (pl.ANY, pltpu.SMEM))
    dma, dmas = pltpu.SemaphoreType.DMA, pltpu.SemaphoreType.DMA((slots,))
    return pl.pallas_call(
        functools.partial(merge_kernel, slots // 2, shape[0]),
        out_shape=jax.ShapeDtypeStruct(shape, bf16),
        in_specs=[anywhere] * 3 + [smem],
        out_specs=anywhere,
        scratch_shapes=[
            pltpu.VMEM(kept.shape, f32),
            pltpu.VMEM(codes.shape, jnp.int16),
            pltpu.VMEM(scales.shape, f32),
            pltpu.VMEM((rows, cells), f32),
            pltpu.VMEM((rows, cells), bf16),
            pltpu.VMEM((2 * slots, rows, cells), bf16),
            dmas, dmas, dmas, dma,
        ],
        compiler_params=pltpu.CompilerParams(vmem_limit_bytes=60 * 2**20),
        name="merge_rows",
    )(kept, codes, scales, info)


def per_device(orbitals, pair_first, pair_second, pair_count):
    kept, codes, scales, info = exchange(orbitals, pair_first, pair_second, pair_count)
    return merge(kept, codes, scales, info, orbitals.shape)


def solution(mesh):
    return jax.shard_map(
        per_device,
        mesh=mesh,
        in_specs=(P("blk", "grid", None), P("blk", None), P("blk", None), P("blk")),
        out_specs=P("blk", "grid", None),
        check_vma=False,
    )
```

```python
import functools
import math

import jax
import jax.numpy as jnp
import ml_dtypes
import numpy as np
from jax import lax
from jax.experimental import pallas as pl
from jax.experimental.pallas import tpu as pltpu
from jax.sharding import PartitionSpec as P

spacing = 0.5
fraction = 0.25
L = 64
HALF = L // 2
LANES = 128
ROWS = 17
LOADS = 4
CODE = 32767.0
f32 = jnp.float32
bf16 = jnp.bfloat16


def split_table(table):
    high = table.astype(ml_dtypes.bfloat16)
    low = (table - high.astype(np.float64)).astype(ml_dtypes.bfloat16)
    return high, low


def lane_tables():
    position = np.arange(L)
    angle = 2.0 * np.pi * (np.outer(position, position) % L) / L
    sign = np.array([[1.0, 1.0], [1.0, -1.0]])
    real = np.kron(sign, np.cos(angle))
    imag = np.kron(sign, -np.sin(angle))
    forward = np.block([[real, imag], [-imag, real]])
    inverse = np.block([[real, -imag], [imag, real]])
    (forward, low), (inverse, inverse_low) = split_table(forward), split_table(inverse)
    return np.concatenate([forward, forward, low]), np.concatenate([inverse, inverse, inverse_low])


def row_tables():
    position = np.arange(L)
    angle = 2.0 * np.pi * (np.outer(position, position) % L) / L
    both = np.concatenate([np.cos(angle), np.sin(angle)], 0)
    high, low = split_table(both)
    table = np.concatenate([high, high, low], 1)
    return table, table


def filter_table():
    wrapped = np.arange(L)
    wrapped = np.where(wrapped >= HALF, wrapped - L, wrapped)
    squares = (wrapped * (2.0 * np.pi / (L * spacing))) ** 2
    ky = np.arange(ROWS)[:, None] + HALF * np.arange(2)[None, :]
    total = squares[None, :, None, None] + squares[ky][:, None, :, None] + squares[None, None, None, :]
    kernel = np.where(total > 0, 4.0 * np.pi / np.where(total > 0, total, 1.0), 0.0)
    return (-fraction / L**3 * kernel).reshape(ROWS, L, LANES).astype(np.float32)


def twiddle_table():
    odd = np.repeat(np.arange(2), L)
    angle = 2.0 * np.pi * np.outer(np.arange(ROWS), odd) / L
    return np.stack([np.cos(angle), -np.sin(angle)], 1).astype(np.float32)


def real_forward(values):
    count = len(values)
    if count == 2:
        return [values[0] + values[1], values[0] - values[1]], [None, None]
    even_re, even_im = real_forward(values[0::2])
    odd_re, odd_im = real_forward(values[1::2])
    half, quarter = count // 2, count // 4
    re, im = [None] * (half + 1), [None] * (half + 1)
    re[0], re[half] = even_re[0] + odd_re[0], even_re[0] - odd_re[0]
    re[quarter], im[quarter] = even_re[quarter], -odd_re[quarter]
    for k in range(1, quarter):
        c, s = math.cos(2.0 * math.pi * k / count), math.sin(2.0 * math.pi * k / count)
        if 2 * k == quarter:
            turned_re, turned_im = c * (odd_re[k] + odd_im[k]), c * (odd_im[k] - odd_re[k])
        else:
            turned_re = c * odd_re[k] + s * odd_im[k]
            turned_im = c * odd_im[k] - s * odd_re[k]
        re[k], im[k] = even_re[k] + turned_re, even_im[k] + turned_im
        re[half - k], im[half - k] = even_re[k] - turned_re, turned_im - even_im[k]
    return re, im


def real_inverse(re, im):
    half = len(re) - 1
    count = 2 * half
    if count == 2:
        return [re[0] + re[1], re[0] - re[1]]
    quarter = half // 2
    even_re, even_im = [None] * (quarter + 1), [None] * (quarter + 1)
    odd_re, odd_im = [None] * (quarter + 1), [None] * (quarter + 1)
    even_re[0], odd_re[0] = re[0] + re[half], re[0] - re[half]
    even_re[quarter], odd_re[quarter] = 2.0 * re[quarter], -2.0 * im[quarter]
    for k in range(1, quarter):
        c, s = math.cos(2.0 * math.pi * k / count), math.sin(2.0 * math.pi * k / count)
        even_re[k], even_im[k] = re[k] + re[half - k], im[k] - im[half - k]
        part_re, part_im = re[k] - re[half - k], im[k] + im[half - k]
        if 2 * k == quarter:
            odd_re[k], odd_im[k] = c * (part_re - part_im), c * (part_re + part_im)
        else:
            odd_re[k] = c * part_re - s * part_im
            odd_im[k] = s * part_re + c * part_im
    evens, odds = real_inverse(even_re, even_im), real_inverse(odd_re, odd_im)
    return [value for pair in zip(evens, odds) for value in pair]


def split(values):
    high = values.astype(bf16)
    return high, (values - high.astype(f32)).astype(bf16)


def dot(left, right):
    return jnp.dot(left, right, preferred_element_type=f32)


def pair_kernel(
    blocks, slots,
    orbitals, first_in, second_in, count_in,
    lane_fwd, lane_inv, row_fwd, row_inv, filters, twiddles,
    kept_out, codes_out, scales_out, info,
    orb, sending, arriving, sharing, whole, kept, codes, scales,
    spectra, planes, result,
    lane_fwd_v, lane_inv_v, row_fwd_v, row_inv_v, filters_v, twiddles_v, first_s, second_s, count_s,
    next_second, next_count, relay_second, relay_count, final_here, relay_send, relay_recv, load_sem,
    table_sem, index_send, index_recv, orbital_send, orbital_recv,
    share_send, share_recv, code_send, code_recv, scale_send, scale_recv, kept_sem, kept_send, kept_recv,
):
    half = slots // 2
    me, core = lax.axis_index("blk"), lax.axis_index("grid")
    right, left = lax.rem(me + 1, blocks), lax.rem(me + blocks - 1, blocks)
    to_partner = {"grid": 1 - core}

    final, relay = blocks - 1, max(2, blocks // 4) - 1
    is_first, is_final = me == 0, me == final
    sends_index, is_relay = core == 1, (me == relay) & (core == 1)
    barrier = pltpu.get_barrier_semaphore()
    for place in range(2):
        pl.semaphore_signal(barrier, inc=1, device_id={"blk": left, "grid": place})
    pl.semaphore_signal(barrier, inc=1, device_id=to_partner)

    @pl.when(jnp.logical_not(is_final))
    def _():
        for place in range(2):
            pl.semaphore_signal(barrier, inc=1, device_id={"blk": right, "grid": place})

    @pl.when(is_relay)
    def _():
        for device in ({"blk": 0, "grid": 1}, {"blk": final, "grid": 0}, {"blk": final, "grid": 1}):
            pl.semaphore_signal(barrier, inc=1, device_id=device)

    size = orb.shape[0] // LOADS
    loads = [
        pltpu.make_async_copy(orbitals.at[pl.ds(size * n, size)], orb.at[pl.ds(size * n, size)], load_sem.at[n])
        for n in range(LOADS)
    ]
    for load in loads:
        load.start()
    tables = [
        pltpu.make_async_copy(source, target, table_sem.at[place])
        for place, (source, target) in enumerate([
            (first_in, first_s), (second_in, second_s), (count_in, count_s),
            (lane_fwd, lane_fwd_v), (lane_inv, lane_inv_v), (row_fwd, row_fwd_v), (row_inv, row_inv_v),
            (filters, filters_v), (twiddles, twiddles_v),
        ])
    ]
    for table in tables:
        table.start()

    def remote(source, target, send, recv, device):
        return pltpu.make_async_remote_copy(
            src_ref=source, dst_ref=target, send_sem=send, recv_sem=recv, device_id=device
        )

    def index_copies(targets, sent, arrived, device, sources=(second_in, count_in)):
        return [
            remote(source, target, sent.at[part], arrived.at[part], device)
            for part, (source, target) in enumerate(zip(sources, targets))
        ]

    def to_both(block, sent, sources=(second_in, count_in)):
        targets = (next_second, next_count)
        return [
            copy
            for place in range(2)
            for copy in index_copies(targets, sent.at[place], index_recv, {"blk": block, "grid": place}, sources)
        ]

    to_next = to_both(left, index_send)
    to_relay = index_copies((relay_second, relay_count), index_send.at[0], relay_recv, {"blk": relay, "grid": 1})

    def orbital_copy(m, group):
        visits = m < half
        device = {"blk": right if visits else left, "grid": 1 if visits else 0}
        place = 2 * core + group
        return remote(
            sending.at[m, pl.ds(16 * group, 16)],
            arriving.at[m % half, pl.ds(pl.multiple_of(16 * place, 16), 16)],
            orbital_send.at[m, group], orbital_recv.at[m % half, place], device,
        )

    def arrival(stage, place):
        rows = pl.ds(pl.multiple_of(16 * place, 16), 16)
        return remote(
            sending.at[0, pl.ds(0, 16)], arriving.at[stage, rows],
            orbital_send.at[0, 0], orbital_recv.at[stage, place], to_partner,
        )

    def worked_on(stage, by):
        return jnp.where(by == 1, first_s[0, stage], next_second[0, half + stage])

    def share_copy(stage):
        rows = pl.ds(pl.multiple_of(HALF * core, HALF), HALF)
        return remote(sharing.at[stage], whole.at[stage, rows], share_send.at[stage], share_recv.at[stage], to_partner)

    def send_first(m):
        for group in range(2):
            orbital_copy(m, group).start()

    def load_own():
        for table in tables[:3]:
            table.wait()
        for load in loads:
            load.wait()
        for m in range(half, slots):
            sending[m] = orb[first_s[0, m]]

    def load_visits():
        for copy in to_next[:2]:
            copy.wait_recv()
        for m in range(half):
            sending[m] = orb[next_second[0, m]]

    normal = 5 + is_final.astype(jnp.int32)
    pl.semaphore_wait(barrier, jnp.where(is_first, 3 + core, normal))

    @pl.when(is_final)
    def _():
        for place in range(2):
            pl.semaphore_signal(final_here, inc=1, device_id={"blk": right, "grid": place})
        pl.semaphore_signal(final_here, inc=1, device_id={"blk": relay, "grid": 1})

    @pl.when(is_first)
    def _():
        @pl.when(sends_index)
        def _():
            for copy in to_relay:
                copy.start()

        load_own()
        load_visits()
        send_first(0)
        pl.semaphore_wait(final_here, 2)
        send_first(half)

        @pl.when(sends_index)
        def _():
            for copy in to_relay:
                copy.wait_send()

    @pl.when(jnp.logical_not(is_first))
    def _():
        @pl.when(sends_index)
        def _():
            for copy in to_next:
                copy.start()

        load_own()
        send_first(half)

        @pl.when(is_relay)
        def _():
            for copy in to_relay:
                copy.wait_recv()
            pl.semaphore_wait(final_here, 2)
            onward = to_both(final, relay_send, (relay_second, relay_count))
            for copy in onward:
                copy.start()
            for copy in onward:
                copy.wait_send()

        load_visits()
        send_first(0)

        @pl.when(sends_index)
        def _():
            for copy in to_next:
                copy.wait_send()

    for stage in range(half):
        sharing[stage] = orb[worked_on(stage, 1 - core)]
        share_copy(stage).start()
        whole[stage, pl.ds(pl.multiple_of(HALF * core, HALF), HALF)] = orb[worked_on(stage, core)]
    for stage in range(1, half):
        for group in range(2):
            for m in (half + stage, stage):
                orbital_copy(m - 1, group).wait_send()
                orbital_copy(m, group).start()
    for table in tables[3:]:
        table.wait()
    for m in range(slots):
        info[0, m] = first_s[0, m]
        info[0, slots + m] = next_second[0, m]
    info[0, 2 * slots] = count_s[0]
    info[0, 2 * slots + 1] = next_count[0]

    def solved(stage):
        return stage + half * (1 - core)

    def kept_local(stage):
        rows = pl.ds(pl.multiple_of(HALF * core, HALF), HALF)
        return pltpu.make_async_copy(kept.at[stage, rows], kept_out.at[solved(stage)], kept_sem.at[stage])

    def kept_remote(stage, m):
        rows = pl.ds(pl.multiple_of(HALF * (1 - core), HALF), HALF)
        return remote(kept.at[stage, rows], kept_out.at[m], kept_send.at[stage], kept_recv.at[stage], to_partner)

    def code_copy(stage, place, m):
        device = {"blk": jnp.where(core == 1, left, right), "grid": lax.div(place, 2)}
        rows = pl.ds(pl.multiple_of(16 * place, 16), 16)
        there = pl.ds(pl.multiple_of(16 * lax.rem(place, 2), 16), 16)
        return remote(
            codes.at[stage, rows], codes_out.at[m, there],
            code_send.at[stage, place], code_recv.at[m, lax.rem(place, 2)], device,
        )

    def scale_copy(stage, place, m):
        device = {"blk": jnp.where(core == 1, left, right), "grid": place}
        return remote(
            scales.at[stage, pl.ds(HALF * place, HALF)], scales_out.at[m],
            scale_send.at[stage, place], scale_recv.at[m], device,
        )

    def one_stage(stage, carry):
        m = solved(stage)
        share_copy(stage).wait_recv()

        def forward_group(turn, carry):
            place = 2 * lax.rem(turn, 2) + lax.div(turn, 2)
            rows = pl.ds(pl.multiple_of(16 * place, 16), 16)
            arrival(stage, place).wait_recv()
            values = []
            for column in range(HALF):
                lanes = pl.ds(LANES * column, LANES)
                values.append(whole[stage, rows, lanes].astype(f32) * arriving[stage, rows, lanes].astype(f32))
            re, im = real_forward(values)
            for k in range(ROWS):
                if k == 0:
                    turned_re, turned_im = re[0], jnp.zeros_like(re[0])
                else:
                    c, s = twiddles_v[k, 0:1], twiddles_v[k, 1:2]
                    if im[k] is None:
                        turned_re, turned_im = re[k] * c, re[k] * s
                    else:
                        turned_re, turned_im = re[k] * c - im[k] * s, re[k] * s + im[k] * c
                for part, value in enumerate((turned_re, turned_im)):
                    high, low = split(value)
                    for place, piece in enumerate((high, low, high)):
                        start = LANES * (2 * place + part)
                        spectra[k, :, start : start + LANES] = piece
            out = dot(spectra[...].reshape(ROWS * 16, 6 * LANES), lane_fwd_v[...])
            planes[:, rows, :] = out.reshape(ROWS, 16, 2 * LANES)
            return carry

        lax.fori_loop(0, 4, forward_group, 0)

        for k in range(ROWS):
            high, low = split(planes[k])
            out = dot(row_fwd_v[...], jnp.concatenate([high, low, high], 0))
            kernel = filters_v[k]
            re = (out[:L, :LANES] + out[L:, LANES:]) * kernel
            im = (out[:L, LANES:] - out[L:, :LANES]) * kernel
            high, low = split(jnp.concatenate([re, im], 1))
            out = dot(row_inv_v[...], jnp.concatenate([high, low, high], 0))
            re = out[:L, :LANES] - out[L:, LANES:]
            im = out[:L, LANES:] + out[L:, :LANES]
            planes[k] = jnp.concatenate([re, im], 1)

        live = jnp.where(m < jnp.where(core == 1, count_s[0], next_count[0]), 1.0, 0.0).astype(f32)

        def inverse_group(place, carry):
            rows = pl.ds(pl.multiple_of(16 * place, 16), 16)
            high, low = split(planes[:, rows, :].reshape(ROWS * 16, 2 * LANES))
            out = dot(jnp.concatenate([high, low, high], 1), lane_inv_v[...])
            result[...] = out.reshape(ROWS, 16, 2 * LANES)
            re, im = [], []
            for k in range(ROWS):
                value_re = result[k, :, :LANES]
                if k == 0:
                    re.append(value_re)
                    im.append(None)
                    continue
                value_im = result[k, :, LANES:]
                c, s = twiddles_v[k, 0:1], twiddles_v[k, 1:2]
                re.append(value_re * c + value_im * s)
                im.append(None if k == ROWS - 1 else value_im * c - value_re * s)
            potential = real_inverse(re, im)
            terms, largest = [], None
            for column in range(HALF):
                lanes = pl.ds(LANES * column, LANES)
                value = potential[column] * live
                kept[stage, rows, lanes] = value * arriving[stage, rows, lanes].astype(f32)
                terms.append(value * whole[stage, rows, lanes].astype(f32))
                size = jnp.abs(terms[-1])
                largest = size if largest is None else jnp.maximum(largest, size)
            bound = jnp.maximum(jnp.max(largest, axis=1, keepdims=True), 1e-30)
            scales[stage, rows, :] = jnp.broadcast_to(bound * (1.0 / CODE), (16, LANES))
            inverse_scale = CODE / bound
            for column in range(HALF):
                lanes = pl.ds(LANES * column, LANES)
                code = jnp.round(terms[column] * inverse_scale)
                codes[stage, rows, lanes] = code.astype(jnp.int32).astype(jnp.int16)
            code_copy(stage, place, m).start()
            return carry

        lax.fori_loop(0, 4, inverse_group, 0)
        for place in range(2):
            scale_copy(stage, place, m).start()
        kept_local(stage).start()
        kept_remote(stage, m).start()
        return carry

    lax.fori_loop(0, half, one_stage, 0)
    for stage in range(half):
        share_copy(stage).wait_send()
        kept_local(stage).wait()
        kept_remote(stage, stage + half * core).wait()
        for place in range(4):
            code_copy(stage, place, solved(stage)).wait_send()
        for place in range(2):
            scale_copy(stage, place, solved(stage)).wait_send()
    for m in range(slots):
        for group in range(2):
            if m % half == half - 1:
                orbital_copy(m, group).wait_send()
            code_copy(0, group, m).wait_recv()
        scale_copy(0, 0, m).wait_recv()


def exchange(orbitals, pair_first, pair_second, pair_count):
    blocks = lax.axis_size("blk")
    slots = pair_first.shape[1]
    block, rows, cells = orbitals.shape
    lane_fwd, lane_inv = lane_tables()
    row_fwd, row_inv = row_tables()
    tables = [jnp.asarray(t) for t in (lane_fwd, lane_inv, row_fwd, row_inv, filter_table(), twiddle_table())]
    anywhere, smem = (pl.BlockSpec(memory_space=space) for space in (pl.ANY, pltpu.SMEM))
    dma, dmas = pltpu.SemaphoreType.DMA, lambda *shape: pltpu.SemaphoreType.DMA(shape)
    half = slots // 2
    return pl.pallas_call(
        functools.partial(pair_kernel, blocks, slots),
        out_shape=[
            jax.ShapeDtypeStruct((slots, rows, cells), f32),
            jax.ShapeDtypeStruct((slots, rows, cells), jnp.int16),
            jax.ShapeDtypeStruct((slots, rows, LANES), f32),
            jax.ShapeDtypeStruct((1, 2 * slots + 2), jnp.int32),
        ],
        in_specs=[anywhere] * (4 + len(tables)),
        out_specs=[anywhere, anywhere, anywhere, smem],
        scratch_shapes=[
            pltpu.VMEM((block, rows, cells), bf16),
            pltpu.VMEM((slots, rows, cells), bf16),
            pltpu.VMEM((half, L, cells), bf16),
            pltpu.VMEM((half, rows, cells), bf16),
            pltpu.VMEM((half, L, cells), bf16),
            pltpu.VMEM((half, L, cells), f32),
            pltpu.VMEM((half, L, cells), jnp.int16),
            pltpu.VMEM((half, L, LANES), f32),
            pltpu.VMEM((ROWS, 16, 6 * LANES), bf16),
            pltpu.VMEM((ROWS, L, 2 * LANES), f32),
            pltpu.VMEM((ROWS, 16, 2 * LANES), f32),
            pltpu.VMEM(lane_fwd.shape, bf16),
            pltpu.VMEM(lane_inv.shape, bf16),
            pltpu.VMEM(row_fwd.shape, bf16),
            pltpu.VMEM(row_inv.shape, bf16),
            pltpu.VMEM((ROWS, L, LANES), f32),
            pltpu.VMEM((ROWS, 2, LANES), f32),
            pltpu.SMEM(pair_first.shape, jnp.int32),
            pltpu.SMEM(pair_second.shape, jnp.int32),
            pltpu.SMEM(pair_count.shape, jnp.int32),
            pltpu.SMEM(pair_second.shape, jnp.int32),
            pltpu.SMEM(pair_count.shape, jnp.int32),
            pltpu.SMEM(pair_second.shape, jnp.int32),
            pltpu.SMEM(pair_count.shape, jnp.int32),
            pltpu.SemaphoreType.REGULAR, dmas(2, 2), dmas(2), dmas(LOADS),
            dmas(9), dmas(2, 2), dmas(2), dmas(slots, 2), dmas(half, 4),
            dmas(half), dmas(half), dmas(half, 4), dmas(slots, 2), dmas(half, 2), dmas(slots),
            dmas(half), dmas(half), dmas(half),
        ],
        compiler_params=pltpu.CompilerParams(
            collective_id=0, has_side_effects=True, vmem_limit_bytes=60 * 2**20
        ),
        name="pair_exchange",
    )(orbitals, pair_first, pair_second, pair_count, *tables)


def merge_kernel(
    half, block, kept_in, codes_in, scales_in, info,
    out, kept, codes, scales, total, zero, staged, kept_sem, code_sem, scale_sem, out_sem,
):
    slots = 2 * half
    first = [info[0, slot] for slot in range(slots)]
    second = [info[0, slots + slot] for slot in range(slots)]
    count, second_count = info[0, 2 * slots], info[0, 2 * slots + 1]
    pieces, width = 8, zero.shape[1] // 8

    def own_live(slot):
        return slot < count

    def back_live(slot):
        return slot < second_count

    loads = []
    for m in range(slots):
        kept_live, code_live = (own_live(m), back_live(m)) if m < half else (back_live(m), own_live(m))
        loads.append((kept_live, pltpu.make_async_copy(kept_in.at[m], kept.at[m], kept_sem.at[m])))
        loads.append((code_live, pltpu.make_async_copy(codes_in.at[m], codes.at[m], code_sem.at[m])))
        loads.append((code_live, pltpu.make_async_copy(scales_in.at[m], scales.at[m], scale_sem.at[m])))
    for needed, load in loads:
        pl.when(needed)(load.start)
    zero[...] = jnp.zeros_like(zero)

    for row in range(block):
        touched = jnp.bool_(False)
        for slot in range(slots):
            touched |= own_live(slot) & (first[slot] == row)
            touched |= back_live(slot) & (second[slot] == row)

        @pl.when(jnp.logical_not(touched))
        def _():
            pltpu.make_async_copy(zero, out.at[row], out_sem).start()

    for needed, load in loads:
        pl.when(needed)(load.wait)

    def over_pieces(body):
        def piece(index, carry):
            body(pl.ds(pl.multiple_of(width * index, width), width))
            return carry

        lax.fori_loop(0, pieces, piece, 0)

    def term(is_kept, m, lanes):
        if is_kept:
            return kept[m, :, lanes]
        return codes[m, :, lanes].astype(f32) * scales[m, :, 0:1]

    def add_up(place, kind_half, lead, live, rows, extra):
        several = jnp.bool_(False)
        for later in range(lead + 1, slots):
            several |= live(later) & (rows[later] == rows[lead])
        for flag, other in extra:
            several |= flag

        @pl.when(jnp.logical_not(several))
        def _():
            def only(lanes):
                staged[place, :, lanes] = term(kind_half(lead), lead, lanes).astype(bf16)

            over_pieces(only)

        @pl.when(several)
        def _():
            def begin(lanes):
                total[:, lanes] = term(kind_half(lead), lead, lanes)

            over_pieces(begin)
            for later in range(lead + 1, slots):

                @pl.when(live(later) & (rows[later] == rows[lead]))
                def _():
                    def more(lanes):
                        total[:, lanes] += term(kind_half(later), later, lanes)

                    over_pieces(more)

            for flag, other in extra:

                @pl.when(flag)
                def _():
                    def more(lanes):
                        total[:, lanes] += staged[other, :, lanes].astype(f32)

                    over_pieces(more)

            def end(lanes):
                staged[place, :, lanes] = total[:, lanes].astype(bf16)

            over_pieces(end)

    leads = []
    for slot in range(slots):
        lead = back_live(slot)
        for earlier in range(slot):
            lead &= second[earlier] != second[slot]
        leads.append(lead)

        @pl.when(lead)
        def _():
            add_up(slot, lambda s: s >= half, slot, back_live, second, [])
            owned = jnp.bool_(False)
            for other in range(slots):
                owned |= own_live(other) & (first[other] == second[slot])

            @pl.when(jnp.logical_not(owned))
            def _():
                pltpu.make_async_copy(staged.at[slot], out.at[second[slot]], out_sem).start()

    for slot in range(slots):
        lead = own_live(slot)
        for earlier in range(slot):
            lead &= first[earlier] != first[slot]

        @pl.when(lead)
        def _():
            extra = [(leads[other] & (second[other] == first[slot]), other) for other in range(slots)]
            add_up(slots + slot, lambda s: s < half, slot, own_live, first, extra)
            pltpu.make_async_copy(staged.at[slots + slot], out.at[first[slot]], out_sem).start()

    pltpu.make_async_copy(out, out, out_sem).wait()


def merge(kept, codes, scales, info, shape):
    slots, rows, cells = kept.shape
    anywhere, smem = (pl.BlockSpec(memory_space=space) for space in (pl.ANY, pltpu.SMEM))
    dma, dmas = pltpu.SemaphoreType.DMA, pltpu.SemaphoreType.DMA((slots,))
    return pl.pallas_call(
        functools.partial(merge_kernel, slots // 2, shape[0]),
        out_shape=jax.ShapeDtypeStruct(shape, bf16),
        in_specs=[anywhere] * 3 + [smem],
        out_specs=anywhere,
        scratch_shapes=[
            pltpu.VMEM(kept.shape, f32),
            pltpu.VMEM(codes.shape, jnp.int16),
            pltpu.VMEM(scales.shape, f32),
            pltpu.VMEM((rows, cells), f32),
            pltpu.VMEM((rows, cells), bf16),
            pltpu.VMEM((2 * slots, rows, cells), bf16),
            dmas, dmas, dmas, dma,
        ],
        compiler_params=pltpu.CompilerParams(vmem_limit_bytes=60 * 2**20),
        name="merge_rows",
    )(kept, codes, scales, info)


def per_device(orbitals, pair_first, pair_second, pair_count):
    kept, codes, scales, info = exchange(orbitals, pair_first, pair_second, pair_count)
    return merge(kept, codes, scales, info, orbitals.shape)


def solution(mesh):
    return jax.shard_map(
        per_device,
        mesh=mesh,
        in_specs=(P("blk", "grid", None), P("blk", None), P("blk", None), P("blk")),
        out_specs=P("blk", "grid", None),
        check_vma=False,
    )
```

```python
import functools
import math

import jax
import jax.numpy as jnp
import ml_dtypes
import numpy as np
from jax import lax
from jax.experimental import pallas as pl
from jax.experimental.pallas import tpu as pltpu
from jax.sharding import PartitionSpec as P

spacing = 0.5
fraction = 0.25
L = 64
HALF = L // 2
LANES = 128
ROWS = 17
LOADS = 4
CODE = 32767.0
MANTISSA = 16384.0
CELLS = L * L
f32 = jnp.float32
bf16 = jnp.bfloat16


def split_table(table):
    high = table.astype(ml_dtypes.bfloat16)
    low = (table - high.astype(np.float64)).astype(ml_dtypes.bfloat16)
    return high, low


def lane_tables():
    position = np.arange(L)
    angle = 2.0 * np.pi * (np.outer(position, position) % L) / L
    sign = np.array([[1.0, 1.0], [1.0, -1.0]])
    real = np.kron(sign, np.cos(angle))
    imag = np.kron(sign, -np.sin(angle))
    forward = np.block([[real, imag], [-imag, real]])
    inverse = np.block([[real, -imag], [imag, real]])
    (forward, low), (inverse, inverse_low) = split_table(forward), split_table(inverse)
    return np.concatenate([forward, forward, low]), np.concatenate([inverse, inverse, inverse_low])


def row_tables():
    position = np.arange(L)
    angle = 2.0 * np.pi * (np.outer(position, position) % L) / L
    both = np.concatenate([np.cos(angle), np.sin(angle)], 0)
    high, low = split_table(both)
    table = np.concatenate([high, high, low], 1)
    return table, table


def filter_table():
    wrapped = np.arange(L)
    wrapped = np.where(wrapped >= HALF, wrapped - L, wrapped)
    squares = (wrapped * (2.0 * np.pi / (L * spacing))) ** 2
    ky = np.arange(ROWS)[:, None] + HALF * np.arange(2)[None, :]
    total = squares[None, :, None, None] + squares[ky][:, None, :, None] + squares[None, None, None, :]
    kernel = np.where(total > 0, 4.0 * np.pi / np.where(total > 0, total, 1.0), 0.0)
    return (-fraction / L**3 * kernel).reshape(ROWS, L, LANES).astype(np.float32)


def twiddle_table():
    odd = np.repeat(np.arange(2), L)
    angle = 2.0 * np.pi * np.outer(np.arange(ROWS), odd) / L
    return np.stack([np.cos(angle), -np.sin(angle)], 1).astype(np.float32)


def real_forward(values):
    count = len(values)
    if count == 2:
        return [values[0] + values[1], values[0] - values[1]], [None, None]
    even_re, even_im = real_forward(values[0::2])
    odd_re, odd_im = real_forward(values[1::2])
    half, quarter = count // 2, count // 4
    re, im = [None] * (half + 1), [None] * (half + 1)
    re[0], re[half] = even_re[0] + odd_re[0], even_re[0] - odd_re[0]
    re[quarter], im[quarter] = even_re[quarter], -odd_re[quarter]
    for k in range(1, quarter):
        c, s = math.cos(2.0 * math.pi * k / count), math.sin(2.0 * math.pi * k / count)
        if 2 * k == quarter:
            turned_re, turned_im = c * (odd_re[k] + odd_im[k]), c * (odd_im[k] - odd_re[k])
        else:
            turned_re = c * odd_re[k] + s * odd_im[k]
            turned_im = c * odd_im[k] - s * odd_re[k]
        re[k], im[k] = even_re[k] + turned_re, even_im[k] + turned_im
        re[half - k], im[half - k] = even_re[k] - turned_re, turned_im - even_im[k]
    return re, im


def real_inverse(re, im):
    half = len(re) - 1
    count = 2 * half
    if count == 2:
        return [re[0] + re[1], re[0] - re[1]]
    quarter = half // 2
    even_re, even_im = [None] * (quarter + 1), [None] * (quarter + 1)
    odd_re, odd_im = [None] * (quarter + 1), [None] * (quarter + 1)
    even_re[0], odd_re[0] = re[0] + re[half], re[0] - re[half]
    even_re[quarter], odd_re[quarter] = 2.0 * re[quarter], -2.0 * im[quarter]
    for k in range(1, quarter):
        c, s = math.cos(2.0 * math.pi * k / count), math.sin(2.0 * math.pi * k / count)
        even_re[k], even_im[k] = re[k] + re[half - k], im[k] - im[half - k]
        part_re, part_im = re[k] - re[half - k], im[k] + im[half - k]
        if 2 * k == quarter:
            odd_re[k], odd_im[k] = c * (part_re - part_im), c * (part_re + part_im)
        else:
            odd_re[k] = c * part_re - s * part_im
            odd_im[k] = s * part_re + c * part_im
    evens, odds = real_inverse(even_re, even_im), real_inverse(odd_re, odd_im)
    return [value for pair in zip(evens, odds) for value in pair]


def split(values):
    high = values.astype(bf16)
    return high, (values - high.astype(f32)).astype(bf16)


def scale_of(mantissa, exponent):
    return mantissa * jnp.exp2(exponent) * (1.0 / (MANTISSA * CODE))


def dot(left, right):
    return jnp.dot(left, right, preferred_element_type=f32)


def pair_kernel(
    blocks, slots,
    orbitals, first_in, second_in, count_in,
    lane_fwd, lane_inv, row_fwd, row_inv, filters, twiddles,
    kept_out, codes_out, info,
    orb, sending, arriving, sharing, whole, kept, codes,
    spectra, planes, result,
    lane_fwd_v, lane_inv_v, row_fwd_v, row_inv_v, filters_v, twiddles_v, first_s, second_s, count_s,
    next_second, next_count, relay_second, relay_count, final_here, relay_send, relay_recv, load_sem,
    table_sem, index_send, index_recv, orbital_send, orbital_recv,
    share_send, share_recv, code_send, code_recv, kept_sem, kept_send, kept_recv,
):
    half = slots // 2
    me, core = lax.axis_index("blk"), lax.axis_index("grid")
    right, left = lax.rem(me + 1, blocks), lax.rem(me + blocks - 1, blocks)
    to_partner = {"grid": 1 - core}

    final, relay = blocks - 1, max(2, blocks // 4) - 1
    is_first, is_final = me == 0, me == final
    sends_index, is_relay = core == 1, (me == relay) & (core == 1)
    barrier = pltpu.get_barrier_semaphore()
    for place in range(2):
        pl.semaphore_signal(barrier, inc=1, device_id={"blk": left, "grid": place})
    pl.semaphore_signal(barrier, inc=1, device_id=to_partner)

    @pl.when(jnp.logical_not(is_final))
    def _():
        for place in range(2):
            pl.semaphore_signal(barrier, inc=1, device_id={"blk": right, "grid": place})

    @pl.when(is_relay)
    def _():
        for device in ({"blk": 0, "grid": 1}, {"blk": final, "grid": 0}, {"blk": final, "grid": 1}):
            pl.semaphore_signal(barrier, inc=1, device_id=device)

    size = orb.shape[0] // LOADS
    loads = [
        pltpu.make_async_copy(orbitals.at[pl.ds(size * n, size)], orb.at[pl.ds(size * n, size)], load_sem.at[n])
        for n in range(LOADS)
    ]
    for load in loads:
        load.start()
    tables = [
        pltpu.make_async_copy(source, target, table_sem.at[place])
        for place, (source, target) in enumerate([
            (first_in, first_s), (second_in, second_s), (count_in, count_s),
            (lane_fwd, lane_fwd_v), (lane_inv, lane_inv_v), (row_fwd, row_fwd_v), (row_inv, row_inv_v),
            (filters, filters_v), (twiddles, twiddles_v),
        ])
    ]
    for table in tables:
        table.start()

    def remote(source, target, send, recv, device):
        return pltpu.make_async_remote_copy(
            src_ref=source, dst_ref=target, send_sem=send, recv_sem=recv, device_id=device
        )

    def index_copies(targets, sent, arrived, device, sources=(second_in, count_in)):
        return [
            remote(source, target, sent.at[part], arrived.at[part], device)
            for part, (source, target) in enumerate(zip(sources, targets))
        ]

    def to_both(block, sent, sources=(second_in, count_in)):
        targets = (next_second, next_count)
        return [
            copy
            for place in range(2)
            for copy in index_copies(targets, sent.at[place], index_recv, {"blk": block, "grid": place}, sources)
        ]

    to_next = to_both(left, index_send)
    to_relay = index_copies((relay_second, relay_count), index_send.at[0], relay_recv, {"blk": relay, "grid": 1})

    def orbital_copy(m, group):
        visits = m < half
        device = {"blk": right if visits else left, "grid": 0 if visits else 1}
        place = 2 * core + group
        return remote(
            sending.at[m, pl.ds(16 * group, 16)],
            arriving.at[m % half, pl.ds(pl.multiple_of(16 * place, 16), 16)],
            orbital_send.at[m, group], orbital_recv.at[m % half, place], device,
        )

    def arrival(stage, place):
        rows = pl.ds(pl.multiple_of(16 * place, 16), 16)
        return remote(
            sending.at[0, pl.ds(0, 16)], arriving.at[stage, rows],
            orbital_send.at[0, 0], orbital_recv.at[stage, place], to_partner,
        )

    def worked_on(stage, by):
        return jnp.where(by == 0, first_s[0, stage], next_second[0, half + stage])

    def share_copy(stage):
        rows = pl.ds(pl.multiple_of(HALF * core, HALF), HALF)
        return remote(sharing.at[stage], whole.at[stage, rows], share_send.at[stage], share_recv.at[stage], to_partner)

    def send_first(m):
        for group in range(2):
            orbital_copy(m, group).start()

    def load_own():
        for table in tables[:3]:
            table.wait()
        for load in loads:
            load.wait()
        for m in range(half, slots):
            sending[m] = orb[first_s[0, m]]

    def load_visits():
        for copy in to_next[:2]:
            copy.wait_recv()
        for m in range(half):
            sending[m] = orb[next_second[0, m]]

    normal = 5 + is_final.astype(jnp.int32)
    pl.semaphore_wait(barrier, jnp.where(is_first, 3 + core, normal))

    @pl.when(is_final)
    def _():
        for place in range(2):
            pl.semaphore_signal(final_here, inc=1, device_id={"blk": right, "grid": place})
        pl.semaphore_signal(final_here, inc=1, device_id={"blk": relay, "grid": 1})

    @pl.when(is_first)
    def _():
        @pl.when(sends_index)
        def _():
            for copy in to_relay:
                copy.start()

        load_own()
        load_visits()
        send_first(0)
        pl.semaphore_wait(final_here, 2)
        send_first(half)

        @pl.when(sends_index)
        def _():
            for copy in to_relay:
                copy.wait_send()

    @pl.when(jnp.logical_not(is_first))
    def _():
        @pl.when(sends_index)
        def _():
            for copy in to_next:
                copy.start()

        load_own()
        send_first(half)

        @pl.when(is_relay)
        def _():
            for copy in to_relay:
                copy.wait_recv()
            pl.semaphore_wait(final_here, 2)
            onward = to_both(final, relay_send, (relay_second, relay_count))
            for copy in onward:
                copy.start()
            for copy in onward:
                copy.wait_send()

        load_visits()
        send_first(0)

        @pl.when(sends_index)
        def _():
            for copy in to_next:
                copy.wait_send()

    for stage in range(half):
        sharing[stage] = orb[worked_on(stage, 1 - core)]
        share_copy(stage).start()
        whole[stage, pl.ds(pl.multiple_of(HALF * core, HALF), HALF)] = orb[worked_on(stage, core)]
    for stage in range(1, half):
        for group in range(2):
            for m in (half + stage, stage):
                orbital_copy(m - 1, group).wait_send()
                orbital_copy(m, group).start()
    for table in tables[3:]:
        table.wait()
    for m in range(slots):
        info[0, m] = first_s[0, m]
        info[0, slots + m] = next_second[0, m]
    info[0, 2 * slots] = count_s[0]
    info[0, 2 * slots + 1] = next_count[0]

    def solved(stage):
        return stage + half * core

    def kept_local(stage):
        rows = pl.ds(pl.multiple_of(HALF * core, HALF), HALF)
        return pltpu.make_async_copy(kept.at[stage, rows], kept_out.at[solved(stage)], kept_sem.at[stage])

    def kept_remote(stage, m):
        rows = pl.ds(pl.multiple_of(HALF * (1 - core), HALF), HALF)
        return remote(kept.at[stage, rows], kept_out.at[m], kept_send.at[stage], kept_recv.at[stage], to_partner)

    def code_copy(stage, place, m):
        device = {"blk": jnp.where(core == 0, left, right), "grid": lax.div(place, 2)}
        rows = pl.ds(pl.multiple_of(16 * place, 16), 16)
        there = pl.ds(pl.multiple_of(16 * lax.rem(place, 2), 16), 16)
        return remote(
            codes.at[stage, rows], codes_out.at[m, there],
            code_send.at[stage, place], code_recv.at[m, lax.rem(place, 2)], device,
        )

    def one_stage(stage, carry):
        m = solved(stage)
        share_copy(stage).wait_recv()

        def forward_group(turn, carry):
            place = 2 * lax.rem(turn, 2) + lax.div(turn, 2)
            rows = pl.ds(pl.multiple_of(16 * place, 16), 16)
            arrival(stage, place).wait_recv()
            values = []
            for column in range(HALF):
                lanes = pl.ds(LANES * column, LANES)
                values.append(whole[stage, rows, lanes].astype(f32) * arriving[stage, rows, lanes].astype(f32))
            re, im = real_forward(values)
            for k in range(ROWS):
                if k == 0:
                    turned_re, turned_im = re[0], jnp.zeros_like(re[0])
                else:
                    c, s = twiddles_v[k, 0:1], twiddles_v[k, 1:2]
                    if im[k] is None:
                        turned_re, turned_im = re[k] * c, re[k] * s
                    else:
                        turned_re, turned_im = re[k] * c - im[k] * s, re[k] * s + im[k] * c
                for part, value in enumerate((turned_re, turned_im)):
                    high, low = split(value)
                    for place, piece in enumerate((high, low, high)):
                        start = LANES * (2 * place + part)
                        spectra[k, :, start : start + LANES] = piece
            out = dot(spectra[...].reshape(ROWS * 16, 6 * LANES), lane_fwd_v[...])
            planes[:, rows, :] = out.reshape(ROWS, 16, 2 * LANES)
            return carry

        lax.fori_loop(0, 4, forward_group, 0)

        for k in range(ROWS):
            high, low = split(planes[k])
            out = dot(row_fwd_v[...], jnp.concatenate([high, low, high], 0))
            kernel = filters_v[k]
            re = (out[:L, :LANES] + out[L:, LANES:]) * kernel
            im = (out[:L, LANES:] - out[L:, :LANES]) * kernel
            high, low = split(jnp.concatenate([re, im], 1))
            out = dot(row_inv_v[...], jnp.concatenate([high, low, high], 0))
            re = out[:L, :LANES] - out[L:, LANES:]
            im = out[:L, LANES:] + out[L:, :LANES]
            planes[k] = jnp.concatenate([re, im], 1)

        live = jnp.where(m < jnp.where(core == 0, count_s[0], next_count[0]), 1.0, 0.0).astype(f32)

        def inverse_group(place, carry):
            rows = pl.ds(pl.multiple_of(16 * place, 16), 16)
            high, low = split(planes[:, rows, :].reshape(ROWS * 16, 2 * LANES))
            out = dot(jnp.concatenate([high, low, high], 1), lane_inv_v[...])
            result[...] = out.reshape(ROWS, 16, 2 * LANES)
            re, im = [], []
            for k in range(ROWS):
                value_re = result[k, :, :LANES]
                if k == 0:
                    re.append(value_re)
                    im.append(None)
                    continue
                value_im = result[k, :, LANES:]
                c, s = twiddles_v[k, 0:1], twiddles_v[k, 1:2]
                re.append(value_re * c + value_im * s)
                im.append(None if k == ROWS - 1 else value_im * c - value_re * s)
            potential = real_inverse(re, im)
            terms, largest = [], None
            for column in range(HALF):
                lanes = pl.ds(LANES * column, LANES)
                value = potential[column] * live
                kept[stage, rows, lanes] = value * arriving[stage, rows, lanes].astype(f32)
                terms.append(value * whole[stage, rows, lanes].astype(f32))
                size = jnp.abs(terms[-1])
                largest = size if largest is None else jnp.maximum(largest, size)
            bound = jnp.broadcast_to(jnp.maximum(jnp.max(largest, axis=1, keepdims=True), 1e-30), (16, LANES))
            exponent = jnp.ceil(jnp.log2(bound))
            mantissa = jnp.ceil(bound * jnp.exp2(-exponent) * MANTISSA)
            side = lax.broadcasted_iota(jnp.int32, (16, LANES), 1) < LANES // 2
            codes[stage, rows, CELLS:] = jnp.where(side, mantissa, exponent).astype(jnp.int32).astype(jnp.int16)
            inverse_scale = 1.0 / scale_of(mantissa, exponent)
            for column in range(HALF):
                lanes = pl.ds(LANES * column, LANES)
                code = jnp.round(terms[column] * inverse_scale)
                codes[stage, rows, lanes] = code.astype(jnp.int32).astype(jnp.int16)
            code_copy(stage, place, m).start()
            return carry

        lax.fori_loop(0, 4, inverse_group, 0)
        kept_local(stage).start()
        kept_remote(stage, m).start()
        return carry

    lax.fori_loop(0, half, one_stage, 0)
    for stage in range(half):
        share_copy(stage).wait_send()
        kept_local(stage).wait()
        kept_remote(stage, stage + half * (1 - core)).wait()
        for place in range(4):
            code_copy(stage, place, solved(stage)).wait_send()
    for m in range(slots):
        for group in range(2):
            if m % half == half - 1:
                orbital_copy(m, group).wait_send()
            code_copy(0, group, m).wait_recv()


def exchange(orbitals, pair_first, pair_second, pair_count):
    blocks = lax.axis_size("blk")
    slots = pair_first.shape[1]
    block, rows, cells = orbitals.shape
    lane_fwd, lane_inv = lane_tables()
    row_fwd, row_inv = row_tables()
    tables = [jnp.asarray(t) for t in (lane_fwd, lane_inv, row_fwd, row_inv, filter_table(), twiddle_table())]
    anywhere, smem = (pl.BlockSpec(memory_space=space) for space in (pl.ANY, pltpu.SMEM))
    dma, dmas = pltpu.SemaphoreType.DMA, lambda *shape: pltpu.SemaphoreType.DMA(shape)
    half = slots // 2
    return pl.pallas_call(
        functools.partial(pair_kernel, blocks, slots),
        out_shape=[
            jax.ShapeDtypeStruct((slots, rows, cells), f32),
            jax.ShapeDtypeStruct((slots, rows, cells + LANES), jnp.int16),
            jax.ShapeDtypeStruct((1, 2 * slots + 2), jnp.int32),
        ],
        in_specs=[anywhere] * (4 + len(tables)),
        out_specs=[anywhere, anywhere, smem],
        scratch_shapes=[
            pltpu.VMEM((block, rows, cells), bf16),
            pltpu.VMEM((slots, rows, cells), bf16),
            pltpu.VMEM((half, L, cells), bf16),
            pltpu.VMEM((half, rows, cells), bf16),
            pltpu.VMEM((half, L, cells), bf16),
            pltpu.VMEM((half, L, cells), f32),
            pltpu.VMEM((half, L, cells + LANES), jnp.int16),
            pltpu.VMEM((ROWS, 16, 6 * LANES), bf16),
            pltpu.VMEM((ROWS, L, 2 * LANES), f32),
            pltpu.VMEM((ROWS, 16, 2 * LANES), f32),
            pltpu.VMEM(lane_fwd.shape, bf16),
            pltpu.VMEM(lane_inv.shape, bf16),
            pltpu.VMEM(row_fwd.shape, bf16),
            pltpu.VMEM(row_inv.shape, bf16),
            pltpu.VMEM((ROWS, L, LANES), f32),
            pltpu.VMEM((ROWS, 2, LANES), f32),
            pltpu.SMEM(pair_first.shape, jnp.int32),
            pltpu.SMEM(pair_second.shape, jnp.int32),
            pltpu.SMEM(pair_count.shape, jnp.int32),
            pltpu.SMEM(pair_second.shape, jnp.int32),
            pltpu.SMEM(pair_count.shape, jnp.int32),
            pltpu.SMEM(pair_second.shape, jnp.int32),
            pltpu.SMEM(pair_count.shape, jnp.int32),
            pltpu.SemaphoreType.REGULAR, dmas(2, 2), dmas(2), dmas(LOADS),
            dmas(9), dmas(2, 2), dmas(2), dmas(slots, 2), dmas(half, 4),
            dmas(half), dmas(half), dmas(half, 4), dmas(slots, 2),
            dmas(half), dmas(half), dmas(half),
        ],
        compiler_params=pltpu.CompilerParams(
            collective_id=0, has_side_effects=True, vmem_limit_bytes=60 * 2**20
        ),
        name="pair_exchange",
    )(orbitals, pair_first, pair_second, pair_count, *tables)


def merge_kernel(
    half, block, kept_in, codes_in, info,
    out, kept, codes, scales, total, zero, staged, kept_sem, code_sem, out_sem,
):
    slots = 2 * half
    first = [info[0, slot] for slot in range(slots)]
    second = [info[0, slots + slot] for slot in range(slots)]
    count, second_count = info[0, 2 * slots], info[0, 2 * slots + 1]
    pieces, width = 4, zero.shape[1] // 4

    def own_live(slot):
        return slot < count

    def back_live(slot):
        return slot < second_count

    loads = []
    for m in range(slots):
        kept_live, code_live = (own_live(m), back_live(m)) if m < half else (back_live(m), own_live(m))
        loads.append((kept_live, pltpu.make_async_copy(kept_in.at[m], kept.at[m], kept_sem.at[m])))
        loads.append((code_live, pltpu.make_async_copy(codes_in.at[m], codes.at[m], code_sem.at[m])))
    for needed, load in loads:
        pl.when(needed)(load.start)
    zero[...] = jnp.zeros_like(zero)

    for row in range(block):
        touched = jnp.bool_(False)
        for slot in range(slots):
            touched |= own_live(slot) & (first[slot] == row)
            touched |= back_live(slot) & (second[slot] == row)

        @pl.when(jnp.logical_not(touched))
        def _():
            pltpu.make_async_copy(zero, out.at[row], out_sem).start()

    for needed, load in loads:
        pl.when(needed)(load.wait)
    for m in range(slots):
        @pl.when(back_live(m) if m < half else own_live(m))
        def _():
            side = codes[m, :, CELLS:].astype(f32)
            scale = scale_of(side[:, :1], side[:, LANES // 2 : LANES // 2 + 1])
            scales[m] = jnp.broadcast_to(scale, scales.shape[1:])

    def over_pieces(body):
        def piece(index, carry):
            body(pl.ds(pl.multiple_of(width * index, width), width))
            return carry

        lax.fori_loop(0, pieces, piece, 0)

    def term(is_kept, m, lanes):
        if is_kept:
            return kept[m, :, lanes]
        return codes[m, :, lanes].astype(f32) * scales[m, :, 0:1]

    def add_up(place, kind_half, lead, live, rows, extra):
        several = jnp.bool_(False)
        for later in range(lead + 1, slots):
            several |= live(later) & (rows[later] == rows[lead])
        for flag, other in extra:
            several |= flag

        @pl.when(jnp.logical_not(several))
        def _():
            def only(lanes):
                staged[place, :, lanes] = term(kind_half(lead), lead, lanes).astype(bf16)

            over_pieces(only)

        @pl.when(several)
        def _():
            def begin(lanes):
                total[:, lanes] = term(kind_half(lead), lead, lanes)

            over_pieces(begin)
            for later in range(lead + 1, slots):

                @pl.when(live(later) & (rows[later] == rows[lead]))
                def _():
                    def more(lanes):
                        total[:, lanes] += term(kind_half(later), later, lanes)

                    over_pieces(more)

            for flag, other in extra:

                @pl.when(flag)
                def _():
                    def more(lanes):
                        total[:, lanes] += staged[other, :, lanes].astype(f32)

                    over_pieces(more)

            def end(lanes):
                staged[place, :, lanes] = total[:, lanes].astype(bf16)

            over_pieces(end)

    leads = []
    for slot in range(slots):
        lead = back_live(slot)
        for earlier in range(slot):
            lead &= second[earlier] != second[slot]
        leads.append(lead)

        @pl.when(lead)
        def _():
            add_up(slot, lambda s: s >= half, slot, back_live, second, [])
            owned = jnp.bool_(False)
            for other in range(slots):
                owned |= own_live(other) & (first[other] == second[slot])

            @pl.when(jnp.logical_not(owned))
            def _():
                pltpu.make_async_copy(staged.at[slot], out.at[second[slot]], out_sem).start()

    for slot in range(slots):
        lead = own_live(slot)
        for earlier in range(slot):
            lead &= first[earlier] != first[slot]

        @pl.when(lead)
        def _():
            extra = [(leads[other] & (second[other] == first[slot]), other) for other in range(slots)]
            add_up(slots + slot, lambda s: s < half, slot, own_live, first, extra)
            pltpu.make_async_copy(staged.at[slots + slot], out.at[first[slot]], out_sem).start()

    pltpu.make_async_copy(out, out, out_sem).wait()


def merge(kept, codes, info, shape):
    slots, rows, cells = kept.shape
    anywhere, smem = (pl.BlockSpec(memory_space=space) for space in (pl.ANY, pltpu.SMEM))
    dma, dmas = pltpu.SemaphoreType.DMA, pltpu.SemaphoreType.DMA((slots,))
    return pl.pallas_call(
        functools.partial(merge_kernel, slots // 2, shape[0]),
        out_shape=jax.ShapeDtypeStruct(shape, bf16),
        in_specs=[anywhere] * 2 + [smem],
        out_specs=anywhere,
        scratch_shapes=[
            pltpu.VMEM(kept.shape, f32),
            pltpu.VMEM(codes.shape, jnp.int16),
            pltpu.VMEM((slots, rows, LANES), f32),
            pltpu.VMEM((rows, cells), f32),
            pltpu.VMEM((rows, cells), bf16),
            pltpu.VMEM((2 * slots, rows, cells), bf16),
            dmas, dmas, dma,
        ],
        compiler_params=pltpu.CompilerParams(vmem_limit_bytes=60 * 2**20),
        name="merge_rows",
    )(kept, codes, info)


def per_device(orbitals, pair_first, pair_second, pair_count):
    kept, codes, info = exchange(orbitals, pair_first, pair_second, pair_count)
    return merge(kept, codes, info, orbitals.shape)


def solution(mesh):
    return jax.shard_map(
        per_device,
        mesh=mesh,
        in_specs=(P("blk", "grid", None), P("blk", None), P("blk", None), P("blk")),
        out_specs=P("blk", "grid", None),
        check_vma=False,
    )
```

```python
import functools
import math

import jax
import jax.numpy as jnp
import ml_dtypes
import numpy as np
from jax import lax
from jax.experimental import pallas as pl
from jax.experimental.pallas import tpu as pltpu
from jax.sharding import PartitionSpec as P

spacing = 0.5
fraction = 0.25
L = 64
HALF = L // 2
LANES = 128
ROWS = 17
LOADS = 4
CODE = 32767.0
MANTISSA = 16384.0
CELLS = L * L
f32 = jnp.float32
bf16 = jnp.bfloat16


def split_table(table):
    high = table.astype(ml_dtypes.bfloat16)
    low = (table - high.astype(np.float64)).astype(ml_dtypes.bfloat16)
    return high, low


def lane_tables():
    position = np.arange(L)
    angle = 2.0 * np.pi * (np.outer(position, position) % L) / L
    sign = np.array([[1.0, 1.0], [1.0, -1.0]])
    real = np.kron(sign, np.cos(angle))
    imag = np.kron(sign, -np.sin(angle))
    forward = np.block([[real, imag], [-imag, real]])
    inverse = np.block([[real, -imag], [imag, real]])
    (forward, low), (inverse, inverse_low) = split_table(forward), split_table(inverse)
    return np.concatenate([forward, forward, low]), np.concatenate([inverse, inverse, inverse_low])


def row_tables():
    position = np.arange(L)
    angle = 2.0 * np.pi * (np.outer(position, position) % L) / L
    both = np.concatenate([np.cos(angle), np.sin(angle)], 0)
    high, low = split_table(both)
    table = np.concatenate([high, high, low], 1)
    return table, table


def filter_table():
    wrapped = np.arange(L)
    wrapped = np.where(wrapped >= HALF, wrapped - L, wrapped)
    squares = (wrapped * (2.0 * np.pi / (L * spacing))) ** 2
    ky = np.arange(ROWS)[:, None] + HALF * np.arange(2)[None, :]
    total = squares[None, :, None, None] + squares[ky][:, None, :, None] + squares[None, None, None, :]
    kernel = np.where(total > 0, 4.0 * np.pi / np.where(total > 0, total, 1.0), 0.0)
    return (-fraction / L**3 * kernel).reshape(ROWS, L, LANES).astype(np.float32)


def twiddle_table():
    odd = np.repeat(np.arange(2), L)
    angle = 2.0 * np.pi * np.outer(np.arange(ROWS), odd) / L
    return np.stack([np.cos(angle), -np.sin(angle)], 1).astype(np.float32)


def real_forward(values):
    count = len(values)
    if count == 2:
        return [values[0] + values[1], values[0] - values[1]], [None, None]
    even_re, even_im = real_forward(values[0::2])
    odd_re, odd_im = real_forward(values[1::2])
    half, quarter = count // 2, count // 4
    re, im = [None] * (half + 1), [None] * (half + 1)
    re[0], re[half] = even_re[0] + odd_re[0], even_re[0] - odd_re[0]
    re[quarter], im[quarter] = even_re[quarter], -odd_re[quarter]
    for k in range(1, quarter):
        c, s = math.cos(2.0 * math.pi * k / count), math.sin(2.0 * math.pi * k / count)
        if 2 * k == quarter:
            turned_re, turned_im = c * (odd_re[k] + odd_im[k]), c * (odd_im[k] - odd_re[k])
        else:
            turned_re = c * odd_re[k] + s * odd_im[k]
            turned_im = c * odd_im[k] - s * odd_re[k]
        re[k], im[k] = even_re[k] + turned_re, even_im[k] + turned_im
        re[half - k], im[half - k] = even_re[k] - turned_re, turned_im - even_im[k]
    return re, im


def real_inverse(re, im):
    half = len(re) - 1
    count = 2 * half
    if count == 2:
        return [re[0] + re[1], re[0] - re[1]]
    quarter = half // 2
    even_re, even_im = [None] * (quarter + 1), [None] * (quarter + 1)
    odd_re, odd_im = [None] * (quarter + 1), [None] * (quarter + 1)
    even_re[0], odd_re[0] = re[0] + re[half], re[0] - re[half]
    even_re[quarter], odd_re[quarter] = 2.0 * re[quarter], -2.0 * im[quarter]
    for k in range(1, quarter):
        c, s = math.cos(2.0 * math.pi * k / count), math.sin(2.0 * math.pi * k / count)
        even_re[k], even_im[k] = re[k] + re[half - k], im[k] - im[half - k]
        part_re, part_im = re[k] - re[half - k], im[k] + im[half - k]
        if 2 * k == quarter:
            odd_re[k], odd_im[k] = c * (part_re - part_im), c * (part_re + part_im)
        else:
            odd_re[k] = c * part_re - s * part_im
            odd_im[k] = s * part_re + c * part_im
    evens, odds = real_inverse(even_re, even_im), real_inverse(odd_re, odd_im)
    return [value for pair in zip(evens, odds) for value in pair]


def split(values):
    high = values.astype(bf16)
    return high, (values - high.astype(f32)).astype(bf16)


def scale_of(mantissa, exponent):
    return mantissa * jnp.exp2(exponent) * (1.0 / (MANTISSA * CODE))


def dot(left, right):
    return jnp.dot(left, right, preferred_element_type=f32)


def pair_kernel(
    blocks, slots,
    orbitals, first_in, second_in, count_in,
    lane_fwd, lane_inv, row_fwd, row_inv, filters, twiddles,
    kept_out, codes_out, info,
    orb, sending, arriving, sharing, whole, kept, codes,
    spectra, planes, result,
    lane_fwd_v, lane_inv_v, row_fwd_v, row_inv_v, filters_v, twiddles_v, first_s, second_s, count_s,
    next_second, next_count, relay_second, relay_count, final_here, left_here, relay_send, relay_recv, load_sem,
    table_sem, index_send, index_recv, orbital_send, orbital_recv,
    share_send, share_recv, code_send, code_recv, kept_sem, kept_send, kept_recv,
):
    half = slots // 2
    me, core = lax.axis_index("blk"), lax.axis_index("grid")
    right, left = lax.rem(me + 1, blocks), lax.rem(me + blocks - 1, blocks)
    to_partner = {"grid": 1 - core}

    final, relay = blocks - 1, max(2, blocks // 4) - 1
    is_first, is_final, before_final = me == 0, me == final, me == final - 1
    sends_index, is_relay = core == 1, (me == relay) & (core == 1)
    barrier = pltpu.get_barrier_semaphore()
    for place in range(2):
        pl.semaphore_signal(barrier, inc=1, device_id={"blk": left, "grid": place})
    pl.semaphore_signal(barrier, inc=1, device_id=to_partner)

    @pl.when(jnp.logical_not(is_final | before_final))
    def _():
        for place in range(2):
            pl.semaphore_signal(barrier, inc=1, device_id={"blk": right, "grid": place})

    @pl.when(is_relay)
    def _():
        for device in ({"blk": 0, "grid": 1}, {"blk": final, "grid": 0}, {"blk": final, "grid": 1}):
            pl.semaphore_signal(barrier, inc=1, device_id=device)

    size = orb.shape[0] // LOADS
    loads = [
        pltpu.make_async_copy(orbitals.at[pl.ds(size * n, size)], orb.at[pl.ds(size * n, size)], load_sem.at[n])
        for n in range(LOADS)
    ]
    for load in loads:
        load.start()
    tables = [
        pltpu.make_async_copy(source, target, table_sem.at[place])
        for place, (source, target) in enumerate([
            (first_in, first_s), (second_in, second_s), (count_in, count_s),
            (lane_fwd, lane_fwd_v), (lane_inv, lane_inv_v), (row_fwd, row_fwd_v), (row_inv, row_inv_v),
            (filters, filters_v), (twiddles, twiddles_v),
        ])
    ]
    for table in tables:
        table.start()

    def remote(source, target, send, recv, device):
        return pltpu.make_async_remote_copy(
            src_ref=source, dst_ref=target, send_sem=send, recv_sem=recv, device_id=device
        )

    def index_copies(targets, sent, arrived, device, sources=(second_in, count_in)):
        return [
            remote(source, target, sent.at[part], arrived.at[part], device)
            for part, (source, target) in enumerate(zip(sources, targets))
        ]

    def to_both(block, sent, sources=(second_in, count_in)):
        targets = (next_second, next_count)
        return [
            copy
            for place in range(2)
            for copy in index_copies(targets, sent.at[place], index_recv, {"blk": block, "grid": place}, sources)
        ]

    to_next = to_both(left, index_send)
    to_relay = index_copies((relay_second, relay_count), index_send.at[0], relay_recv, {"blk": relay, "grid": 1})

    def orbital_copy(m, group):
        visits = m < half
        device = {"blk": right if visits else left, "grid": 0 if visits else 1}
        place = 2 * core + group
        return remote(
            sending.at[m, pl.ds(16 * group, 16)],
            arriving.at[m % half, pl.ds(pl.multiple_of(16 * place, 16), 16)],
            orbital_send.at[m, group], orbital_recv.at[m % half, place], device,
        )

    def arrival(stage, place):
        rows = pl.ds(pl.multiple_of(16 * place, 16), 16)
        return remote(
            sending.at[0, pl.ds(0, 16)], arriving.at[stage, rows],
            orbital_send.at[0, 0], orbital_recv.at[stage, place], to_partner,
        )

    def worked_on(stage, by):
        return jnp.where(by == 0, first_s[0, stage], next_second[0, half + stage])

    def share_copy(stage):
        rows = pl.ds(pl.multiple_of(HALF * core, HALF), HALF)
        return remote(sharing.at[stage], whole.at[stage, rows], share_send.at[stage], share_recv.at[stage], to_partner)

    def send_first(m):
        for group in range(2):
            orbital_copy(m, group).start()

    def load_own():
        for table in tables[:3]:
            table.wait()
        for load in loads:
            load.wait()
        for m in range(half, slots):
            sending[m] = orb[first_s[0, m]]

    def load_visits():
        for copy in to_next[:2]:
            copy.wait_recv()
        for m in range(half):
            sending[m] = orb[next_second[0, m]]

    normal = 5 - is_final.astype(jnp.int32)
    pl.semaphore_wait(barrier, jnp.where(is_first, 3 + core, normal))

    @pl.when(before_final)
    def _():
        for place in range(2):
            pl.semaphore_signal(left_here, inc=1, device_id={"blk": right, "grid": place})

    @pl.when(is_final)
    def _():
        for place in range(2):
            pl.semaphore_signal(final_here, inc=1, device_id={"blk": right, "grid": place})
        pl.semaphore_signal(final_here, inc=1, device_id={"blk": relay, "grid": 1})
        pl.semaphore_wait(left_here, 2)

    @pl.when(is_first)
    def _():
        @pl.when(sends_index)
        def _():
            for copy in to_relay:
                copy.start()

        load_own()
        load_visits()
        send_first(0)
        pl.semaphore_wait(final_here, 2)
        send_first(half)

        @pl.when(sends_index)
        def _():
            for copy in to_relay:
                copy.wait_send()

    @pl.when(jnp.logical_not(is_first))
    def _():
        @pl.when(sends_index)
        def _():
            for copy in to_next:
                copy.start()

        load_own()
        send_first(half)

        @pl.when(is_relay)
        def _():
            for copy in to_relay:
                copy.wait_recv()
            pl.semaphore_wait(final_here, 2)
            onward = to_both(final, relay_send, (relay_second, relay_count))
            for copy in onward:
                copy.start()
            for copy in onward:
                copy.wait_send()

        load_visits()
        send_first(0)

        @pl.when(sends_index)
        def _():
            for copy in to_next:
                copy.wait_send()

    for stage in range(half):
        sharing[stage] = orb[worked_on(stage, 1 - core)]
        share_copy(stage).start()
        whole[stage, pl.ds(pl.multiple_of(HALF * core, HALF), HALF)] = orb[worked_on(stage, core)]
    for stage in range(1, half):
        for group in range(2):
            for m in (half + stage, stage):
                orbital_copy(m - 1, group).wait_send()
                orbital_copy(m, group).start()
    for table in tables[3:]:
        table.wait()
    for m in range(slots):
        info[0, m] = first_s[0, m]
        info[0, slots + m] = next_second[0, m]
    info[0, 2 * slots] = count_s[0]
    info[0, 2 * slots + 1] = next_count[0]

    def solved(stage):
        return stage + half * core

    def kept_local(stage):
        rows = pl.ds(pl.multiple_of(HALF * core, HALF), HALF)
        return pltpu.make_async_copy(kept.at[stage, rows], kept_out.at[solved(stage)], kept_sem.at[stage])

    def kept_remote(stage, m):
        rows = pl.ds(pl.multiple_of(HALF * (1 - core), HALF), HALF)
        return remote(kept.at[stage, rows], kept_out.at[m], kept_send.at[stage], kept_recv.at[stage], to_partner)

    def code_copy(stage, place, m):
        device = {"blk": jnp.where(core == 0, left, right), "grid": lax.div(place, 2)}
        rows = pl.ds(pl.multiple_of(16 * place, 16), 16)
        there = pl.ds(pl.multiple_of(16 * lax.rem(place, 2), 16), 16)
        return remote(
            codes.at[stage, rows], codes_out.at[m, there],
            code_send.at[stage, place], code_recv.at[m, lax.rem(place, 2)], device,
        )

    def one_stage(stage, carry):
        m = solved(stage)
        share_copy(stage).wait_recv()

        def forward_group(turn, carry):
            place = 2 * lax.rem(turn, 2) + lax.div(turn, 2)
            rows = pl.ds(pl.multiple_of(16 * place, 16), 16)
            arrival(stage, place).wait_recv()
            values = []
            for column in range(HALF):
                lanes = pl.ds(LANES * column, LANES)
                values.append(whole[stage, rows, lanes].astype(f32) * arriving[stage, rows, lanes].astype(f32))
            re, im = real_forward(values)
            for k in range(ROWS):
                if k == 0:
                    turned_re, turned_im = re[0], jnp.zeros_like(re[0])
                else:
                    c, s = twiddles_v[k, 0:1], twiddles_v[k, 1:2]
                    if im[k] is None:
                        turned_re, turned_im = re[k] * c, re[k] * s
                    else:
                        turned_re, turned_im = re[k] * c - im[k] * s, re[k] * s + im[k] * c
                for part, value in enumerate((turned_re, turned_im)):
                    high, low = split(value)
                    for place, piece in enumerate((high, low, high)):
                        start = LANES * (2 * place + part)
                        spectra[k, :, start : start + LANES] = piece
            out = dot(spectra[...].reshape(ROWS * 16, 6 * LANES), lane_fwd_v[...])
            planes[:, rows, :] = out.reshape(ROWS, 16, 2 * LANES)
            return carry

        lax.fori_loop(0, 4, forward_group, 0)

        for k in range(ROWS):
            high, low = split(planes[k])
            out = dot(row_fwd_v[...], jnp.concatenate([high, low, high], 0))
            kernel = filters_v[k]
            re = (out[:L, :LANES] + out[L:, LANES:]) * kernel
            im = (out[:L, LANES:] - out[L:, :LANES]) * kernel
            high, low = split(jnp.concatenate([re, im], 1))
            out = dot(row_inv_v[...], jnp.concatenate([high, low, high], 0))
            re = out[:L, :LANES] - out[L:, LANES:]
            im = out[:L, LANES:] + out[L:, :LANES]
            planes[k] = jnp.concatenate([re, im], 1)

        live = jnp.where(m < jnp.where(core == 0, count_s[0], next_count[0]), 1.0, 0.0).astype(f32)

        def inverse_group(turn, carry):
            place = 2 * (1 - lax.rem(turn, 2)) + lax.div(turn, 2)
            rows = pl.ds(pl.multiple_of(16 * place, 16), 16)
            high, low = split(planes[:, rows, :].reshape(ROWS * 16, 2 * LANES))
            out = dot(jnp.concatenate([high, low, high], 1), lane_inv_v[...])
            result[...] = out.reshape(ROWS, 16, 2 * LANES)
            re, im = [], []
            for k in range(ROWS):
                value_re = result[k, :, :LANES]
                if k == 0:
                    re.append(value_re)
                    im.append(None)
                    continue
                value_im = result[k, :, LANES:]
                c, s = twiddles_v[k, 0:1], twiddles_v[k, 1:2]
                re.append(value_re * c + value_im * s)
                im.append(None if k == ROWS - 1 else value_im * c - value_re * s)
            potential = real_inverse(re, im)
            terms, largest = [], None
            for column in range(HALF):
                lanes = pl.ds(LANES * column, LANES)
                value = potential[column] * live
                kept[stage, rows, lanes] = value * arriving[stage, rows, lanes].astype(f32)
                terms.append(value * whole[stage, rows, lanes].astype(f32))
                size = jnp.abs(terms[-1])
                largest = size if largest is None else jnp.maximum(largest, size)
            bound = jnp.broadcast_to(jnp.maximum(jnp.max(largest, axis=1, keepdims=True), 1e-30), (16, LANES))
            exponent = jnp.ceil(jnp.log2(bound))
            mantissa = jnp.ceil(bound * jnp.exp2(-exponent) * MANTISSA)
            side = lax.broadcasted_iota(jnp.int32, (16, LANES), 1) < LANES // 2
            codes[stage, rows, CELLS:] = jnp.where(side, mantissa, exponent).astype(jnp.int32).astype(jnp.int16)
            inverse_scale = 1.0 / scale_of(mantissa, exponent)
            for column in range(HALF):
                lanes = pl.ds(LANES * column, LANES)
                code = jnp.round(terms[column] * inverse_scale)
                codes[stage, rows, lanes] = code.astype(jnp.int32).astype(jnp.int16)
            code_copy(stage, place, m).start()
            return carry

        lax.fori_loop(0, 4, inverse_group, 0)
        kept_local(stage).start()
        kept_remote(stage, m).start()
        return carry

    lax.fori_loop(0, half, one_stage, 0)
    for stage in range(half):
        share_copy(stage).wait_send()
        kept_local(stage).wait()
        kept_remote(stage, stage + half * (1 - core)).wait()
        for place in range(4):
            code_copy(stage, place, solved(stage)).wait_send()
    for m in range(slots):
        for group in range(2):
            if m % half == half - 1:
                orbital_copy(m, group).wait_send()
            code_copy(0, group, m).wait_recv()


def exchange(orbitals, pair_first, pair_second, pair_count):
    blocks = lax.axis_size("blk")
    slots = pair_first.shape[1]
    block, rows, cells = orbitals.shape
    lane_fwd, lane_inv = lane_tables()
    row_fwd, row_inv = row_tables()
    tables = [jnp.asarray(t) for t in (lane_fwd, lane_inv, row_fwd, row_inv, filter_table(), twiddle_table())]
    anywhere, smem = (pl.BlockSpec(memory_space=space) for space in (pl.ANY, pltpu.SMEM))
    dma, dmas = pltpu.SemaphoreType.DMA, lambda *shape: pltpu.SemaphoreType.DMA(shape)
    half = slots // 2
    return pl.pallas_call(
        functools.partial(pair_kernel, blocks, slots),
        out_shape=[
            jax.ShapeDtypeStruct((slots, rows, cells), f32),
            jax.ShapeDtypeStruct((slots, rows, cells + LANES), jnp.int16),
            jax.ShapeDtypeStruct((1, 2 * slots + 2), jnp.int32),
        ],
        in_specs=[anywhere] * (4 + len(tables)),
        out_specs=[anywhere, anywhere, smem],
        scratch_shapes=[
            pltpu.VMEM((block, rows, cells), bf16),
            pltpu.VMEM((slots, rows, cells), bf16),
            pltpu.VMEM((half, L, cells), bf16),
            pltpu.VMEM((half, rows, cells), bf16),
            pltpu.VMEM((half, L, cells), bf16),
            pltpu.VMEM((half, L, cells), f32),
            pltpu.VMEM((half, L, cells + LANES), jnp.int16),
            pltpu.VMEM((ROWS, 16, 6 * LANES), bf16),
            pltpu.VMEM((ROWS, L, 2 * LANES), f32),
            pltpu.VMEM((ROWS, 16, 2 * LANES), f32),
            pltpu.VMEM(lane_fwd.shape, bf16),
            pltpu.VMEM(lane_inv.shape, bf16),
            pltpu.VMEM(row_fwd.shape, bf16),
            pltpu.VMEM(row_inv.shape, bf16),
            pltpu.VMEM((ROWS, L, LANES), f32),
            pltpu.VMEM((ROWS, 2, LANES), f32),
            pltpu.SMEM(pair_first.shape, jnp.int32),
            pltpu.SMEM(pair_second.shape, jnp.int32),
            pltpu.SMEM(pair_count.shape, jnp.int32),
            pltpu.SMEM(pair_second.shape, jnp.int32),
            pltpu.SMEM(pair_count.shape, jnp.int32),
            pltpu.SMEM(pair_second.shape, jnp.int32),
            pltpu.SMEM(pair_count.shape, jnp.int32),
            pltpu.SemaphoreType.REGULAR, pltpu.SemaphoreType.REGULAR, dmas(2, 2), dmas(2), dmas(LOADS),
            dmas(9), dmas(2, 2), dmas(2), dmas(slots, 2), dmas(half, 4),
            dmas(half), dmas(half), dmas(half, 4), dmas(slots, 2),
            dmas(half), dmas(half), dmas(half),
        ],
        compiler_params=pltpu.CompilerParams(
            collective_id=0, has_side_effects=True, vmem_limit_bytes=60 * 2**20
        ),
        name="pair_exchange",
    )(orbitals, pair_first, pair_second, pair_count, *tables)


def merge_kernel(
    half, block, kept_in, codes_in, info,
    out, kept, codes, scales, total, zero, staged, kept_sem, code_sem, out_sem,
):
    slots = 2 * half
    first = [info[0, slot] for slot in range(slots)]
    second = [info[0, slots + slot] for slot in range(slots)]
    count, second_count = info[0, 2 * slots], info[0, 2 * slots + 1]
    pieces, width = 4, zero.shape[1] // 4

    def own_live(slot):
        return slot < count

    def back_live(slot):
        return slot < second_count

    loads = []
    for m in range(slots):
        kept_live, code_live = (own_live(m), back_live(m)) if m < half else (back_live(m), own_live(m))
        loads.append((kept_live, pltpu.make_async_copy(kept_in.at[m], kept.at[m], kept_sem.at[m])))
        loads.append((code_live, pltpu.make_async_copy(codes_in.at[m], codes.at[m], code_sem.at[m])))
    for needed, load in loads:
        pl.when(needed)(load.start)
    zero[...] = jnp.zeros_like(zero)

    for row in range(block):
        touched = jnp.bool_(False)
        for slot in range(slots):
            touched |= own_live(slot) & (first[slot] == row)
            touched |= back_live(slot) & (second[slot] == row)

        @pl.when(jnp.logical_not(touched))
        def _():
            pltpu.make_async_copy(zero, out.at[row], out_sem).start()

    for needed, load in loads:
        pl.when(needed)(load.wait)
    for m in range(slots):
        @pl.when(back_live(m) if m < half else own_live(m))
        def _():
            side = codes[m, :, CELLS:].astype(f32)
            scale = scale_of(side[:, :1], side[:, LANES // 2 : LANES // 2 + 1])
            scales[m] = jnp.broadcast_to(scale, scales.shape[1:])

    def over_pieces(body):
        def piece(index, carry):
            body(pl.ds(pl.multiple_of(width * index, width), width))
            return carry

        lax.fori_loop(0, pieces, piece, 0)

    def term(is_kept, m, lanes):
        if is_kept:
            return kept[m, :, lanes]
        return codes[m, :, lanes].astype(f32) * scales[m, :, 0:1]

    def add_up(place, kind_half, lead, live, rows, extra):
        several = jnp.bool_(False)
        for later in range(lead + 1, slots):
            several |= live(later) & (rows[later] == rows[lead])
        for flag, other in extra:
            several |= flag

        @pl.when(jnp.logical_not(several))
        def _():
            def only(lanes):
                staged[place, :, lanes] = term(kind_half(lead), lead, lanes).astype(bf16)

            over_pieces(only)

        @pl.when(several)
        def _():
            def begin(lanes):
                total[:, lanes] = term(kind_half(lead), lead, lanes)

            over_pieces(begin)
            for later in range(lead + 1, slots):

                @pl.when(live(later) & (rows[later] == rows[lead]))
                def _():
                    def more(lanes):
                        total[:, lanes] += term(kind_half(later), later, lanes)

                    over_pieces(more)

            for flag, other in extra:

                @pl.when(flag)
                def _():
                    def more(lanes):
                        total[:, lanes] += staged[other, :, lanes].astype(f32)

                    over_pieces(more)

            def end(lanes):
                staged[place, :, lanes] = total[:, lanes].astype(bf16)

            over_pieces(end)

    leads = []
    for slot in range(slots):
        lead = back_live(slot)
        for earlier in range(slot):
            lead &= second[earlier] != second[slot]
        leads.append(lead)

        @pl.when(lead)
        def _():
            add_up(slot, lambda s: s >= half, slot, back_live, second, [])
            owned = jnp.bool_(False)
            for other in range(slots):
                owned |= own_live(other) & (first[other] == second[slot])

            @pl.when(jnp.logical_not(owned))
            def _():
                pltpu.make_async_copy(staged.at[slot], out.at[second[slot]], out_sem).start()

    for slot in range(slots):
        lead = own_live(slot)
        for earlier in range(slot):
            lead &= first[earlier] != first[slot]

        @pl.when(lead)
        def _():
            extra = [(leads[other] & (second[other] == first[slot]), other) for other in range(slots)]
            add_up(slots + slot, lambda s: s < half, slot, own_live, first, extra)
            pltpu.make_async_copy(staged.at[slots + slot], out.at[first[slot]], out_sem).start()

    pltpu.make_async_copy(out, out, out_sem).wait()


def merge(kept, codes, info, shape):
    slots, rows, cells = kept.shape
    anywhere, smem = (pl.BlockSpec(memory_space=space) for space in (pl.ANY, pltpu.SMEM))
    dma, dmas = pltpu.SemaphoreType.DMA, pltpu.SemaphoreType.DMA((slots,))
    return pl.pallas_call(
        functools.partial(merge_kernel, slots // 2, shape[0]),
        out_shape=jax.ShapeDtypeStruct(shape, bf16),
        in_specs=[anywhere] * 2 + [smem],
        out_specs=anywhere,
        scratch_shapes=[
            pltpu.VMEM(kept.shape, f32),
            pltpu.VMEM(codes.shape, jnp.int16),
            pltpu.VMEM((slots, rows, LANES), f32),
            pltpu.VMEM((rows, cells), f32),
            pltpu.VMEM((rows, cells), bf16),
            pltpu.VMEM((2 * slots, rows, cells), bf16),
            dmas, dmas, dma,
        ],
        compiler_params=pltpu.CompilerParams(vmem_limit_bytes=60 * 2**20),
        name="merge_rows",
    )(kept, codes, info)


def per_device(orbitals, pair_first, pair_second, pair_count):
    kept, codes, info = exchange(orbitals, pair_first, pair_second, pair_count)
    return merge(kept, codes, info, orbitals.shape)


def solution(mesh):
    return jax.shard_map(
        per_device,
        mesh=mesh,
        in_specs=(P("blk", "grid", None), P("blk", None), P("blk", None), P("blk")),
        out_specs=P("blk", "grid", None),
        check_vma=False,
    )
```

```python
import functools
import math

import jax
import jax.numpy as jnp
import ml_dtypes
import numpy as np
from jax import lax
from jax.experimental import pallas as pl
from jax.experimental.pallas import tpu as pltpu
from jax.sharding import PartitionSpec as P

spacing = 0.5
fraction = 0.25
L = 64
HALF = L // 2
LANES = 128
ROWS = 17
LOADS = 4
CODE = 32767.0
MANTISSA = 16384.0
CELLS = L * L
f32 = jnp.float32
bf16 = jnp.bfloat16


def split_table(table):
    high = table.astype(ml_dtypes.bfloat16)
    low = (table - high.astype(np.float64)).astype(ml_dtypes.bfloat16)
    return high, low


def lane_tables():
    position = np.arange(L)
    angle = 2.0 * np.pi * (np.outer(position, position) % L) / L
    sign = np.array([[1.0, 1.0], [1.0, -1.0]])
    real = np.kron(sign, np.cos(angle))
    imag = np.kron(sign, -np.sin(angle))
    forward = np.block([[real, imag], [-imag, real]])
    inverse = np.block([[real, -imag], [imag, real]])
    (forward, low), (inverse, inverse_low) = split_table(forward), split_table(inverse)
    return np.concatenate([forward, forward, low]), np.concatenate([inverse, inverse, inverse_low])


def row_tables():
    position = np.arange(L)
    angle = 2.0 * np.pi * (np.outer(position, position) % L) / L
    both = np.concatenate([np.cos(angle), np.sin(angle)], 0)
    high, low = split_table(both)
    table = np.concatenate([high, high, low], 1)
    return table, table


def filter_table():
    wrapped = np.arange(L)
    wrapped = np.where(wrapped >= HALF, wrapped - L, wrapped)
    squares = (wrapped * (2.0 * np.pi / (L * spacing))) ** 2
    ky = np.arange(ROWS)[:, None] + HALF * np.arange(2)[None, :]
    total = squares[None, :, None, None] + squares[ky][:, None, :, None] + squares[None, None, None, :]
    kernel = np.where(total > 0, 4.0 * np.pi / np.where(total > 0, total, 1.0), 0.0)
    return (-fraction / L**3 * kernel).reshape(ROWS, L, LANES).astype(np.float32)


def twiddle_table():
    odd = np.repeat(np.arange(2), L)
    angle = 2.0 * np.pi * np.outer(np.arange(ROWS), odd) / L
    return np.stack([np.cos(angle), -np.sin(angle)], 1).astype(np.float32)


def real_forward(values):
    count = len(values)
    if count == 2:
        return [values[0] + values[1], values[0] - values[1]], [None, None]
    even_re, even_im = real_forward(values[0::2])
    odd_re, odd_im = real_forward(values[1::2])
    half, quarter = count // 2, count // 4
    re, im = [None] * (half + 1), [None] * (half + 1)
    re[0], re[half] = even_re[0] + odd_re[0], even_re[0] - odd_re[0]
    re[quarter], im[quarter] = even_re[quarter], -odd_re[quarter]
    for k in range(1, quarter):
        c, s = math.cos(2.0 * math.pi * k / count), math.sin(2.0 * math.pi * k / count)
        if 2 * k == quarter:
            turned_re, turned_im = c * (odd_re[k] + odd_im[k]), c * (odd_im[k] - odd_re[k])
        else:
            turned_re = c * odd_re[k] + s * odd_im[k]
            turned_im = c * odd_im[k] - s * odd_re[k]
        re[k], im[k] = even_re[k] + turned_re, even_im[k] + turned_im
        re[half - k], im[half - k] = even_re[k] - turned_re, turned_im - even_im[k]
    return re, im


def real_inverse(re, im):
    half = len(re) - 1
    count = 2 * half
    if count == 2:
        return [re[0] + re[1], re[0] - re[1]]
    quarter = half // 2
    even_re, even_im = [None] * (quarter + 1), [None] * (quarter + 1)
    odd_re, odd_im = [None] * (quarter + 1), [None] * (quarter + 1)
    even_re[0], odd_re[0] = re[0] + re[half], re[0] - re[half]
    even_re[quarter], odd_re[quarter] = 2.0 * re[quarter], -2.0 * im[quarter]
    for k in range(1, quarter):
        c, s = math.cos(2.0 * math.pi * k / count), math.sin(2.0 * math.pi * k / count)
        even_re[k], even_im[k] = re[k] + re[half - k], im[k] - im[half - k]
        part_re, part_im = re[k] - re[half - k], im[k] + im[half - k]
        if 2 * k == quarter:
            odd_re[k], odd_im[k] = c * (part_re - part_im), c * (part_re + part_im)
        else:
            odd_re[k] = c * part_re - s * part_im
            odd_im[k] = s * part_re + c * part_im
    evens, odds = real_inverse(even_re, even_im), real_inverse(odd_re, odd_im)
    return [value for pair in zip(evens, odds) for value in pair]


def split(values):
    high = values.astype(bf16)
    return high, (values - high.astype(f32)).astype(bf16)


def scale_of(mantissa, exponent):
    return mantissa * jnp.exp2(exponent) * (1.0 / (MANTISSA * CODE))


def dot(left, right):
    return jnp.dot(left, right, preferred_element_type=f32)


def pair_kernel(
    blocks, slots,
    orbitals, first_in, second_in, count_in,
    lane_fwd, lane_inv, row_fwd, row_inv, filters, twiddles,
    kept_out, codes_out, info,
    orb, sending, arriving, sharing, whole, kept, codes,
    spectra, planes, result,
    lane_fwd_v, lane_inv_v, row_fwd_v, row_inv_v, filters_v, twiddles_v, first_s, second_s, count_s,
    next_second, next_count, relay_second, relay_count, final_here, left_here, relay_send, relay_recv, load_sem,
    table_sem, index_send, index_recv, orbital_send, orbital_recv,
    share_send, share_recv, code_send, code_recv, kept_sem, kept_send, kept_recv,
):
    half = slots // 2
    me, core = lax.axis_index("blk"), lax.axis_index("grid")
    right, left = lax.rem(me + 1, blocks), lax.rem(me + blocks - 1, blocks)
    to_partner = {"grid": 1 - core}

    final, relay = blocks - 1, max(2, blocks // 4) - 1
    is_first, is_final, before_final = me == 0, me == final, me == final - 1
    sends_index, is_relay = core == 1, (me == relay) & (core == 1)
    barrier = pltpu.get_barrier_semaphore()
    for place in range(2):
        pl.semaphore_signal(barrier, inc=1, device_id={"blk": left, "grid": place})
    pl.semaphore_signal(barrier, inc=1, device_id=to_partner)

    @pl.when(jnp.logical_not(is_final | before_final))
    def _():
        for place in range(2):
            pl.semaphore_signal(barrier, inc=1, device_id={"blk": right, "grid": place})

    @pl.when(is_relay)
    def _():
        for device in ({"blk": 0, "grid": 1}, {"blk": final, "grid": 0}, {"blk": final, "grid": 1}):
            pl.semaphore_signal(barrier, inc=1, device_id=device)

    size = orb.shape[0] // LOADS
    loads = [
        pltpu.make_async_copy(orbitals.at[pl.ds(size * n, size)], orb.at[pl.ds(size * n, size)], load_sem.at[n])
        for n in range(LOADS)
    ]
    for load in loads:
        load.start()
    tables = [
        pltpu.make_async_copy(source, target, table_sem.at[place])
        for place, (source, target) in enumerate([
            (first_in, first_s), (second_in, second_s), (count_in, count_s),
            (lane_fwd, lane_fwd_v), (lane_inv, lane_inv_v), (row_fwd, row_fwd_v), (row_inv, row_inv_v),
            (filters, filters_v), (twiddles, twiddles_v),
        ])
    ]
    for table in tables:
        table.start()

    def remote(source, target, send, recv, device):
        return pltpu.make_async_remote_copy(
            src_ref=source, dst_ref=target, send_sem=send, recv_sem=recv, device_id=device
        )

    def index_copies(targets, sent, arrived, device, sources=(second_in, count_in)):
        return [
            remote(source, target, sent.at[part], arrived.at[part], device)
            for part, (source, target) in enumerate(zip(sources, targets))
        ]

    def to_both(block, sent, sources=(second_in, count_in)):
        targets = (next_second, next_count)
        return [
            copy
            for place in range(2)
            for copy in index_copies(targets, sent.at[place], index_recv, {"blk": block, "grid": place}, sources)
        ]

    to_next = to_both(left, index_send)
    to_relay = index_copies((relay_second, relay_count), index_send.at[0], relay_recv, {"blk": relay, "grid": 1})

    def orbital_copy(m, group):
        visits = m < half
        device = {"blk": right if visits else left, "grid": 0 if visits else 1}
        place = 2 * core + group
        return remote(
            sending.at[m, pl.ds(16 * group, 16)],
            arriving.at[m % half, pl.ds(pl.multiple_of(16 * place, 16), 16)],
            orbital_send.at[m, group], orbital_recv.at[m % half, place], device,
        )

    def arrival(stage, place):
        rows = pl.ds(pl.multiple_of(16 * place, 16), 16)
        return remote(
            sending.at[0, pl.ds(0, 16)], arriving.at[stage, rows],
            orbital_send.at[0, 0], orbital_recv.at[stage, place], to_partner,
        )

    def worked_on(stage, by):
        return jnp.where(by == 0, first_s[0, stage], next_second[0, half + stage])

    def share_copy(stage):
        rows = pl.ds(pl.multiple_of(HALF * core, HALF), HALF)
        return remote(sharing.at[stage], whole.at[stage, rows], share_send.at[stage], share_recv.at[stage], to_partner)

    def send_first(m):
        for group in range(2):
            orbital_copy(m, group).start()

    def load_own():
        for table in tables[:3]:
            table.wait()
        for load in loads:
            load.wait()
        for m in range(half, slots):
            sending[m] = orb[first_s[0, m]]

    def load_visits():
        for copy in to_next[:2]:
            copy.wait_recv()
        for m in range(half):
            sending[m] = orb[next_second[0, m]]

    normal = 5 - is_final.astype(jnp.int32)
    pl.semaphore_wait(barrier, jnp.where(is_first, 3 + core, normal))

    @pl.when(before_final)
    def _():
        for place in range(2):
            pl.semaphore_signal(left_here, inc=1, device_id={"blk": right, "grid": place})

    @pl.when(is_final)
    def _():
        for place in range(2):
            pl.semaphore_signal(final_here, inc=1, device_id={"blk": right, "grid": place})
        pl.semaphore_signal(final_here, inc=1, device_id={"blk": relay, "grid": 1})
        pl.semaphore_wait(left_here, 2)

    @pl.when(is_first)
    def _():
        @pl.when(sends_index)
        def _():
            for copy in to_relay:
                copy.start()

        load_own()
        load_visits()
        send_first(0)
        pl.semaphore_wait(final_here, 2)
        send_first(half)

        @pl.when(sends_index)
        def _():
            for copy in to_relay:
                copy.wait_send()

    @pl.when(jnp.logical_not(is_first))
    def _():
        @pl.when(sends_index)
        def _():
            for copy in to_next:
                copy.start()

        load_own()
        send_first(half)

        @pl.when(is_relay)
        def _():
            for copy in to_relay:
                copy.wait_recv()
            pl.semaphore_wait(final_here, 2)
            onward = to_both(final, relay_send, (relay_second, relay_count))
            for copy in onward:
                copy.start()
            for copy in onward:
                copy.wait_send()

        load_visits()
        send_first(0)

        @pl.when(sends_index)
        def _():
            for copy in to_next:
                copy.wait_send()

    for stage in range(half):
        sharing[stage] = orb[worked_on(stage, 1 - core)]
        share_copy(stage).start()
        whole[stage, pl.ds(pl.multiple_of(HALF * core, HALF), HALF)] = orb[worked_on(stage, core)]
    for stage in range(1, half):
        for group in range(2):
            for m in (half + stage, stage):
                orbital_copy(m - 1, group).wait_send()
                orbital_copy(m, group).start()
    for table in tables[3:]:
        table.wait()
    for m in range(slots):
        info[0, m] = first_s[0, m]
        info[0, slots + m] = next_second[0, m]
    info[0, 2 * slots] = count_s[0]
    info[0, 2 * slots + 1] = next_count[0]

    def solved(stage):
        return stage + half * core

    def kept_local(stage):
        rows = pl.ds(pl.multiple_of(HALF * core, HALF), HALF)
        return pltpu.make_async_copy(kept.at[stage, rows], kept_out.at[solved(stage)], kept_sem.at[stage])

    def kept_remote(stage, m):
        rows = pl.ds(pl.multiple_of(HALF * (1 - core), HALF), HALF)
        return remote(kept.at[stage, rows], kept_out.at[m], kept_send.at[stage], kept_recv.at[stage], to_partner)

    def code_copy(stage, place, m):
        device = {"blk": jnp.where(core == 0, left, right), "grid": lax.div(place, 2)}
        rows = pl.ds(pl.multiple_of(16 * place, 16), 16)
        there = pl.ds(pl.multiple_of(16 * lax.rem(place, 2), 16), 16)
        return remote(
            codes.at[stage, rows], codes_out.at[m, there],
            code_send.at[stage, place], code_recv.at[m, lax.rem(place, 2)], device,
        )

    def one_stage(stage, carry):
        m = solved(stage)
        share_copy(stage).wait_recv()

        def forward_group(turn, carry):
            place = 2 * lax.rem(turn, 2) + lax.div(turn, 2)
            rows = pl.ds(pl.multiple_of(16 * place, 16), 16)
            arrival(stage, place).wait_recv()
            values = []
            for column in range(HALF):
                lanes = pl.ds(LANES * column, LANES)
                values.append(whole[stage, rows, lanes].astype(f32) * arriving[stage, rows, lanes].astype(f32))
            re, im = real_forward(values)
            for k in range(ROWS):
                if k == 0:
                    turned_re, turned_im = re[0], jnp.zeros_like(re[0])
                else:
                    c, s = twiddles_v[k, 0:1], twiddles_v[k, 1:2]
                    if im[k] is None:
                        turned_re, turned_im = re[k] * c, re[k] * s
                    else:
                        turned_re, turned_im = re[k] * c - im[k] * s, re[k] * s + im[k] * c
                for part, value in enumerate((turned_re, turned_im)):
                    high, low = split(value)
                    for place, piece in enumerate((high, low, high)):
                        start = LANES * (2 * place + part)
                        spectra[k, :, start : start + LANES] = piece
            out = dot(spectra[...].reshape(ROWS * 16, 6 * LANES), lane_fwd_v[...])
            planes[:, rows, :] = out.reshape(ROWS, 16, 2 * LANES)
            return carry

        lax.fori_loop(0, 4, forward_group, 0)

        for k in range(ROWS):
            high, low = split(planes[k])
            out = dot(row_fwd_v[...], jnp.concatenate([high, low, high], 0))
            kernel = filters_v[k]
            re = (out[:L, :LANES] + out[L:, LANES:]) * kernel
            im = (out[:L, LANES:] - out[L:, :LANES]) * kernel
            high, low = split(jnp.concatenate([re, im], 1))
            out = dot(row_inv_v[...], jnp.concatenate([high, low, high], 0))
            re = out[:L, :LANES] - out[L:, LANES:]
            im = out[:L, LANES:] + out[L:, :LANES]
            planes[k] = jnp.concatenate([re, im], 1)

        live = jnp.where(m < jnp.where(core == 0, count_s[0], next_count[0]), 1.0, 0.0).astype(f32)

        def inverse_group(turn, carry):
            place = 2 * (1 - lax.rem(turn, 2)) + lax.div(turn, 2)
            rows = pl.ds(pl.multiple_of(16 * place, 16), 16)
            high, low = split(planes[:, rows, :].reshape(ROWS * 16, 2 * LANES))
            out = dot(jnp.concatenate([high, low, high], 1), lane_inv_v[...])
            result[...] = out.reshape(ROWS, 16, 2 * LANES)
            re, im = [], []
            for k in range(ROWS):
                value_re = result[k, :, :LANES]
                if k == 0:
                    re.append(value_re)
                    im.append(None)
                    continue
                value_im = result[k, :, LANES:]
                c, s = twiddles_v[k, 0:1], twiddles_v[k, 1:2]
                re.append(value_re * c + value_im * s)
                im.append(None if k == ROWS - 1 else value_im * c - value_re * s)
            potential = real_inverse(re, im)
            terms, largest = [], None
            for column in range(HALF):
                lanes = pl.ds(LANES * column, LANES)
                value = potential[column] * live
                kept[stage, rows, lanes] = value * arriving[stage, rows, lanes].astype(f32)
                terms.append(value * whole[stage, rows, lanes].astype(f32))
                size = jnp.abs(terms[-1])
                largest = size if largest is None else jnp.maximum(largest, size)
            bound = jnp.broadcast_to(jnp.maximum(jnp.max(largest, axis=1, keepdims=True), 1e-30), (16, LANES))
            exponent = jnp.ceil(jnp.log2(bound))
            mantissa = jnp.ceil(bound * jnp.exp2(-exponent) * MANTISSA)
            side = lax.broadcasted_iota(jnp.int32, (16, LANES), 1) < LANES // 2
            codes[stage, rows, CELLS:] = jnp.where(side, mantissa, exponent).astype(jnp.int32).astype(jnp.int16)
            inverse_scale = 1.0 / scale_of(mantissa, exponent)
            for column in range(HALF):
                lanes = pl.ds(LANES * column, LANES)
                code = jnp.round(terms[column] * inverse_scale)
                codes[stage, rows, lanes] = code.astype(jnp.int32).astype(jnp.int16)
            code_copy(stage, place, m).start()
            return carry

        lax.fori_loop(0, 4, inverse_group, 0)
        kept_local(stage).start()
        kept_remote(stage, m).start()
        return carry

    lax.fori_loop(0, half, one_stage, 0)
    for stage in range(half):
        share_copy(stage).wait_send()
        kept_local(stage).wait()
        kept_remote(stage, stage + half * (1 - core)).wait()
        for place in range(4):
            code_copy(stage, place, solved(stage)).wait_send()
    for m in range(slots):
        for group in range(2):
            if m % half == half - 1:
                orbital_copy(m, group).wait_send()
            code_copy(0, group, m).wait_recv()


def exchange(orbitals, pair_first, pair_second, pair_count):
    blocks = lax.axis_size("blk")
    slots = pair_first.shape[1]
    block, rows, cells = orbitals.shape
    lane_fwd, lane_inv = lane_tables()
    row_fwd, row_inv = row_tables()
    tables = [jnp.asarray(t) for t in (lane_fwd, lane_inv, row_fwd, row_inv, filter_table(), twiddle_table())]
    anywhere, smem = (pl.BlockSpec(memory_space=space) for space in (pl.ANY, pltpu.SMEM))
    dma, dmas = pltpu.SemaphoreType.DMA, lambda *shape: pltpu.SemaphoreType.DMA(shape)
    half = slots // 2
    return pl.pallas_call(
        functools.partial(pair_kernel, blocks, slots),
        out_shape=[
            jax.ShapeDtypeStruct((slots, rows, cells), f32),
            jax.ShapeDtypeStruct((slots, rows, cells + LANES), jnp.int16),
            jax.ShapeDtypeStruct((1, 2 * slots + 2), jnp.int32),
        ],
        in_specs=[anywhere] * (4 + len(tables)),
        out_specs=[anywhere, anywhere, smem],
        scratch_shapes=[
            pltpu.VMEM((block, rows, cells), bf16),
            pltpu.VMEM((slots, rows, cells), bf16),
            pltpu.VMEM((half, L, cells), bf16),
            pltpu.VMEM((half, rows, cells), bf16),
            pltpu.VMEM((half, L, cells), bf16),
            pltpu.VMEM((half, L, cells), f32),
            pltpu.VMEM((half, L, cells + LANES), jnp.int16),
            pltpu.VMEM((ROWS, 16, 6 * LANES), bf16),
            pltpu.VMEM((ROWS, L, 2 * LANES), f32),
            pltpu.VMEM((ROWS, 16, 2 * LANES), f32),
            pltpu.VMEM(lane_fwd.shape, bf16),
            pltpu.VMEM(lane_inv.shape, bf16),
            pltpu.VMEM(row_fwd.shape, bf16),
            pltpu.VMEM(row_inv.shape, bf16),
            pltpu.VMEM((ROWS, L, LANES), f32),
            pltpu.VMEM((ROWS, 2, LANES), f32),
            pltpu.SMEM(pair_first.shape, jnp.int32),
            pltpu.SMEM(pair_second.shape, jnp.int32),
            pltpu.SMEM(pair_count.shape, jnp.int32),
            pltpu.SMEM(pair_second.shape, jnp.int32),
            pltpu.SMEM(pair_count.shape, jnp.int32),
            pltpu.SMEM(pair_second.shape, jnp.int32),
            pltpu.SMEM(pair_count.shape, jnp.int32),
            pltpu.SemaphoreType.REGULAR, pltpu.SemaphoreType.REGULAR, dmas(2, 2), dmas(2), dmas(LOADS),
            dmas(9), dmas(2, 2), dmas(2), dmas(slots, 2), dmas(half, 4),
            dmas(half), dmas(half), dmas(half, 4), dmas(slots, 2),
            dmas(half), dmas(half), dmas(half),
        ],
        compiler_params=pltpu.CompilerParams(
            collective_id=0, has_side_effects=True, vmem_limit_bytes=60 * 2**20
        ),
        name="pair_exchange",
    )(orbitals, pair_first, pair_second, pair_count, *tables)


def merge_kernel(
    half, block, kept_in, codes_in, info,
    out, kept, codes, scales, total, zero, staged, single, goes_to, kept_sem, code_sem, out_sem,
):
    slots = 2 * half
    first = [info[0, slot] for slot in range(slots)]
    second = [info[0, slots + slot] for slot in range(slots)]
    count, second_count = info[0, 2 * slots], info[0, 2 * slots + 1]
    pieces, width = 4, zero.shape[1] // 4

    def own_live(slot):
        return slot < count

    def back_live(slot):
        return slot < second_count

    loads = []
    for m in range(slots):
        kept_live, code_live = (own_live(m), back_live(m)) if m < half else (back_live(m), own_live(m))
        loads.append((kept_live, pltpu.make_async_copy(kept_in.at[m], kept.at[m], kept_sem.at[m])))
        loads.append((code_live, pltpu.make_async_copy(codes_in.at[m], codes.at[m], code_sem.at[m])))
    for needed, load in loads:
        pl.when(needed)(load.start)
    zero[...] = jnp.zeros_like(zero)

    for row in range(block):
        touched = jnp.bool_(False)
        for slot in range(slots):
            touched |= own_live(slot) & (first[slot] == row)
            touched |= back_live(slot) & (second[slot] == row)

        @pl.when(jnp.logical_not(touched))
        def _():
            pltpu.make_async_copy(zero, out.at[row], out_sem).start()

    for needed, load in loads:
        pl.when(needed)(load.wait)
    for m in range(slots):
        @pl.when(back_live(m) if m < half else own_live(m))
        def _():
            side = codes[m, :, CELLS:].astype(f32)
            scale = scale_of(side[:, :1], side[:, LANES // 2 : LANES // 2 + 1])
            scales[m] = jnp.broadcast_to(scale, scales.shape[1:])

    def over_pieces(body):
        def piece(index, carry):
            body(pl.ds(pl.multiple_of(width * index, width), width))
            return carry

        lax.fori_loop(0, pieces, piece, 0)

    def term(is_kept, m, lanes):
        if is_kept:
            return kept[m, :, lanes]
        return codes[m, :, lanes].astype(f32) * scales[m, :, 0:1]

    def add_up(place, kind_half, lead, live, rows, extra):
        def begin(lanes):
            total[:, lanes] = term(kind_half(lead), lead, lanes)

        over_pieces(begin)
        for later in range(lead + 1, slots):

            @pl.when(live(later) & (rows[later] == rows[lead]))
            def _():
                def more(lanes):
                    total[:, lanes] += term(kind_half(later), later, lanes)

                over_pieces(more)

        for flag, other in extra:

            @pl.when(flag)
            def _():
                def more(lanes):
                    total[:, lanes] += staged[other, :, lanes].astype(f32)

                over_pieces(more)

        def end(lanes):
            staged[place, :, lanes] = total[:, lanes].astype(bf16)

        over_pieces(end)

    def alone(n, carry):
        m = lax.rem(n, slots)
        is_kept = (n < slots) == (m >= half)

        @pl.when((single[n] == 1) & is_kept)
        def _():
            for piece in range(2):
                lanes = pl.ds(CELLS // 2 * piece, CELLS // 2)
                staged[n, :, lanes] = kept[m, :, lanes].astype(bf16)

        @pl.when((single[n] == 1) & jnp.logical_not(is_kept))
        def _():
            for piece in range(2):
                lanes = pl.ds(CELLS // 2 * piece, CELLS // 2)
                staged[n, :, lanes] = (codes[m, :, lanes].astype(f32) * scales[m, :, 0:1]).astype(bf16)

        @pl.when(goes_to[n] >= 0)
        def _():
            pltpu.make_async_copy(staged.at[n], out.at[goes_to[n]], out_sem).start()

        return carry

    def plan(n, lead, several, has_row, row):
        single[n] = (lead & jnp.logical_not(several)).astype(jnp.int32)
        goes_to[n] = jnp.where(lead & jnp.logical_not(several) & has_row, row, -1)

    leads, sums = [], []
    for slot in range(slots):
        lead, several, owned = back_live(slot), jnp.bool_(False), jnp.bool_(False)
        for earlier in range(slot):
            lead &= second[earlier] != second[slot]
        for later in range(slot + 1, slots):
            several |= back_live(later) & (second[later] == second[slot])
        for other in range(slots):
            owned |= own_live(other) & (first[other] == second[slot])
        leads.append(lead)
        sums.append((lead & several, owned))
        plan(slot, lead, several, jnp.logical_not(owned), second[slot])
    lax.fori_loop(0, slots, alone, 0)
    for slot, (several, owned) in enumerate(sums):

        @pl.when(several)
        def _():
            add_up(slot, lambda s: s >= half, slot, back_live, second, [])

            @pl.when(jnp.logical_not(owned))
            def _():
                pltpu.make_async_copy(staged.at[slot], out.at[second[slot]], out_sem).start()

    sums = []
    for slot in range(slots):
        lead, several = own_live(slot), jnp.bool_(False)
        for earlier in range(slot):
            lead &= first[earlier] != first[slot]
        for later in range(slot + 1, slots):
            several |= own_live(later) & (first[later] == first[slot])
        extra = [(leads[other] & (second[other] == first[slot]), other) for other in range(slots)]
        for flag, other in extra:
            several |= flag
        sums.append((lead & several, extra))
        plan(slots + slot, lead, several, jnp.bool_(True), first[slot])
    lax.fori_loop(slots, 2 * slots, alone, 0)
    for slot, (several, extra) in enumerate(sums):

        @pl.when(several)
        def _():
            add_up(slots + slot, lambda s: s < half, slot, own_live, first, extra)
            pltpu.make_async_copy(staged.at[slots + slot], out.at[first[slot]], out_sem).start()

    pltpu.make_async_copy(out, out, out_sem).wait()


def merge(kept, codes, info, shape):
    slots, rows, cells = kept.shape
    anywhere, smem = (pl.BlockSpec(memory_space=space) for space in (pl.ANY, pltpu.SMEM))
    dma, dmas = pltpu.SemaphoreType.DMA, pltpu.SemaphoreType.DMA((slots,))
    return pl.pallas_call(
        functools.partial(merge_kernel, slots // 2, shape[0]),
        out_shape=jax.ShapeDtypeStruct(shape, bf16),
        in_specs=[anywhere] * 2 + [smem],
        out_specs=anywhere,
        scratch_shapes=[
            pltpu.VMEM(kept.shape, f32),
            pltpu.VMEM(codes.shape, jnp.int16),
            pltpu.VMEM((slots, rows, LANES), f32),
            pltpu.VMEM((rows, cells), f32),
            pltpu.VMEM((rows, cells), bf16),
            pltpu.VMEM((2 * slots, rows, cells), bf16),
            pltpu.SMEM((2 * slots,), jnp.int32),
            pltpu.SMEM((2 * slots,), jnp.int32),
            dmas, dmas, dma,
        ],
        compiler_params=pltpu.CompilerParams(vmem_limit_bytes=60 * 2**20),
        name="merge_rows",
    )(kept, codes, info)


def per_device(orbitals, pair_first, pair_second, pair_count):
    kept, codes, info = exchange(orbitals, pair_first, pair_second, pair_count)
    return merge(kept, codes, info, orbitals.shape)


def solution(mesh):
    return jax.shard_map(
        per_device,
        mesh=mesh,
        in_specs=(P("blk", "grid", None), P("blk", None), P("blk", None), P("blk")),
        out_specs=P("blk", "grid", None),
        check_vma=False,
    )
```

```python
import functools
import math

import jax
import jax.numpy as jnp
import ml_dtypes
import numpy as np
from jax import lax
from jax.experimental import pallas as pl
from jax.experimental.pallas import tpu as pltpu
from jax.sharding import PartitionSpec as P

spacing = 0.5
fraction = 0.25
L = 64
HALF = L // 2
LANES = 128
ROWS = 17
LOADS = 4
CODE = 32767.0
MANTISSA = 16384.0
CELLS = L * L
f32 = jnp.float32
bf16 = jnp.bfloat16


def split_table(table):
    high = table.astype(ml_dtypes.bfloat16)
    low = (table - high.astype(np.float64)).astype(ml_dtypes.bfloat16)
    return high, low


def lane_tables():
    position = np.arange(L)
    angle = 2.0 * np.pi * (np.outer(position, position) % L) / L
    sign = np.array([[1.0, 1.0], [1.0, -1.0]])
    real = np.kron(sign, np.cos(angle))
    imag = np.kron(sign, -np.sin(angle))
    forward = np.block([[real, imag], [-imag, real]])
    inverse = np.block([[real, -imag], [imag, real]])
    (forward, low), (inverse, inverse_low) = split_table(forward), split_table(inverse)
    return np.concatenate([forward, forward, low]), np.concatenate([inverse, inverse, inverse_low])


def row_tables():
    position = np.arange(L)
    angle = 2.0 * np.pi * (np.outer(position, position) % L) / L
    both = np.concatenate([np.cos(angle), np.sin(angle)], 0)
    high, low = split_table(both)
    table = np.concatenate([high, high, low], 1)
    return table, table


def filter_table():
    wrapped = np.arange(L)
    wrapped = np.where(wrapped >= HALF, wrapped - L, wrapped)
    squares = (wrapped * (2.0 * np.pi / (L * spacing))) ** 2
    ky = np.arange(ROWS)[:, None] + HALF * np.arange(2)[None, :]
    total = squares[None, :, None, None] + squares[ky][:, None, :, None] + squares[None, None, None, :]
    kernel = np.where(total > 0, 4.0 * np.pi / np.where(total > 0, total, 1.0), 0.0)
    return (-fraction / L**3 * kernel).reshape(ROWS, L, LANES).astype(np.float32)


def twiddle_table():
    odd = np.repeat(np.arange(2), L)
    angle = 2.0 * np.pi * np.outer(np.arange(ROWS), odd) / L
    return np.stack([np.cos(angle), -np.sin(angle)], 1).astype(np.float32)


def real_forward(values):
    count = len(values)
    if count == 2:
        return [values[0] + values[1], values[0] - values[1]], [None, None]
    even_re, even_im = real_forward(values[0::2])
    odd_re, odd_im = real_forward(values[1::2])
    half, quarter = count // 2, count // 4
    re, im = [None] * (half + 1), [None] * (half + 1)
    re[0], re[half] = even_re[0] + odd_re[0], even_re[0] - odd_re[0]
    re[quarter], im[quarter] = even_re[quarter], -odd_re[quarter]
    for k in range(1, quarter):
        c, s = math.cos(2.0 * math.pi * k / count), math.sin(2.0 * math.pi * k / count)
        if 2 * k == quarter:
            turned_re, turned_im = c * (odd_re[k] + odd_im[k]), c * (odd_im[k] - odd_re[k])
        else:
            turned_re = c * odd_re[k] + s * odd_im[k]
            turned_im = c * odd_im[k] - s * odd_re[k]
        re[k], im[k] = even_re[k] + turned_re, even_im[k] + turned_im
        re[half - k], im[half - k] = even_re[k] - turned_re, turned_im - even_im[k]
    return re, im


def real_inverse(re, im):
    half = len(re) - 1
    count = 2 * half
    if count == 2:
        return [re[0] + re[1], re[0] - re[1]]
    quarter = half // 2
    even_re, even_im = [None] * (quarter + 1), [None] * (quarter + 1)
    odd_re, odd_im = [None] * (quarter + 1), [None] * (quarter + 1)
    even_re[0], odd_re[0] = re[0] + re[half], re[0] - re[half]
    even_re[quarter], odd_re[quarter] = 2.0 * re[quarter], -2.0 * im[quarter]
    for k in range(1, quarter):
        c, s = math.cos(2.0 * math.pi * k / count), math.sin(2.0 * math.pi * k / count)
        even_re[k], even_im[k] = re[k] + re[half - k], im[k] - im[half - k]
        part_re, part_im = re[k] - re[half - k], im[k] + im[half - k]
        if 2 * k == quarter:
            odd_re[k], odd_im[k] = c * (part_re - part_im), c * (part_re + part_im)
        else:
            odd_re[k] = c * part_re - s * part_im
            odd_im[k] = s * part_re + c * part_im
    evens, odds = real_inverse(even_re, even_im), real_inverse(odd_re, odd_im)
    return [value for pair in zip(evens, odds) for value in pair]


def split(values):
    high = values.astype(bf16)
    return high, (values - high.astype(f32)).astype(bf16)


def scale_of(mantissa, exponent):
    return mantissa * jnp.exp2(exponent) * (1.0 / (MANTISSA * CODE))


def dot(left, right):
    return jnp.dot(left, right, preferred_element_type=f32)


def pair_kernel(
    blocks, slots,
    orbitals, first_in, second_in, count_in,
    lane_fwd, lane_inv, row_fwd, row_inv, filters, twiddles,
    kept_out, codes_out, info,
    orb, sending, arriving, sharing, whole, kept, codes,
    spectra, planes, result,
    lane_fwd_v, lane_inv_v, row_fwd_v, row_inv_v, filters_v, twiddles_v, first_s, second_s, count_s,
    next_second, next_count, relay_second, relay_count, final_here, left_here, relay_send, relay_recv, load_sem,
    table_sem, index_send, index_recv, orbital_send, orbital_recv,
    share_send, share_recv, code_send, code_recv, kept_sem, kept_send, kept_recv,
):
    half = slots // 2
    me, core = lax.axis_index("blk"), lax.axis_index("grid")
    right, left = lax.rem(me + 1, blocks), lax.rem(me + blocks - 1, blocks)
    to_partner = {"grid": 1 - core}

    final, relay = blocks - 1, max(2, blocks // 4) - 1
    is_first, is_final, before_final = me == 0, me == final, me == final - 1
    sends_index, is_relay = core == 1, (me == relay) & (core == 1)
    barrier = pltpu.get_barrier_semaphore()
    for place in range(2):
        pl.semaphore_signal(barrier, inc=1, device_id={"blk": left, "grid": place})
    pl.semaphore_signal(barrier, inc=1, device_id=to_partner)

    @pl.when(jnp.logical_not(is_final | before_final))
    def _():
        for place in range(2):
            pl.semaphore_signal(barrier, inc=1, device_id={"blk": right, "grid": place})

    @pl.when(is_relay)
    def _():
        for device in ({"blk": 0, "grid": 1}, {"blk": final, "grid": 0}, {"blk": final, "grid": 1}):
            pl.semaphore_signal(barrier, inc=1, device_id=device)

    size = orb.shape[0] // LOADS
    loads = [
        pltpu.make_async_copy(orbitals.at[pl.ds(size * n, size)], orb.at[pl.ds(size * n, size)], load_sem.at[n])
        for n in range(LOADS)
    ]
    for load in loads:
        load.start()
    tables = [
        pltpu.make_async_copy(source, target, table_sem.at[place])
        for place, (source, target) in enumerate([
            (first_in, first_s), (second_in, second_s), (count_in, count_s),
            (lane_fwd, lane_fwd_v), (lane_inv, lane_inv_v), (row_fwd, row_fwd_v), (row_inv, row_inv_v),
            (filters, filters_v), (twiddles, twiddles_v),
        ])
    ]
    for table in tables:
        table.start()

    def remote(source, target, send, recv, device):
        return pltpu.make_async_remote_copy(
            src_ref=source, dst_ref=target, send_sem=send, recv_sem=recv, device_id=device
        )

    def index_copies(targets, sent, arrived, device, sources=(second_in, count_in)):
        return [
            remote(source, target, sent.at[part], arrived.at[part], device)
            for part, (source, target) in enumerate(zip(sources, targets))
        ]

    def to_both(block, sent, sources=(second_in, count_in)):
        targets = (next_second, next_count)
        return [
            copy
            for place in range(2)
            for copy in index_copies(targets, sent.at[place], index_recv, {"blk": block, "grid": place}, sources)
        ]

    to_next = to_both(left, index_send)
    to_relay = index_copies((relay_second, relay_count), index_send.at[0], relay_recv, {"blk": relay, "grid": 1})

    def orbital_copy(m, group):
        visits = m < half
        device = {"blk": right if visits else left, "grid": 0 if visits else 1}
        place = 2 * core + group
        return remote(
            sending.at[m, pl.ds(16 * group, 16)],
            arriving.at[m % half, pl.ds(pl.multiple_of(16 * place, 16), 16)],
            orbital_send.at[m, group], orbital_recv.at[m % half, place], device,
        )

    def arrival(stage, place):
        rows = pl.ds(pl.multiple_of(16 * place, 16), 16)
        return remote(
            sending.at[0, pl.ds(0, 16)], arriving.at[stage, rows],
            orbital_send.at[0, 0], orbital_recv.at[stage, place], to_partner,
        )

    def worked_on(stage, by):
        return jnp.where(by == 0, first_s[0, stage], next_second[0, half + stage])

    def share_copy(stage):
        rows = pl.ds(pl.multiple_of(HALF * core, HALF), HALF)
        return remote(sharing.at[stage], whole.at[stage, rows], share_send.at[stage], share_recv.at[stage], to_partner)

    def send_first(m):
        for group in range(2):
            orbital_copy(m, group).start()

    def load_own():
        for table in tables[:3]:
            table.wait()
        for load in loads:
            load.wait()
        for m in range(half, slots):
            sending[m] = orb[first_s[0, m]]

    def load_visits():
        for copy in to_next[:2]:
            copy.wait_recv()
        for m in range(half):
            sending[m] = orb[next_second[0, m]]

    normal = 5 - is_final.astype(jnp.int32)
    pl.semaphore_wait(barrier, jnp.where(is_first, 3 + core, normal))

    @pl.when(before_final)
    def _():
        for place in range(2):
            pl.semaphore_signal(left_here, inc=1, device_id={"blk": right, "grid": place})

    @pl.when(is_final)
    def _():
        for place in range(2):
            pl.semaphore_signal(final_here, inc=1, device_id={"blk": right, "grid": place})
        pl.semaphore_signal(final_here, inc=1, device_id={"blk": relay, "grid": 1})
        pl.semaphore_wait(left_here, 2)

    @pl.when(is_first)
    def _():
        @pl.when(sends_index)
        def _():
            for copy in to_relay:
                copy.start()

        load_own()
        load_visits()
        send_first(0)
        pl.semaphore_wait(final_here, 2)
        send_first(half)

        @pl.when(sends_index)
        def _():
            for copy in to_relay:
                copy.wait_send()

    @pl.when(jnp.logical_not(is_first))
    def _():
        @pl.when(sends_index)
        def _():
            for copy in to_next:
                copy.start()

        load_own()
        send_first(half)

        @pl.when(is_relay)
        def _():
            for copy in to_relay:
                copy.wait_recv()
            pl.semaphore_wait(final_here, 2)
            onward = to_both(final, relay_send, (relay_second, relay_count))
            for copy in onward:
                copy.start()
            for copy in onward:
                copy.wait_send()

        load_visits()
        send_first(0)

        @pl.when(sends_index)
        def _():
            for copy in to_next:
                copy.wait_send()

    for stage in range(half):
        sharing[stage] = orb[worked_on(stage, 1 - core)]
        share_copy(stage).start()
        whole[stage, pl.ds(pl.multiple_of(HALF * core, HALF), HALF)] = orb[worked_on(stage, core)]
    for stage in range(1, half):
        for group in range(2):
            for m in (half + stage, stage):
                orbital_copy(m - 1, group).wait_send()
                orbital_copy(m, group).start()
    for table in tables[3:]:
        table.wait()
    for m in range(slots):
        info[0, m] = first_s[0, m]
        info[0, slots + m] = next_second[0, m]
    info[0, 2 * slots] = count_s[0]
    info[0, 2 * slots + 1] = next_count[0]

    def solved(stage):
        return stage + half * core

    def kept_local(stage):
        rows = pl.ds(pl.multiple_of(HALF * core, HALF), HALF)
        return pltpu.make_async_copy(kept.at[stage, rows], kept_out.at[solved(stage)], kept_sem.at[stage])

    def kept_remote(stage, m):
        rows = pl.ds(pl.multiple_of(HALF * (1 - core), HALF), HALF)
        return remote(kept.at[stage, rows], kept_out.at[m], kept_send.at[stage], kept_recv.at[stage], to_partner)

    def code_copy(stage, place, m):
        device = {"blk": jnp.where(core == 0, left, right), "grid": lax.div(place, 2)}
        rows = pl.ds(pl.multiple_of(16 * place, 16), 16)
        there = pl.ds(pl.multiple_of(16 * lax.rem(place, 2), 16), 16)
        return remote(
            codes.at[stage, rows], codes_out.at[m, there],
            code_send.at[stage, place], code_recv.at[m, lax.rem(place, 2)], device,
        )

    def one_stage(stage, carry):
        m = solved(stage)
        share_copy(stage).wait_recv()

        def forward_group(turn, carry):
            place = 2 * lax.rem(turn, 2) + lax.div(turn, 2)
            rows = pl.ds(pl.multiple_of(16 * place, 16), 16)
            arrival(stage, place).wait_recv()
            values = []
            for column in range(HALF):
                lanes = pl.ds(LANES * column, LANES)
                values.append(whole[stage, rows, lanes].astype(f32) * arriving[stage, rows, lanes].astype(f32))
            re, im = real_forward(values)
            for k in range(ROWS):
                if k == 0:
                    turned_re, turned_im = re[0], jnp.zeros_like(re[0])
                else:
                    c, s = twiddles_v[k, 0:1], twiddles_v[k, 1:2]
                    if im[k] is None:
                        turned_re, turned_im = re[k] * c, re[k] * s
                    else:
                        turned_re, turned_im = re[k] * c - im[k] * s, re[k] * s + im[k] * c
                for part, value in enumerate((turned_re, turned_im)):
                    high, low = split(value)
                    for place, piece in enumerate((high, low, high)):
                        start = LANES * (2 * place + part)
                        spectra[k, :, start : start + LANES] = piece
            out = dot(spectra[...].reshape(ROWS * 16, 6 * LANES), lane_fwd_v[...])
            planes[:, rows, :] = out.reshape(ROWS, 16, 2 * LANES)
            return carry

        lax.fori_loop(0, 4, forward_group, 0)

        for k in range(ROWS):
            high, low = split(planes[k])
            out = dot(row_fwd_v[...], jnp.concatenate([high, low, high], 0))
            kernel = filters_v[k]
            re = (out[:L, :LANES] + out[L:, LANES:]) * kernel
            im = (out[:L, LANES:] - out[L:, :LANES]) * kernel
            high, low = split(jnp.concatenate([re, im], 1))
            out = dot(row_inv_v[...], jnp.concatenate([high, low, high], 0))
            re = out[:L, :LANES] - out[L:, LANES:]
            im = out[:L, LANES:] + out[L:, :LANES]
            planes[k] = jnp.concatenate([re, im], 1)

        live = jnp.where(m < jnp.where(core == 0, count_s[0], next_count[0]), 1.0, 0.0).astype(f32)

        def inverse_group(turn, carry):
            place = 2 * (1 - lax.rem(turn, 2)) + lax.div(turn, 2)
            rows = pl.ds(pl.multiple_of(16 * place, 16), 16)
            high, low = split(planes[:, rows, :].reshape(ROWS * 16, 2 * LANES))
            out = dot(jnp.concatenate([high, low, high], 1), lane_inv_v[...])
            result[...] = out.reshape(ROWS, 16, 2 * LANES)
            re, im = [], []
            for k in range(ROWS):
                value_re = result[k, :, :LANES]
                if k == 0:
                    re.append(value_re)
                    im.append(None)
                    continue
                value_im = result[k, :, LANES:]
                c, s = twiddles_v[k, 0:1], twiddles_v[k, 1:2]
                re.append(value_re * c + value_im * s)
                im.append(None if k == ROWS - 1 else value_im * c - value_re * s)
            potential = real_inverse(re, im)
            terms, largest = [], None
            for column in range(HALF):
                lanes = pl.ds(LANES * column, LANES)
                value = potential[column] * live
                kept[stage, rows, lanes] = value * arriving[stage, rows, lanes].astype(f32)
                terms.append(value * whole[stage, rows, lanes].astype(f32))
                size = jnp.abs(terms[-1])
                largest = size if largest is None else jnp.maximum(largest, size)
            bound = jnp.broadcast_to(jnp.maximum(jnp.max(largest, axis=1, keepdims=True), 1e-30), (16, LANES))
            exponent = jnp.ceil(jnp.log2(bound))
            mantissa = jnp.ceil(bound * jnp.exp2(-exponent) * MANTISSA)
            side = lax.broadcasted_iota(jnp.int32, (16, LANES), 1) < LANES // 2
            codes[stage, rows, CELLS:] = jnp.where(side, mantissa, exponent).astype(jnp.int32).astype(jnp.int16)
            inverse_scale = 1.0 / scale_of(mantissa, exponent)
            for column in range(HALF):
                lanes = pl.ds(LANES * column, LANES)
                code = jnp.round(terms[column] * inverse_scale)
                codes[stage, rows, lanes] = code.astype(jnp.int32).astype(jnp.int16)
            code_copy(stage, place, m).start()
            return carry

        lax.fori_loop(0, 4, inverse_group, 0)
        kept_local(stage).start()
        kept_remote(stage, m).start()
        return carry

    lax.fori_loop(0, half, one_stage, 0)
    for stage in range(half):
        share_copy(stage).wait_send()
        kept_local(stage).wait()
        kept_remote(stage, stage + half * (1 - core)).wait()
        for place in range(4):
            code_copy(stage, place, solved(stage)).wait_send()
    for m in range(slots):
        for group in range(2):
            if m % half == half - 1:
                orbital_copy(m, group).wait_send()
            code_copy(0, group, m).wait_recv()


def exchange(orbitals, pair_first, pair_second, pair_count):
    blocks = lax.axis_size("blk")
    slots = pair_first.shape[1]
    block, rows, cells = orbitals.shape
    lane_fwd, lane_inv = lane_tables()
    row_fwd, row_inv = row_tables()
    tables = [jnp.asarray(t) for t in (lane_fwd, lane_inv, row_fwd, row_inv, filter_table(), twiddle_table())]
    anywhere, smem = (pl.BlockSpec(memory_space=space) for space in (pl.ANY, pltpu.SMEM))
    dma, dmas = pltpu.SemaphoreType.DMA, lambda *shape: pltpu.SemaphoreType.DMA(shape)
    half = slots // 2
    return pl.pallas_call(
        functools.partial(pair_kernel, blocks, slots),
        out_shape=[
            jax.ShapeDtypeStruct((slots, rows, cells), f32),
            jax.ShapeDtypeStruct((slots, rows, cells + LANES), jnp.int16),
            jax.ShapeDtypeStruct((1, 2 * slots + 2), jnp.int32),
        ],
        in_specs=[anywhere] * (4 + len(tables)),
        out_specs=[anywhere, anywhere, smem],
        scratch_shapes=[
            pltpu.VMEM((block, rows, cells), bf16),
            pltpu.VMEM((slots, rows, cells), bf16),
            pltpu.VMEM((half, L, cells), bf16),
            pltpu.VMEM((half, rows, cells), bf16),
            pltpu.VMEM((half, L, cells), bf16),
            pltpu.VMEM((half, L, cells), f32),
            pltpu.VMEM((half, L, cells + LANES), jnp.int16),
            pltpu.VMEM((ROWS, 16, 6 * LANES), bf16),
            pltpu.VMEM((ROWS, L, 2 * LANES), f32),
            pltpu.VMEM((ROWS, 16, 2 * LANES), f32),
            pltpu.VMEM(lane_fwd.shape, bf16),
            pltpu.VMEM(lane_inv.shape, bf16),
            pltpu.VMEM(row_fwd.shape, bf16),
            pltpu.VMEM(row_inv.shape, bf16),
            pltpu.VMEM((ROWS, L, LANES), f32),
            pltpu.VMEM((ROWS, 2, LANES), f32),
            pltpu.SMEM(pair_first.shape, jnp.int32),
            pltpu.SMEM(pair_second.shape, jnp.int32),
            pltpu.SMEM(pair_count.shape, jnp.int32),
            pltpu.SMEM(pair_second.shape, jnp.int32),
            pltpu.SMEM(pair_count.shape, jnp.int32),
            pltpu.SMEM(pair_second.shape, jnp.int32),
            pltpu.SMEM(pair_count.shape, jnp.int32),
            pltpu.SemaphoreType.REGULAR, pltpu.SemaphoreType.REGULAR, dmas(2, 2), dmas(2), dmas(LOADS),
            dmas(9), dmas(2, 2), dmas(2), dmas(slots, 2), dmas(half, 4),
            dmas(half), dmas(half), dmas(half, 4), dmas(slots, 2),
            dmas(half), dmas(half), dmas(half),
        ],
        compiler_params=pltpu.CompilerParams(
            collective_id=0, has_side_effects=True, vmem_limit_bytes=60 * 2**20
        ),
        name="pair_exchange",
    )(orbitals, pair_first, pair_second, pair_count, *tables)


def merge_kernel(
    half, block, kept_in, codes_in, info,
    out, kept, codes, scales, total, zero, staged, single, goes_to, kept_sem, code_sem, out_sem,
):
    slots = 2 * half
    first = [info[0, slot] for slot in range(slots)]
    second = [info[0, slots + slot] for slot in range(slots)]
    count, second_count = info[0, 2 * slots], info[0, 2 * slots + 1]
    pieces, width = 4, zero.shape[1] // 4

    def own_live(slot):
        return slot < count

    def back_live(slot):
        return slot < second_count

    loads = []
    for m in range(slots):
        kept_live, code_live = (own_live(m), back_live(m)) if m < half else (back_live(m), own_live(m))
        loads.append((kept_live, pltpu.make_async_copy(kept_in.at[m], kept.at[m], kept_sem.at[m])))
        loads.append((code_live, pltpu.make_async_copy(codes_in.at[m], codes.at[m], code_sem.at[m])))
    back_loads = loads[1:slots:2] + loads[slots::2]
    own_loads = loads[0:slots:2] + loads[slots + 1 :: 2]
    for needed, load in back_loads + own_loads:
        pl.when(needed)(load.start)
    zero[...] = jnp.zeros_like(zero)

    for row in range(block):
        touched = jnp.bool_(False)
        for slot in range(slots):
            touched |= own_live(slot) & (first[slot] == row)
            touched |= back_live(slot) & (second[slot] == row)

        @pl.when(jnp.logical_not(touched))
        def _():
            pltpu.make_async_copy(zero, out.at[row], out_sem).start()

    def arrive(some_loads, messages, live):
        for needed, load in some_loads:
            pl.when(needed)(load.wait)
        for m in messages:

            @pl.when(live(m))
            def _():
                side = codes[m, :, CELLS:].astype(f32)
                scale = scale_of(side[:, :1], side[:, LANES // 2 : LANES // 2 + 1])
                scales[m] = jnp.broadcast_to(scale, scales.shape[1:])

    def over_pieces(body):
        def piece(index, carry):
            body(pl.ds(pl.multiple_of(width * index, width), width))
            return carry

        lax.fori_loop(0, pieces, piece, 0)

    def term(is_kept, m, lanes):
        if is_kept:
            return kept[m, :, lanes]
        return codes[m, :, lanes].astype(f32) * scales[m, :, 0:1]

    def add_up(place, kind_half, lead, live, rows, extra):
        def begin(lanes):
            total[:, lanes] = term(kind_half(lead), lead, lanes)

        over_pieces(begin)
        for later in range(lead + 1, slots):

            @pl.when(live(later) & (rows[later] == rows[lead]))
            def _():
                def more(lanes):
                    total[:, lanes] += term(kind_half(later), later, lanes)

                over_pieces(more)

        for flag, other in extra:

            @pl.when(flag)
            def _():
                def more(lanes):
                    total[:, lanes] += staged[other, :, lanes].astype(f32)

                over_pieces(more)

        def end(lanes):
            staged[place, :, lanes] = total[:, lanes].astype(bf16)

        over_pieces(end)

    def alone(n, carry):
        m = lax.rem(n, slots)
        is_kept = (n < slots) == (m >= half)

        @pl.when((single[n] == 1) & is_kept)
        def _():
            for piece in range(2):
                lanes = pl.ds(CELLS // 2 * piece, CELLS // 2)
                staged[n, :, lanes] = kept[m, :, lanes].astype(bf16)

        @pl.when((single[n] == 1) & jnp.logical_not(is_kept))
        def _():
            for piece in range(2):
                lanes = pl.ds(CELLS // 2 * piece, CELLS // 2)
                staged[n, :, lanes] = (codes[m, :, lanes].astype(f32) * scales[m, :, 0:1]).astype(bf16)

        @pl.when(goes_to[n] >= 0)
        def _():
            pltpu.make_async_copy(staged.at[n], out.at[goes_to[n]], out_sem).start()

        return carry

    def plan(n, lead, several, has_row, row):
        single[n] = (lead & jnp.logical_not(several)).astype(jnp.int32)
        goes_to[n] = jnp.where(lead & jnp.logical_not(several) & has_row, row, -1)

    leads, sums = [], []
    for slot in range(slots):
        lead, several, owned = back_live(slot), jnp.bool_(False), jnp.bool_(False)
        for earlier in range(slot):
            lead &= second[earlier] != second[slot]
        for later in range(slot + 1, slots):
            several |= back_live(later) & (second[later] == second[slot])
        for other in range(slots):
            owned |= own_live(other) & (first[other] == second[slot])
        leads.append(lead)
        sums.append((lead & several, owned))
        plan(slot, lead, several, jnp.logical_not(owned), second[slot])
    arrive(back_loads, range(half), back_live)
    lax.fori_loop(0, slots, alone, 0)
    for slot, (several, owned) in enumerate(sums):

        @pl.when(several)
        def _():
            add_up(slot, lambda s: s >= half, slot, back_live, second, [])

            @pl.when(jnp.logical_not(owned))
            def _():
                pltpu.make_async_copy(staged.at[slot], out.at[second[slot]], out_sem).start()

    sums = []
    for slot in range(slots):
        lead, several = own_live(slot), jnp.bool_(False)
        for earlier in range(slot):
            lead &= first[earlier] != first[slot]
        for later in range(slot + 1, slots):
            several |= own_live(later) & (first[later] == first[slot])
        extra = [(leads[other] & (second[other] == first[slot]), other) for other in range(slots)]
        for flag, other in extra:
            several |= flag
        sums.append((lead & several, extra))
        plan(slots + slot, lead, several, jnp.bool_(True), first[slot])
    arrive(own_loads, range(half, slots), own_live)
    lax.fori_loop(slots, 2 * slots, alone, 0)
    for slot, (several, extra) in enumerate(sums):

        @pl.when(several)
        def _():
            add_up(slots + slot, lambda s: s < half, slot, own_live, first, extra)
            pltpu.make_async_copy(staged.at[slots + slot], out.at[first[slot]], out_sem).start()

    pltpu.make_async_copy(out, out, out_sem).wait()


def merge(kept, codes, info, shape):
    slots, rows, cells = kept.shape
    anywhere, smem = (pl.BlockSpec(memory_space=space) for space in (pl.ANY, pltpu.SMEM))
    dma, dmas = pltpu.SemaphoreType.DMA, pltpu.SemaphoreType.DMA((slots,))
    return pl.pallas_call(
        functools.partial(merge_kernel, slots // 2, shape[0]),
        out_shape=jax.ShapeDtypeStruct(shape, bf16),
        in_specs=[anywhere] * 2 + [smem],
        out_specs=anywhere,
        scratch_shapes=[
            pltpu.VMEM(kept.shape, f32),
            pltpu.VMEM(codes.shape, jnp.int16),
            pltpu.VMEM((slots, rows, LANES), f32),
            pltpu.VMEM((rows, cells), f32),
            pltpu.VMEM((rows, cells), bf16),
            pltpu.VMEM((2 * slots, rows, cells), bf16),
            pltpu.SMEM((2 * slots,), jnp.int32),
            pltpu.SMEM((2 * slots,), jnp.int32),
            dmas, dmas, dma,
        ],
        compiler_params=pltpu.CompilerParams(vmem_limit_bytes=60 * 2**20),
        name="merge_rows",
    )(kept, codes, info)


def per_device(orbitals, pair_first, pair_second, pair_count):
    kept, codes, info = exchange(orbitals, pair_first, pair_second, pair_count)
    return merge(kept, codes, info, orbitals.shape)


def solution(mesh):
    return jax.shard_map(
        per_device,
        mesh=mesh,
        in_specs=(P("blk", "grid", None), P("blk", None), P("blk", None), P("blk")),
        out_specs=P("blk", "grid", None),
        check_vma=False,
    )
```
